128 devices in a mesh: user: 16 (over z, x), item: 8 (over y, core).
Axes of the slice: x: 4, y: 4, z: 4, core: 2. Of those that a mesh axis runs over, the one named last changes fastest.
Arguments:
- counts: int32 [32768, 128, 128], P(('user', 'item')), may hold values from 0 to 5, as said below
- tile_user: int32 [32768], P(('user', 'item')), may hold values from 0 to 7
- tile_slot: int32 [32768], P(('user', 'item')), may hold values from 0 to 31
- live_tiles: int32 [128], P(('user', 'item')), may hold values from 64 to 256, as said below
- touched: int32 [2048, 2], P(('user', 'item')), may hold values from 0 to 3, as said below
- user_shape: float32 [16384, 256], P('user'), may hold values from 0.3 to 3
- user_rate: float32 [16384, 256], P('user'), may hold values from 0.5 to 5
- item_shape: float32 [65536, 256], P(('user', 'item')), may hold values from 0.3 to 3
- item_rate: float32 [65536, 256], P(('user', 'item')), may hold values from 32768 to 327680
Outputs:
- user_shape_new: float32 [16384, 256], P('user')
- user_rate_new: float32 [16384, 256], P('user')
- item_shape_new: float32 [65536, 256], P(('user', 'item'))
- item_elog: float32 [65536, 256], P(('user', 'item'))
The draws below stay inside these ranges and needn't reach their ends.
Inputs may be any that keep to these rules, and one draw needn't show every extreme that they name: `counts`: mostly zero. Slots of device d at positions live_tiles[d] and beyond are padding and carry no data; some device has all 256 slots live. `touched`: the 2 block numbers in one row are distinct.
All inputs are finite; a program needn't handle non-finite values.
Results may differ from the reference program's by a relative error of at most 0.0026.
The reference program's roundings to bfloat16 on the way (of `user_gain`, `item_gain` and `ratios`) count: a program that leaves them out, or rounds other values in their place, can miss the bound.
Values may be sent and summed in bfloat16 or wider, within the bound.
No kernel may reach another device: no remote copies, remote signals or barrier semaphores. Data moves between devices by JAX's collectives and lax.ppermute only.
A program may use at most 128 MiB of HBM per device.

```python
import math
import jax
import jax.numpy as jnp
from jax import lax

K = 256
TB = 128
UB = 8
IB_DEV = 4
CAP = 2
TILES = 256
USERS = 16384
ITEMS = 65536
N_USER = 16
N_ITEM = 8
DEVICES = 128


def draw_counts(key, part):
    key = jax.random.fold_in(key, 11)
    first_key, second_key = jax.random.split(key)
    full_shape = (N_USER * N_ITEM * TILES, TB, TB)
    hit_mask = jax.random.randint(first_key, full_shape, 0, 8) == 0
    values = jax.random.randint(second_key, full_shape, 1, 6)
    return jnp.where(hit_mask, values, 0).astype(jnp.int32)


def draw_live_tiles(key, part):
    key = jax.random.fold_in(key, 12)
    first_key, second_key = jax.random.split(key)
    devices = N_USER * N_ITEM
    counts_live = TILES // jax.random.randint(first_key, (devices,), 1, 5)
    busiest = jax.random.randint(second_key, (), 0, devices)
    return jnp.where(jnp.arange(devices) == busiest, TILES, counts_live).astype(jnp.int32)


def draw_touched(key, part):
    key = jax.random.fold_in(key, 13)
    row_count = N_USER * N_ITEM * N_USER
    scores = jax.random.randint(key, (row_count, IB_DEV), 0, 2 ** 20) * IB_DEV + jnp.arange(IB_DEV, dtype=jnp.int32)[None, :]
    order = jnp.argsort(scores, axis=1, stable=True)
    return order[:, :CAP].astype(jnp.int32)


def touch_ends(array, rng, low, top_value):
    longest = array.shape.index(max(array.shape))
    spots = []
    for shift in (0, 1):
        where = [jax.random.randint(jax.random.fold_in(rng, axis), (), 0, length) for axis, length in enumerate(array.shape)]
        where[longest] = (where[longest] + shift) % array.shape[longest]
        spots.append(tuple(where))
    return array.at[spots[0]].set(low).at[spots[1]].set(top_value)


def level_of(stream_key, dims, pieces, least, high):
    loudness = 1.0
    for position, parts in pieces:
        steps = jax.random.uniform(jax.random.fold_in(jax.random.fold_in(stream_key, 6), position), (parts,), jnp.float32, least / len(pieces), high / len(pieces))
        loudness = loudness * jnp.repeat(jnp.exp(steps), dims[position] // parts).reshape((-1,) + (1,) * (len(dims) - 1 - position))
    return loudness


def setup_inputs(seed: int = 0) -> dict:
    streams_of = jax.random.split(jax.random.key(seed), 10)
    counts = draw_counts(jax.random.fold_in(streams_of[9], 71), 0)
    tile_user = touch_ends(jax.random.randint(streams_of[1], (DEVICES * TILES,), 0, UB), jax.random.fold_in(streams_of[1], 1), 0, UB - 1).astype(jnp.int32)
    tile_slot = touch_ends(jax.random.randint(streams_of[2], (DEVICES * TILES,), 0, N_USER * CAP), jax.random.fold_in(streams_of[2], 1), 0, (N_USER * CAP) - 1).astype(jnp.int32)
    live_tiles = draw_live_tiles(jax.random.fold_in(streams_of[9], 71), 0)
    touched = draw_touched(jax.random.fold_in(streams_of[9], 71), 0)
    user_shape = jnp.clip(jnp.exp(math.log(3.0) - 2.3025851 * jax.random.uniform(streams_of[5], (USERS, K), jnp.float32) ** level_of(streams_of[5], (USERS, K), ((0, 16),), -0.2, 0.2)), 0.3, 3.0)
    user_rate = jnp.clip(jnp.exp(math.log(5.0) - 2.3025851 * jax.random.uniform(streams_of[6], (USERS, K), jnp.float32) ** level_of(streams_of[6], (USERS, K), ((0, 16),), -0.2, 0.2)), 0.5, 5.0)
    item_shape = jnp.clip(jnp.exp(math.log(3.0) - 2.3025851 * jax.random.uniform(streams_of[7], (ITEMS, K), jnp.float32) ** level_of(streams_of[7], (ITEMS, K), ((0, 128),), -0.2, 0.2)), 0.3, 3.0)
    item_rate = jnp.clip(jnp.exp(math.log(327680.0) - 2.3025851 * jax.random.uniform(streams_of[8], (ITEMS, K), jnp.float32) ** level_of(streams_of[8], (ITEMS, K), ((0, 128),), -0.2, 0.2)), 32768.0, 327680.0)
    return {"counts": counts, "tile_user": tile_user, "tile_slot": tile_slot, "live_tiles": live_tiles, "touched": touched, "user_shape": user_shape, "user_rate": user_rate, "item_shape": item_shape, "item_rate": item_rate}


user_prior = 0.3
activity_prior = 0.3
activity_scale = 1.0
item_prior = 0.3
popularity_prior = 0.3
popularity_scale = 1.0


def expected_gain(shape_values, rate_values):
    return jnp.exp(lax.digamma(shape_values) - jnp.log(rate_values)).astype(jnp.bfloat16)


def reference(counts, tile_user, tile_slot, live_tiles, touched, user_shape, user_rate, item_shape, item_rate):
    devices = N_USER * N_ITEM
    user_gain = lax.optimization_barrier(expected_gain(user_shape, user_rate)).reshape(N_USER * UB, TB, K)
    item_gain = lax.optimization_barrier(expected_gain(item_shape, item_rate)).reshape(devices * IB_DEV, TB, K)
    counts_all = counts.reshape(devices, TILES, TB, TB)
    users_all = tile_user.reshape(devices, TILES)
    slots_all = tile_slot.reshape(devices, TILES)
    touched_all = touched.reshape(devices, N_USER, CAP)
    positions = jnp.arange(TILES, dtype=jnp.int32)
    highest = lax.Precision.HIGHEST

    def one_device(carry, device):
        user_acc, item_acc = carry
        user_pos = device // N_ITEM
        item_pos = device % N_ITEM
        owner_index = slots_all[device] // CAP
        local_block = touched_all[device][owner_index, slots_all[device] % CAP]
        item_block = (owner_index * N_ITEM + item_pos) * IB_DEV + local_block
        user_block = user_pos * UB + users_all[device]
        user_rows = user_gain[user_block].astype(jnp.float32)
        item_rows = item_gain[item_block].astype(jnp.float32)
        denominator = jnp.einsum("tek,tfk->tef", user_rows, item_rows, precision=highest)
        tile_counts = counts_all[device]
        keep_mask = (tile_counts > 0) & (positions < live_tiles[device])[:, None, None]
        ratios = jnp.where(keep_mask, tile_counts.astype(jnp.float32) / denominator, 0.0)
        ratios = lax.optimization_barrier(ratios.astype(jnp.bfloat16)).astype(jnp.float32)
        user_term = user_rows * jnp.einsum("tef,tfk->tek", ratios, item_rows, precision=highest)
        item_term = item_rows * jnp.einsum("tef,tek->tfk", ratios, user_rows, precision=highest)
        return (user_acc.at[user_block].add(user_term), item_acc.at[item_block].add(item_term)), None

    zeros_user = jnp.zeros((N_USER * UB, TB, K), jnp.float32)
    zeros_item = jnp.zeros((devices * IB_DEV, TB, K), jnp.float32)
    (user_acc, item_acc), _ = lax.scan(one_device, (zeros_user, zeros_item), jnp.arange(devices, dtype=jnp.int32))
    user_shape_new = user_prior + user_acc.reshape(USERS, K)
    kappa_rate = activity_prior / activity_scale + jnp.sum(user_shape / user_rate, axis=1, keepdims=True)
    item_mean = item_shape / item_rate
    item_total = jnp.sum(item_mean, axis=0)
    user_rate_new = (activity_prior + K * user_prior) / kappa_rate + item_total
    user_total = jnp.sum(user_shape_new / user_rate_new, axis=0)
    item_shape_new = item_prior + item_acc.reshape(ITEMS, K)
    tau_rate = popularity_prior / popularity_scale + jnp.sum(item_mean, axis=1, keepdims=True)
    item_rate_new = (popularity_prior + K * item_prior) / tau_rate + user_total
    item_elog = lax.digamma(item_shape_new) - jnp.log(item_rate_new)
    return user_shape_new, user_rate_new, item_shape_new, item_elog
```

```python
import functools

import jax
import jax.numpy as jnp
from jax import lax
from jax.experimental import pallas as pl
from jax.experimental.pallas import tpu as pltpu
from jax.sharding import PartitionSpec as P

user_prior = 0.3
activity_prior = 0.3
activity_scale = 1.0
item_prior = 0.3
popularity_prior = 0.3
popularity_scale = 1.0

VMEM_BYTES = 60 << 20
EXTRA = 16
LANES = 128


def digamma_rest(x):
    w = x * (x + 3.0)
    steps = (2.0 * x + 3.0) * (2.0 * w + 2.0) / (w * (w + 2.0))
    inverse = 1.0 / (x + 4.0)
    z = inverse * inverse
    series = z * (1.0 / 12.0 - z * (1.0 / 120.0 - z * (1.0 / 252.0 - z * (1.0 / 240.0))))
    return steps + 0.5 * inverse + series


def digamma(x):
    return jnp.log(x + 4.0) - digamma_rest(x)


def gains_of(shape_values, rate_values, prior, strength):
    inverse_rate = 1.0 / rate_values
    gain = (shape_values + 4.0) * jnp.exp(-digamma_rest(shape_values)) * inverse_rate
    mean = shape_values * inverse_rate
    return gain.astype(jnp.bfloat16), strength / (prior + jnp.sum(mean, axis=1, keepdims=True)), mean


def item_gain_kernel(strength, touched_ref, shape_ref, rate_ref, gain_ref, level_ref, head_ref):
    turn = pl.program_id(0)
    gain_ref[...], level_ref[...], mean = gains_of(
        shape_ref[...], rate_ref[...], popularity_prior / popularity_scale, strength
    )
    devices, per_owner = touched_ref.shape
    total = jnp.broadcast_to(jnp.sum(mean, axis=0, keepdims=True), (devices, mean.shape[1]))

    @pl.when(turn == 0)
    def _():
        head_ref[:, pl.ds(0, per_owner)] = touched_ref[...].astype(jnp.float32)
        head_ref[:, pl.ds(LANES, mean.shape[1])] = total

    @pl.when(turn > 0)
    def _():
        head_ref[:, pl.ds(LANES, mean.shape[1])] += total


def item_gains(touched, item_shape, item_rate):
    rows, factors = item_shape.shape
    devices = touched.shape[0]
    step = rows // 2
    row_spec = pl.BlockSpec((step, factors), lambda r: (r, 0))
    return pl.pallas_call(
        functools.partial(item_gain_kernel, popularity_prior + factors * item_prior),
        grid=(rows // step,),
        in_specs=[pl.BlockSpec(touched.shape, lambda r: (0, 0)), row_spec, row_spec],
        out_specs=[
            row_spec,
            pl.BlockSpec((step, 1), lambda r: (r, 0)),
            pl.BlockSpec((devices, LANES + factors), lambda r: (0, 0)),
        ],
        out_shape=[
            jax.ShapeDtypeStruct((rows, factors), jnp.bfloat16),
            jax.ShapeDtypeStruct((rows, 1), jnp.float32),
            jax.ShapeDtypeStruct((devices, LANES + factors), jnp.float32),
        ],
        compiler_params=pltpu.CompilerParams(vmem_limit_bytes=VMEM_BYTES),
        cost_estimate=pl.CostEstimate(
            flops=40 * rows * factors, bytes_accessed=10 * rows * factors, transcendentals=4 * rows * factors
        ),
    )(touched, item_shape, item_rate)


def user_gain_kernel(strength, shape_ref, rate_ref, head_ref, gain_ref, level_ref, turned_ref, column_ref):
    gain, level_ref[...], _ = gains_of(shape_ref[...], rate_ref[...], activity_prior / activity_scale, strength)
    gain_ref[...] = gain
    turned_ref[...] = gain.T

    @pl.when(pl.program_id(0) == 0)
    def _():
        column_ref[...] = jnp.sum(head_ref[:, pl.ds(LANES, gain.shape[1])], axis=0, keepdims=True)


def user_gains(user_shape, user_rate, heads):
    rows, factors = user_shape.shape
    step = rows // 4
    row_spec = pl.BlockSpec((step, factors), lambda r: (r, 0))
    return pl.pallas_call(
        functools.partial(user_gain_kernel, activity_prior + factors * user_prior),
        grid=(rows // step,),
        in_specs=[row_spec, row_spec, pl.BlockSpec(heads.shape, lambda r: (0, 0))],
        out_specs=[
            row_spec,
            pl.BlockSpec((step, 1), lambda r: (r, 0)),
            pl.BlockSpec((factors, step), lambda r: (0, r)),
            pl.BlockSpec((1, factors), lambda r: (0, 0)),
        ],
        out_shape=[
            jax.ShapeDtypeStruct((rows, factors), jnp.bfloat16),
            jax.ShapeDtypeStruct((rows, 1), jnp.float32),
            jax.ShapeDtypeStruct((factors, rows), jnp.bfloat16),
            jax.ShapeDtypeStruct((1, factors), jnp.float32),
        ],
        compiler_params=pltpu.CompilerParams(vmem_limit_bytes=VMEM_BYTES),
        cost_estimate=pl.CostEstimate(
            flops=40 * rows * factors, bytes_accessed=12 * rows * factors, transcendentals=4 * rows * factors
        ),
    )(user_shape, user_rate, heads)


def pick_kernel(per_owner, head_ref, gain_ref, picked_ref):
    for device in range(head_ref.shape[0]):
        for place in range(per_owner):
            picked_ref[device * per_owner + place] = gain_ref[head_ref[device, place].astype(jnp.int32)]


def pick(heads, item_gain, edge, per_owner):
    items, factors = item_gain.shape
    devices = heads.shape[0]
    return pl.pallas_call(
        functools.partial(pick_kernel, per_owner),
        grid=(1,),
        in_specs=[
            pl.BlockSpec((devices, LANES), lambda step: (0, 0), memory_space=pltpu.SMEM),
            pl.BlockSpec((items // edge, edge, factors), lambda step: (0, 0, 0)),
        ],
        out_specs=pl.BlockSpec((devices * per_owner, edge, factors), lambda step: (0, 0, 0)),
        out_shape=jax.ShapeDtypeStruct((devices * per_owner, edge, factors), jnp.bfloat16),
        compiler_params=pltpu.CompilerParams(vmem_limit_bytes=VMEM_BYTES),
        cost_estimate=pl.CostEstimate(
            flops=0, bytes_accessed=2 * items * factors + 2 * devices * per_owner * edge * factors, transcendentals=0
        ),
    )(heads, item_gain.reshape(items // edge, edge, factors))


def dense_kernel(user_of, slot_of, live_ref, counts_ref, dense_ref, held_ref, arrived):
    depth, group = held_ref.shape[:2]
    live = live_ref[0]
    groups = (live + group - 1) // group

    def fetch(index):
        place = lax.rem(index, depth)
        return pltpu.make_async_copy(
            counts_ref.at[pl.ds(index * group, group)], held_ref.at[place], arrived.at[place]
        )

    for index in range(depth):

        @pl.when(index < groups)
        def _():
            fetch(index).start()

    def clear(slot, carry):
        dense_ref[slot] = jnp.zeros(dense_ref.shape[1:], dense_ref.dtype)
        return carry

    lax.fori_loop(0, dense_ref.shape[0], clear, 0)

    def add_group(index, carry):
        fetch(index).wait()
        place = lax.rem(index, depth)
        for offset in range(group):
            tile = index * group + offset

            @pl.when(tile < live)
            def _():
                user, slot = user_of[tile], slot_of[tile]
                dense_ref[slot, user] += held_ref[place, offset].astype(jnp.float32).astype(jnp.bfloat16)

        @pl.when(index + depth < groups)
        def _():
            fetch(index + depth).start()

        return carry

    lax.fori_loop(0, groups, add_group, 0)


def dense_counts(counts, tile_user, tile_slot, live_tiles, slot_count, user_blocks):
    tiles, edge, _ = counts.shape
    group = 8
    depth = min(8, tiles // group)
    dense_shape = (slot_count, user_blocks, edge, edge)
    return pl.pallas_call(
        dense_kernel,
        grid_spec=pltpu.PrefetchScalarGridSpec(
            num_scalar_prefetch=3,
            grid=(1,),
            in_specs=[pl.BlockSpec(memory_space=pl.ANY)],
            out_specs=pl.BlockSpec(dense_shape, lambda step, *_: (0, 0, 0, 0)),
            scratch_shapes=[
                pltpu.VMEM((depth, group, edge, edge), jnp.int32),
                pltpu.SemaphoreType.DMA((depth,)),
            ],
        ),
        out_shape=jax.ShapeDtypeStruct(dense_shape, jnp.bfloat16),
        compiler_params=pltpu.CompilerParams(vmem_limit_bytes=VMEM_BYTES),
        cost_estimate=pl.CostEstimate(
            flops=tiles * edge * edge, bytes_accessed=4 * counts.size + 2 * slot_count * user_blocks * edge * edge,
            transcendentals=0,
        ),
    )(tile_user, tile_slot, live_tiles, counts)


def split_rows(value, rows):
    high = value.astype(jnp.bfloat16).astype(jnp.float32)
    middle = (value - high).astype(jnp.bfloat16).astype(jnp.float32)
    low = value - high - middle
    row = lax.broadcasted_iota(jnp.int32, (rows, value.shape[1]), 0)
    block = jnp.where(row == 0, high, jnp.where(row == 1, middle, jnp.where(row == 2, low, 0.0)))
    return block.astype(jnp.bfloat16)


def sweep_kernel(
    prior_share, place_ref, dense_ref, items_ref, gain_ref, turned_ref, level_ref, total_ref, item_ref, *rest
):
    user_refs, acc_ref, ratio_ref = rest[:-2], rest[-2], rest[-1]
    turn = pl.program_id(0)
    per_step, touched_rows, factors = items_ref.shape
    slots, user_blocks, edge, _ = dense_ref.shape
    users = user_blocks * edge
    chunk = users // 2

    @pl.when(turn == 0)
    def _():
        acc_ref[...] = jnp.zeros_like(acc_ref)

    items = items_ref[...].reshape(per_step * touched_rows, factors)
    turned_items = items.T
    denominators = [
        jnp.dot(gain_ref[pl.ds(first, chunk), :], turned_items, preferred_element_type=jnp.float32)
        for first in range(0, users, chunk)
    ]
    for index, denominator in enumerate(denominators):
        blocks = pl.ds(index * (chunk // edge), chunk // edge)
        rows = pl.ds(index * chunk, chunk)
        counted = jnp.concatenate(
            [dense_ref[slot, blocks].reshape(chunk, edge) for slot in range(slots)], axis=1
        ).astype(jnp.float32)
        inverse = pl.reciprocal(denominator, approx=True)
        inverse *= 2.0 - denominator * inverse
        ratios = (counted * inverse).astype(jnp.bfloat16)
        ratio_ref[rows, :] = ratios
        acc_ref[rows, :] += jnp.dot(ratios, items, preferred_element_type=jnp.float32)
    sums = jnp.dot(turned_ref[...], ratio_ref[...], preferred_element_type=jnp.float32)
    sums = sums.astype(jnp.bfloat16).T
    for owner in range(per_step):
        item_ref[turn * per_step + owner, pl.ds(0, touched_rows), :] = sums[
            owner * touched_rows : (owner + 1) * touched_rows
        ]

    @pl.when(turn == pl.num_programs(0) - 1)
    def _():
        own = users // len(user_refs)
        part = jnp.zeros((1, factors), jnp.float32)
        for ahead, user_ref in enumerate(user_refs):
            target = (place_ref[0] + ahead) % len(user_refs)
            rows = pl.ds(pl.multiple_of(target * own, own), own)
            user_sums = acc_ref[rows, :]
            user_ref[...] = user_sums.astype(jnp.bfloat16)
            shape_share = prior_share + gain_ref[rows, :].astype(jnp.float32) * user_sums
            part += jnp.sum(shape_share / (level_ref[rows, :] + total_ref[...]), axis=0, keepdims=True)
        extra = split_rows(part, EXTRA)
        for owner in range(item_ref.shape[0]):
            item_ref[owner, pl.ds(touched_rows, EXTRA), :] = extra


def sweep(place, dense, items, user_gain, turned_gain, user_level, item_total, parts):
    owners, touched_rows, factors = items.shape
    users = user_gain.shape[0]
    user_blocks, edge = dense.shape[1:3]
    per_owner = touched_rows // edge
    per_step = 2
    own = users // parts
    whole = lambda turn, place_ref: (0, 0)
    out = pl.pallas_call(
        functools.partial(sweep_kernel, user_prior / parts),
        grid_spec=pltpu.PrefetchScalarGridSpec(
            num_scalar_prefetch=1,
            grid=(owners // per_step,),
            in_specs=[
                pl.BlockSpec(
                    (per_step * per_owner, user_blocks, edge, edge), lambda turn, place_ref: (turn, 0, 0, 0)
                ),
                pl.BlockSpec((per_step, touched_rows, factors), lambda turn, place_ref: (turn, 0, 0)),
                pl.BlockSpec((users, factors), whole),
                pl.BlockSpec((factors, users), whole),
                pl.BlockSpec((users, 1), whole),
                pl.BlockSpec((1, factors), whole),
            ],
            out_specs=[pl.BlockSpec((owners, touched_rows + EXTRA, factors), lambda turn, place_ref: (0, 0, 0))]
            + [pl.BlockSpec((own, factors), whole)] * parts,
            scratch_shapes=[
                pltpu.VMEM((users, factors), jnp.float32),
                pltpu.VMEM((users, per_step * touched_rows), jnp.bfloat16),
            ],
        ),
        out_shape=[jax.ShapeDtypeStruct((owners, touched_rows + EXTRA, factors), jnp.bfloat16)]
        + [jax.ShapeDtypeStruct((own, factors), jnp.bfloat16)] * parts,
        compiler_params=pltpu.CompilerParams(vmem_limit_bytes=VMEM_BYTES),
        cost_estimate=pl.CostEstimate(
            flops=6 * owners * touched_rows * users * factors,
            bytes_accessed=2 * dense.size + 4 * items.size + 4 * users * factors,
            transcendentals=owners * touched_rows * users,
        ),
    )(place, dense, items, user_gain, turned_gain, user_level, item_total)
    return out[0], out[1:]


def own_kernel(place_ref, gain_ref, *rest):
    sums_refs, sum_ref = rest[:-1], rest[-1]
    sums = jnp.zeros(gain_ref.shape, jnp.float32)
    for sums_ref in sums_refs:
        sums += sums_ref[...].astype(jnp.float32)
    sum_ref[...] = (gain_ref[...].astype(jnp.float32) * sums).astype(jnp.bfloat16)


def own_users(place, sums, user_gain):
    own, factors = sums[0].shape
    first = lambda step, place_ref: (0, 0)
    return pl.pallas_call(
        own_kernel,
        grid_spec=pltpu.PrefetchScalarGridSpec(
            num_scalar_prefetch=1,
            grid=(1,),
            in_specs=[pl.BlockSpec((own, factors), lambda step, place_ref: (place_ref[0], 0))]
            + [pl.BlockSpec((own, factors), first)] * len(sums),
            out_specs=pl.BlockSpec((own, factors), first),
        ),
        out_shape=jax.ShapeDtypeStruct((own, factors), jnp.bfloat16),
        compiler_params=pltpu.CompilerParams(vmem_limit_bytes=VMEM_BYTES),
        cost_estimate=pl.CostEstimate(
            flops=2 * len(sums) * own * factors, bytes_accessed=2 * len(sums) * own * factors, transcendentals=0
        ),
    )(place, user_gain, *sums)


def fold_kernel(sums_ref, part_ref):
    extra = sums_ref[0].astype(jnp.float32)
    for sender in range(1, sums_ref.shape[0]):
        extra += sums_ref[sender].astype(jnp.float32)
    part_ref[...] = jnp.sum(extra, axis=0, keepdims=True)


def fold(sums):
    senders, extended, factors = sums.shape
    return pl.pallas_call(
        fold_kernel,
        grid=(1,),
        in_specs=[pl.BlockSpec((senders, EXTRA, factors), lambda step: (0, extended // EXTRA - 1, 0))],
        out_specs=pl.BlockSpec((1, factors), lambda step: (0, 0)),
        out_shape=jax.ShapeDtypeStruct((1, factors), jnp.float32),
        compiler_params=pltpu.CompilerParams(vmem_limit_bytes=VMEM_BYTES // 2),
        cost_estimate=pl.CostEstimate(flops=0, bytes_accessed=2 * senders * EXTRA * factors, transcendentals=0),
    )(sums)


def item_kernel(per_owner, head_ref, sums_ref, gain_ref, level_ref, total_ref, shape_ref, elog_ref, acc_ref):
    edge = acc_ref.shape[1]
    user_total = jnp.sum(total_ref[...], axis=0, keepdims=True)
    acc_ref[...] = jnp.zeros_like(acc_ref)
    for sender in range(sums_ref.shape[0]):
        for place in range(per_owner):
            block = head_ref[sender, place].astype(jnp.int32)
            acc_ref[block] += sums_ref[sender, pl.ds(place * edge, edge), :].astype(jnp.float32)
    for block in range(acc_ref.shape[0]):
        rows = pl.ds(block * edge, edge)
        shape_new = item_prior + gain_ref[rows, :].astype(jnp.float32) * acc_ref[block]
        shape_ref[rows, :] = shape_new
        rate_new = level_ref[rows, :] + user_total
        elog_ref[rows, :] = digamma(shape_new) - jnp.log(rate_new)


def item_update(heads, sums, item_gain, item_level, user_parts, edge):
    items, factors = item_gain.shape
    senders, extended, _ = sums.shape
    per_owner = (extended - EXTRA) // edge
    whole = lambda step: (0, 0)
    return pl.pallas_call(
        functools.partial(item_kernel, per_owner),
        grid=(1,),
        in_specs=[
            pl.BlockSpec((senders, LANES), whole, memory_space=pltpu.SMEM),
            pl.BlockSpec(sums.shape, lambda step: (0, 0, 0)),
            pl.BlockSpec((items, factors), whole),
            pl.BlockSpec((items, 1), whole),
            pl.BlockSpec(user_parts.shape, whole),
        ],
        out_specs=[pl.BlockSpec((items, factors), whole)] * 2,
        scratch_shapes=[pltpu.VMEM((items // edge, edge, factors), jnp.float32)],
        out_shape=[jax.ShapeDtypeStruct((items, factors), jnp.float32)] * 2,
        compiler_params=pltpu.CompilerParams(vmem_limit_bytes=VMEM_BYTES // 2),
        cost_estimate=pl.CostEstimate(
            flops=40 * items * factors, bytes_accessed=2 * sums.size + 10 * items * factors,
            transcendentals=4 * items * factors,
        ),
    )(heads, sums, item_gain, item_level, user_parts)


def shards(
    counts, tile_user, tile_slot, live_tiles, touched, user_shape, user_rate, item_shape, item_rate
):
    edge = counts.shape[1]
    users, factors = user_shape.shape
    user_blocks = users // edge
    owners, per_owner = touched.shape
    columns = lax.axis_size("item")
    place = lax.axis_index("item").astype(jnp.int32).reshape(1)
    item_gain, item_level, heads = item_gains(touched, item_shape, item_rate)
    heads = lax.all_to_all(heads, "user", 0, 0, tiled=True)
    item_rows = pick(heads, item_gain, edge, per_owner).reshape(owners, per_owner * edge, factors)
    item_rows = lax.all_to_all(item_rows, "user", 0, 0, tiled=True)
    user_gain, user_level, turned_gain, column_total = user_gains(user_shape, user_rate, heads)
    item_total = jnp.sum(lax.all_gather(column_total, "item", axis=0, tiled=True), axis=0, keepdims=True)
    dense = dense_counts(counts, tile_user, tile_slot, live_tiles, owners * per_owner, user_blocks)
    item_sums, user_sums = sweep(
        place, dense, item_rows, user_gain, turned_gain, user_level, item_total, columns
    )
    item_sums = lax.all_to_all(item_sums, "user", 0, 0, tiled=True)
    user_sums = [user_sums[0]] + [
        lax.ppermute(user_sums[k], "item", [(j, (j + k) % columns) for j in range(columns)])
        for k in range(1, columns)
    ]
    user_sum = lax.all_gather(own_users(place, user_sums, user_gain), "item", axis=0, tiled=True)
    user_shape_new = user_prior + user_sum.astype(jnp.float32)
    user_rate_new = user_level + item_total
    user_parts = lax.all_gather(fold(item_sums), "item", axis=0, tiled=True)
    item_shape_new, item_elog = item_update(heads, item_sums, item_gain, item_level, user_parts, edge)
    return (user_shape_new, user_rate_new, item_shape_new, item_elog)


def solution(mesh):
    return jax.shard_map(
        shards,
        mesh=mesh,
        in_specs=(
            P(("user", "item"), None, None),
            P(("user", "item")),
            P(("user", "item")),
            P(("user", "item")),
            P(("user", "item"), None),
            P("user", None),
            P("user", None),
            P(("user", "item"), None),
            P(("user", "item"), None),
        ),
        out_specs=(
            P("user", None),
            P("user", None),
            P(("user", "item"), None),
            P(("user", "item"), None),
        ),
        check_vma=False,
    )
```

```python
import functools

import jax
import jax.numpy as jnp
from jax import lax
from jax.experimental import pallas as pl
from jax.experimental.pallas import tpu as pltpu
from jax.sharding import PartitionSpec as P

user_prior = 0.3
activity_prior = 0.3
activity_scale = 1.0
item_prior = 0.3
popularity_prior = 0.3
popularity_scale = 1.0

VMEM_BYTES = 60 << 20
SWEEP_BYTES = 54 << 20
EXTRA = 16
LANES = 128


def digamma_rest(x):
    w = x * (x + 3.0)
    steps = (2.0 * x + 3.0) * (2.0 * w + 2.0) / (w * (w + 2.0))
    inverse = 1.0 / (x + 4.0)
    z = inverse * inverse
    series = z * (1.0 / 12.0 - z * (1.0 / 120.0 - z * (1.0 / 252.0 - z * (1.0 / 240.0))))
    return steps + 0.5 * inverse + series


def digamma(x):
    return jnp.log(x + 4.0) - digamma_rest(x)


def gains_of(shape_values, rate_values, prior, strength):
    inverse_rate = 1.0 / rate_values
    gain = (shape_values + 4.0) * jnp.exp(-digamma_rest(shape_values)) * inverse_rate
    mean = shape_values * inverse_rate
    return gain.astype(jnp.bfloat16), strength / (prior + jnp.sum(mean, axis=1, keepdims=True)), mean


def item_gain_kernel(strength, touched_ref, shape_ref, rate_ref, gain_ref, level_ref, head_ref):
    turn = pl.program_id(0)
    gain_ref[...], level_ref[...], mean = gains_of(
        shape_ref[...], rate_ref[...], popularity_prior / popularity_scale, strength
    )
    per_owner, devices = touched_ref.shape
    factors = mean.shape[1]
    total = jnp.broadcast_to(jnp.sum(mean, axis=0).reshape(1, 1, factors), (devices, 1, factors))

    @pl.when(turn == 0)
    def _():
        head_ref[...] = jnp.zeros_like(head_ref)
        for place in range(per_owner):
            blocks = touched_ref[pl.ds(place, 1), :].astype(jnp.float32).reshape(1, 1, devices)
            head_ref[:, :, pl.ds(place * LANES, devices)] = jnp.broadcast_to(blocks, (devices, 1, devices))

    head_ref[:, :, pl.ds(per_owner * LANES, factors)] += total


def item_gains(touched, item_shape, item_rate):
    rows, factors = item_shape.shape
    devices, per_owner = touched.shape
    step = rows // 2
    row_spec = pl.BlockSpec((step, factors), lambda r: (r, 0))
    head_shape = (devices, 1, per_owner * LANES + factors)
    return pl.pallas_call(
        functools.partial(item_gain_kernel, popularity_prior + factors * item_prior),
        grid=(rows // step,),
        in_specs=[pl.BlockSpec((per_owner, devices), lambda r: (0, 0)), row_spec, row_spec],
        out_specs=[
            row_spec,
            pl.BlockSpec((step, 1), lambda r: (r, 0)),
            pl.BlockSpec(head_shape, lambda r: (0, 0, 0)),
        ],
        out_shape=[
            jax.ShapeDtypeStruct((rows, factors), jnp.bfloat16),
            jax.ShapeDtypeStruct((rows, 1), jnp.float32),
            jax.ShapeDtypeStruct(head_shape, jnp.float32),
        ],
        compiler_params=pltpu.CompilerParams(vmem_limit_bytes=VMEM_BYTES),
        cost_estimate=pl.CostEstimate(
            flops=40 * rows * factors, bytes_accessed=10 * rows * factors, transcendentals=4 * rows * factors
        ),
    )(touched.T, item_shape, item_rate)


def user_gain_kernel(strength, shape_ref, rate_ref, head_ref, gain_ref, level_ref, turned_ref, column_ref):
    gain, level_ref[...], _ = gains_of(shape_ref[...], rate_ref[...], activity_prior / activity_scale, strength)
    gain_ref[...] = gain
    turned_ref[...] = gain.T

    @pl.when(pl.program_id(0) == 0)
    def _():
        factors = gain.shape[1]
        means = head_ref[:, :, pl.ds(head_ref.shape[2] - factors, factors)]
        column_ref[...] = jnp.sum(means, axis=0).reshape(1, factors)


def user_gains(user_shape, user_rate, heads):
    rows, factors = user_shape.shape
    step = rows // 4
    row_spec = pl.BlockSpec((step, factors), lambda r: (r, 0))
    return pl.pallas_call(
        functools.partial(user_gain_kernel, activity_prior + factors * user_prior),
        grid=(rows // step,),
        in_specs=[row_spec, row_spec, pl.BlockSpec(heads.shape, lambda r: (0, 0, 0))],
        out_specs=[
            row_spec,
            pl.BlockSpec((step, 1), lambda r: (r, 0)),
            pl.BlockSpec((factors, step), lambda r: (0, r)),
            pl.BlockSpec((1, factors), lambda r: (0, 0)),
        ],
        out_shape=[
            jax.ShapeDtypeStruct((rows, factors), jnp.bfloat16),
            jax.ShapeDtypeStruct((rows, 1), jnp.float32),
            jax.ShapeDtypeStruct((factors, rows), jnp.bfloat16),
            jax.ShapeDtypeStruct((1, factors), jnp.float32),
        ],
        compiler_params=pltpu.CompilerParams(vmem_limit_bytes=VMEM_BYTES),
        cost_estimate=pl.CostEstimate(
            flops=40 * rows * factors, bytes_accessed=12 * rows * factors, transcendentals=4 * rows * factors
        ),
    )(user_shape, user_rate, heads)


def pick_kernel(per_owner, seat_ref, head_ref, gain_ref, picked_ref, sent):
    edge = gain_ref.shape[1]
    copies = []
    for device in range(head_ref.shape[0]):
        for place in range(per_owner):
            block = head_ref[device, 0, place * LANES + seat_ref[0]].astype(jnp.int32)
            copies.append(
                pltpu.make_async_copy(
                    gain_ref.at[block],
                    picked_ref.at[device, pl.ds(place * edge, edge)],
                    sent.at[device * per_owner + place],
                )
            )
            copies[-1].start()
    for copy in copies:
        copy.wait()


def pick(seat, heads, item_gain, edge, per_owner):
    items, factors = item_gain.shape
    devices = heads.shape[0]
    return pl.pallas_call(
        functools.partial(pick_kernel, per_owner),
        grid_spec=pltpu.PrefetchScalarGridSpec(
            num_scalar_prefetch=1,
            grid=(1,),
            in_specs=[
                pl.BlockSpec(heads.shape, lambda step, seat_ref: (0, 0, 0), memory_space=pltpu.SMEM),
                pl.BlockSpec((items // edge, edge, factors), lambda step, seat_ref: (0, 0, 0)),
            ],
            out_specs=pl.BlockSpec(memory_space=pl.ANY),
            scratch_shapes=[pltpu.SemaphoreType.DMA((devices * per_owner,))],
        ),
        out_shape=jax.ShapeDtypeStruct((devices, per_owner * edge, factors), jnp.bfloat16),
        compiler_params=pltpu.CompilerParams(vmem_limit_bytes=VMEM_BYTES),
        cost_estimate=pl.CostEstimate(
            flops=0, bytes_accessed=2 * items * factors + 2 * devices * per_owner * edge * factors, transcendentals=0
        ),
    )(seat, heads, item_gain.reshape(items // edge, edge, factors))


def dense_kernel(user_of, slot_of, live_ref, counts_ref, after_ref, dense_ref, held_ref, arrived):
    depth, group = held_ref.shape[:2]
    live = live_ref[0]
    groups = (live + group - 1) // group

    def fetch(index):
        place = lax.rem(index, depth)
        return pltpu.make_async_copy(
            counts_ref.at[pl.ds(index * group, group)], held_ref.at[place], arrived.at[place]
        )

    for index in range(depth):

        @pl.when(index < groups)
        def _():
            fetch(index).start()

    def clear(slot, carry):
        dense_ref[slot] = jnp.zeros(dense_ref.shape[1:], dense_ref.dtype)
        return carry

    lax.fori_loop(0, dense_ref.shape[0], clear, 0)

    def add_group(index, carry):
        fetch(index).wait()
        place = lax.rem(index, depth)
        for offset in range(group):
            tile = index * group + offset

            @pl.when(tile < live)
            def _():
                user, slot = user_of[tile], slot_of[tile]
                dense_ref[slot, user] += held_ref[place, offset].astype(jnp.float32).astype(jnp.bfloat16)

        @pl.when(index + depth < groups)
        def _():
            fetch(index + depth).start()

        return carry

    lax.fori_loop(0, groups, add_group, 0)


def dense_counts(counts, tile_user, tile_slot, live_tiles, slot_count, user_blocks, after):
    tiles, edge, _ = counts.shape
    group = 8
    depth = min(8, tiles // group)
    dense_shape = (slot_count, user_blocks, edge, edge)
    return pl.pallas_call(
        dense_kernel,
        grid_spec=pltpu.PrefetchScalarGridSpec(
            num_scalar_prefetch=3,
            grid=(1,),
            in_specs=[pl.BlockSpec(memory_space=pl.ANY), pl.BlockSpec(after.shape, lambda step, *_: (0, 0))],
            out_specs=pl.BlockSpec(dense_shape, lambda step, *_: (0, 0, 0, 0)),
            scratch_shapes=[
                pltpu.VMEM((depth, group, edge, edge), jnp.int32),
                pltpu.SemaphoreType.DMA((depth,)),
            ],
        ),
        out_shape=jax.ShapeDtypeStruct(dense_shape, jnp.bfloat16),
        compiler_params=pltpu.CompilerParams(vmem_limit_bytes=VMEM_BYTES),
        cost_estimate=pl.CostEstimate(
            flops=tiles * edge * edge, bytes_accessed=4 * counts.size + 2 * slot_count * user_blocks * edge * edge,
            transcendentals=0,
        ),
    )(tile_user, tile_slot, live_tiles, counts, after)


def split_rows(value, rows):
    high = value.astype(jnp.bfloat16).astype(jnp.float32)
    middle = (value - high).astype(jnp.bfloat16).astype(jnp.float32)
    low = value - high - middle
    row = lax.broadcasted_iota(jnp.int32, (rows, value.shape[1]), 0)
    block = jnp.where(row == 0, high, jnp.where(row == 1, middle, jnp.where(row == 2, low, 0.0)))
    return block.astype(jnp.bfloat16)


def sweep_kernel(
    prior_share, place_ref, dense_ref, items_ref, gain_ref, turned_ref, level_ref, total_ref, item_ref, *rest
):
    user_refs, (acc_ref, early_ref, late_ref, held_ref) = rest[:-4], rest[-4:]
    turn = pl.program_id(0)
    per_step, touched_rows, factors = items_ref.shape
    slots, user_blocks, edge, _ = dense_ref.shape
    users = user_blocks * edge
    pair = per_step // 2
    chunk = users // 2

    def items_of(half):
        return items_ref[pl.ds(half * pair, pair)].reshape(pair * touched_rows, factors)

    def denominators(half):
        turned_items = items_of(half).T
        return [
            jnp.dot(gain_ref[pl.ds(first, chunk), :], turned_items, preferred_element_type=jnp.float32)
            for first in range(0, users, chunk)
        ]

    def put_ratios(half, parts, ratio_ref):
        for index, denominator in enumerate(parts):
            blocks = pl.ds(index * (chunk // edge), chunk // edge)
            first = half * (slots // 2)
            counted = jnp.concatenate(
                [dense_ref[slot, blocks].reshape(chunk, edge) for slot in range(first, first + slots // 2)], axis=1
            ).astype(jnp.float32)
            inverse = pl.reciprocal(denominator, approx=True)
            inverse *= 2.0 - denominator * inverse
            ratio_ref[pl.ds(index * chunk, chunk), :] = (counted * inverse).astype(jnp.bfloat16)

    def add_products(ratio_ref, items, owner):
        for first in range(0, users, chunk):
            rows = pl.ds(first, chunk)
            acc_ref[rows, :] += jnp.dot(ratio_ref[rows, :], items, preferred_element_type=jnp.float32)
        sums = jnp.dot(turned_ref[...], ratio_ref[...], preferred_element_type=jnp.float32)
        sums = sums.astype(jnp.bfloat16).T
        for index in range(pair):
            item_ref[owner + index, pl.ds(0, touched_rows), :] = sums[
                index * touched_rows : (index + 1) * touched_rows
            ]

    @pl.when(turn == 0)
    def _():
        acc_ref[...] = jnp.zeros_like(acc_ref)
        late_ref[...] = jnp.zeros_like(late_ref)
        held_ref[...] = jnp.zeros_like(held_ref)

    early = denominators(0)
    add_products(late_ref, held_ref[...], jnp.maximum(turn * per_step - pair, pair))
    put_ratios(0, early, early_ref)
    late = denominators(1)
    add_products(early_ref, items_of(0), turn * per_step)
    put_ratios(1, late, late_ref)
    held_ref[...] = items_of(1)

    @pl.when(turn == pl.num_programs(0) - 1)
    def _():
        add_products(late_ref, held_ref[...], turn * per_step + pair)
        own = users // len(user_refs)
        part = jnp.zeros((1, factors), jnp.float32)
        for ahead, user_ref in enumerate(user_refs):
            target = (place_ref[0] + ahead) % len(user_refs)
            rows = pl.ds(pl.multiple_of(target * own, own), own)
            user_sums = acc_ref[rows, :]
            user_ref[...] = user_sums.astype(jnp.bfloat16)
            shape_share = prior_share + gain_ref[rows, :].astype(jnp.float32) * user_sums
            part += jnp.sum(shape_share / (level_ref[rows, :] + total_ref[...]), axis=0, keepdims=True)
        extra = split_rows(part, EXTRA)
        for owner in range(item_ref.shape[0]):
            item_ref[owner, pl.ds(touched_rows, EXTRA), :] = extra


def sweep(place, dense, items, user_gain, turned_gain, user_level, item_total, parts):
    owners, touched_rows, factors = items.shape
    users = user_gain.shape[0]
    user_blocks, edge = dense.shape[1:3]
    per_owner = touched_rows // edge
    per_step = 4
    own = users // parts
    whole = lambda turn, place_ref: (0, 0)
    out = pl.pallas_call(
        functools.partial(sweep_kernel, user_prior / parts),
        grid_spec=pltpu.PrefetchScalarGridSpec(
            num_scalar_prefetch=1,
            grid=(owners // per_step,),
            in_specs=[
                pl.BlockSpec(
                    (per_step * per_owner, user_blocks, edge, edge), lambda turn, place_ref: (turn, 0, 0, 0)
                ),
                pl.BlockSpec((per_step, touched_rows, factors), lambda turn, place_ref: (turn, 0, 0)),
                pl.BlockSpec((users, factors), whole),
                pl.BlockSpec((factors, users), whole),
                pl.BlockSpec((users, 1), whole),
                pl.BlockSpec((1, factors), whole),
            ],
            out_specs=[pl.BlockSpec((owners, touched_rows + EXTRA, factors), lambda turn, place_ref: (0, 0, 0))]
            + [pl.BlockSpec((own, factors), whole)] * parts,
            scratch_shapes=[
                pltpu.VMEM((users, factors), jnp.float32),
                pltpu.VMEM((users, per_step // 2 * touched_rows), jnp.bfloat16),
                pltpu.VMEM((users, per_step // 2 * touched_rows), jnp.bfloat16),
                pltpu.VMEM((per_step // 2 * touched_rows, factors), jnp.bfloat16),
            ],
        ),
        out_shape=[jax.ShapeDtypeStruct((owners, touched_rows + EXTRA, factors), jnp.bfloat16)]
        + [jax.ShapeDtypeStruct((own, factors), jnp.bfloat16)] * parts,
        compiler_params=pltpu.CompilerParams(vmem_limit_bytes=SWEEP_BYTES),
        cost_estimate=pl.CostEstimate(
            flops=6 * owners * touched_rows * users * factors,
            bytes_accessed=2 * dense.size + 4 * items.size + 4 * users * factors,
            transcendentals=owners * touched_rows * users,
        ),
    )(place, dense, items, user_gain, turned_gain, user_level, item_total)
    return out[0], out[1:]


def own_kernel(place_ref, gain_ref, *rest):
    sums_refs, sum_ref = rest[:-1], rest[-1]
    sums = jnp.zeros(gain_ref.shape, jnp.float32)
    for sums_ref in sums_refs:
        sums += sums_ref[...].astype(jnp.float32)
    sum_ref[...] = (gain_ref[...].astype(jnp.float32) * sums).astype(jnp.bfloat16)


def own_users(place, sums, user_gain):
    own, factors = sums[0].shape
    first = lambda step, place_ref: (0, 0)
    return pl.pallas_call(
        own_kernel,
        grid_spec=pltpu.PrefetchScalarGridSpec(
            num_scalar_prefetch=1,
            grid=(1,),
            in_specs=[pl.BlockSpec((own, factors), lambda step, place_ref: (place_ref[0], 0))]
            + [pl.BlockSpec((own, factors), first)] * len(sums),
            out_specs=pl.BlockSpec((own, factors), first),
        ),
        out_shape=jax.ShapeDtypeStruct((own, factors), jnp.bfloat16),
        compiler_params=pltpu.CompilerParams(vmem_limit_bytes=VMEM_BYTES),
        cost_estimate=pl.CostEstimate(
            flops=2 * len(sums) * own * factors, bytes_accessed=2 * len(sums) * own * factors, transcendentals=0
        ),
    )(place, user_gain, *sums)


def fold_kernel(sums_ref, part_ref):
    extra = sums_ref[0].astype(jnp.float32)
    for sender in range(1, sums_ref.shape[0]):
        extra += sums_ref[sender].astype(jnp.float32)
    part_ref[...] = jnp.broadcast_to(jnp.sum(extra, axis=0).reshape(1, 1, -1), part_ref.shape)


def fold(sums, copies):
    senders, extended, factors = sums.shape
    return pl.pallas_call(
        fold_kernel,
        grid=(1,),
        in_specs=[pl.BlockSpec((senders, EXTRA, factors), lambda step: (0, extended // EXTRA - 1, 0))],
        out_specs=pl.BlockSpec((copies, 1, factors), lambda step: (0, 0, 0)),
        out_shape=jax.ShapeDtypeStruct((copies, 1, factors), jnp.float32),
        compiler_params=pltpu.CompilerParams(vmem_limit_bytes=VMEM_BYTES // 2),
        cost_estimate=pl.CostEstimate(flops=0, bytes_accessed=2 * senders * EXTRA * factors, transcendentals=0),
    )(sums)


def shape_kernel(per_owner, seat_ref, head_ref, sums_ref, gain_ref, shape_ref, digamma_ref, acc_ref):
    edge = acc_ref.shape[1]
    acc_ref[...] = jnp.zeros_like(acc_ref)
    for sender in range(sums_ref.shape[0]):
        for place in range(per_owner):
            block = head_ref[sender, 0, place * LANES + seat_ref[0]].astype(jnp.int32)
            acc_ref[block] += sums_ref[sender, pl.ds(place * edge, edge), :].astype(jnp.float32)
    for block in range(acc_ref.shape[0]):
        rows = pl.ds(block * edge, edge)
        shape_new = item_prior + gain_ref[rows, :].astype(jnp.float32) * acc_ref[block]
        shape_ref[rows, :] = shape_new
        digamma_ref[rows, :] = digamma(shape_new)


def item_shapes(seat, heads, sums, item_gain, edge, per_owner):
    items, factors = item_gain.shape
    whole = lambda step, seat_ref: (0, 0)
    return pl.pallas_call(
        functools.partial(shape_kernel, per_owner),
        grid_spec=pltpu.PrefetchScalarGridSpec(
            num_scalar_prefetch=1,
            grid=(1,),
            in_specs=[
                pl.BlockSpec(heads.shape, lambda step, seat_ref: (0, 0, 0), memory_space=pltpu.SMEM),
                pl.BlockSpec(sums.shape, lambda step, seat_ref: (0, 0, 0)),
                pl.BlockSpec((items, factors), whole),
            ],
            out_specs=[pl.BlockSpec((items, factors), whole)] * 2,
            scratch_shapes=[pltpu.VMEM((items // edge, edge, factors), jnp.float32)],
        ),
        out_shape=[jax.ShapeDtypeStruct((items, factors), jnp.float32)] * 2,
        compiler_params=pltpu.CompilerParams(vmem_limit_bytes=VMEM_BYTES // 2),
        cost_estimate=pl.CostEstimate(
            flops=40 * items * factors, bytes_accessed=2 * sums.size + 10 * items * factors,
            transcendentals=3 * items * factors,
        ),
    )(seat, heads, sums, item_gain)


def elog_kernel(digamma_ref, level_ref, parts_ref, elog_ref):
    user_total = jnp.sum(parts_ref[...], axis=0)
    elog_ref[...] = digamma_ref[...] - jnp.log(level_ref[...] + user_total)


def item_elogs(digammas, item_level, user_parts):
    items, factors = digammas.shape
    step = items // 2
    row_spec = pl.BlockSpec((step, factors), lambda r: (r, 0))
    return pl.pallas_call(
        elog_kernel,
        grid=(items // step,),
        in_specs=[
            row_spec,
            pl.BlockSpec((step, 1), lambda r: (r, 0)),
            pl.BlockSpec(user_parts.shape, lambda r: (0, 0, 0)),
        ],
        out_specs=row_spec,
        out_shape=jax.ShapeDtypeStruct((items, factors), jnp.float32),
        compiler_params=pltpu.CompilerParams(vmem_limit_bytes=VMEM_BYTES // 2),
        cost_estimate=pl.CostEstimate(
            flops=2 * items * factors, bytes_accessed=8 * items * factors, transcendentals=items * factors
        ),
    )(digammas, item_level, user_parts)


def shards(
    counts, tile_user, tile_slot, live_tiles, touched, user_shape, user_rate, item_shape, item_rate
):
    edge = counts.shape[1]
    users, factors = user_shape.shape
    user_blocks = users // edge
    owners, per_owner = touched.shape
    columns = lax.axis_size("item")
    place = lax.axis_index("item").astype(jnp.int32).reshape(1)
    seat = lax.axis_index("user").astype(jnp.int32).reshape(1)
    item_gain, item_level, heads = item_gains(touched, item_shape, item_rate)
    heads = lax.all_to_all(heads, "user", 0, 0)
    item_rows = lax.all_to_all(pick(seat, heads, item_gain, edge, per_owner), "user", 0, 0)
    user_gain, user_level, turned_gain, column_total = user_gains(user_shape, user_rate, heads)
    item_total = jnp.sum(lax.all_gather(column_total, "item", axis=0, tiled=True), axis=0, keepdims=True)
    dense = dense_counts(
        counts, tile_user, tile_slot, live_tiles, owners * per_owner, user_blocks, item_total
    )
    item_sums, user_sums = sweep(
        place, dense, item_rows, user_gain, turned_gain, user_level, item_total, columns
    )
    item_sums = lax.all_to_all(item_sums, "user", 0, 0)
    user_sums = [user_sums[0]] + [
        lax.ppermute(user_sums[k], "item", [(j, (j + k) % columns) for j in range(columns)])
        for k in range(1, columns)
    ]
    user_sum = lax.all_gather(own_users(place, user_sums, user_gain), "item", axis=0, tiled=True)
    user_shape_new = user_prior + user_sum.astype(jnp.float32)
    user_rate_new = user_level + item_total
    user_parts = lax.all_to_all(fold(item_sums, columns), "item", 0, 0)
    item_shape_new, digammas = item_shapes(seat, heads, item_sums, item_gain, edge, per_owner)
    item_elog = item_elogs(digammas, item_level, user_parts)
    return (user_shape_new, user_rate_new, item_shape_new, item_elog)


def solution(mesh):
    return jax.shard_map(
        shards,
        mesh=mesh,
        in_specs=(
            P(("user", "item"), None, None),
            P(("user", "item")),
            P(("user", "item")),
            P(("user", "item")),
            P(("user", "item"), None),
            P("user", None),
            P("user", None),
            P(("user", "item"), None),
            P(("user", "item"), None),
        ),
        out_specs=(
            P("user", None),
            P("user", None),
            P(("user", "item"), None),
            P(("user", "item"), None),
        ),
        check_vma=False,
    )
```

```python
import functools

import jax
import jax.numpy as jnp
from jax import lax
from jax.experimental import pallas as pl
from jax.experimental.pallas import tpu as pltpu
from jax.sharding import PartitionSpec as P

user_prior = 0.3
activity_prior = 0.3
activity_scale = 1.0
item_prior = 0.3
popularity_prior = 0.3
popularity_scale = 1.0

VMEM_BYTES = 16 << 20
SWEEP_BYTES = 28 << 20
EXTRA = 16
LANES = 128
IN_VMEM = pl.BlockSpec(memory_space=pltpu.VMEM)
IN_SMEM = pl.BlockSpec(memory_space=pltpu.SMEM)
IN_PLACE = pl.BlockSpec(memory_space=pl.ANY)


def in_hbm(array):
    return pltpu.with_memory_space_constraint(array, pltpu.HBM)


def digamma_rest(x):
    w = x * (x + 3.0)
    steps = (2.0 * x + 3.0) * (2.0 * w + 2.0) / (w * (w + 2.0))
    inverse = 1.0 / (x + 4.0)
    z = inverse * inverse
    series = z * (1.0 / 12.0 - z * (1.0 / 120.0 - z * (1.0 / 252.0 - z * (1.0 / 240.0))))
    return steps + 0.5 * inverse + series


def digamma(x):
    return jnp.log(x + 4.0) - digamma_rest(x)


def gains_of(shape_values, rate_values, prior, strength):
    inverse_rate = 1.0 / rate_values
    gain = (shape_values + 4.0) * jnp.exp(-digamma_rest(shape_values)) * inverse_rate
    mean = shape_values * inverse_rate
    return gain.astype(jnp.bfloat16), strength / (prior + jnp.sum(mean, axis=1, keepdims=True)), mean


def item_gain_kernel(strength, touched_ref, shape_ref, rate_ref, gain_ref, level_ref, head_ref):
    turn = pl.program_id(0)
    gain_ref[...], level_ref[...], mean = gains_of(
        shape_ref[...], rate_ref[...], popularity_prior / popularity_scale, strength
    )
    per_owner, devices = touched_ref.shape
    factors = mean.shape[1]
    total = jnp.broadcast_to(jnp.sum(mean, axis=0).reshape(1, 1, factors), (devices, 1, factors))

    @pl.when(turn == 0)
    def _():
        head_ref[...] = jnp.zeros_like(head_ref)
        for place in range(per_owner):
            blocks = touched_ref[pl.ds(place, 1), :].astype(jnp.float32).reshape(1, 1, devices)
            head_ref[:, :, pl.ds(place * LANES, devices)] = jnp.broadcast_to(blocks, (devices, 1, devices))

    head_ref[:, :, pl.ds(per_owner * LANES, factors)] += total


def item_gains(touched, item_shape, item_rate):
    rows, factors = item_shape.shape
    devices, per_owner = touched.shape
    step = rows // 2
    row_spec = pl.BlockSpec((step, factors), lambda r: (r, 0))
    head_shape = (devices, 1, per_owner * LANES + factors)
    return pl.pallas_call(
        functools.partial(item_gain_kernel, popularity_prior + factors * item_prior),
        grid=(rows // step,),
        in_specs=[pl.BlockSpec((per_owner, devices), lambda r: (0, 0)), row_spec, row_spec],
        out_specs=[
            row_spec,
            pl.BlockSpec((step, 1), lambda r: (r, 0)),
            pl.BlockSpec(head_shape, lambda r: (0, 0, 0)),
        ],
        out_shape=[
            jax.ShapeDtypeStruct((rows, factors), jnp.bfloat16),
            jax.ShapeDtypeStruct((rows, 1), jnp.float32),
            jax.ShapeDtypeStruct(head_shape, jnp.float32),
        ],
        compiler_params=pltpu.CompilerParams(vmem_limit_bytes=VMEM_BYTES),
        cost_estimate=pl.CostEstimate(
            flops=40 * rows * factors, bytes_accessed=10 * rows * factors, transcendentals=4 * rows * factors
        ),
    )(touched.T, in_hbm(item_shape), in_hbm(item_rate))


def user_gain_kernel(strength, shape_ref, rate_ref, head_ref, gain_ref, level_ref, turned_ref, column_ref):
    gain, level_ref[...], _ = gains_of(shape_ref[...], rate_ref[...], activity_prior / activity_scale, strength)
    gain_ref[...] = gain
    turned_ref[...] = gain.T

    @pl.when(pl.program_id(0) == 0)
    def _():
        factors = gain.shape[1]
        means = head_ref[:, :, pl.ds(head_ref.shape[2] - factors, factors)]
        column_ref[...] = jnp.sum(means, axis=0).reshape(1, factors)


def user_gains(user_shape, user_rate, heads):
    rows, factors = user_shape.shape
    step = rows // 4
    row_spec = pl.BlockSpec((step, factors), lambda r: (r, 0))
    return pl.pallas_call(
        functools.partial(user_gain_kernel, activity_prior + factors * user_prior),
        grid=(rows // step,),
        in_specs=[row_spec, row_spec, pl.BlockSpec(heads.shape, lambda r: (0, 0, 0))],
        out_specs=[
            row_spec,
            pl.BlockSpec((step, 1), lambda r: (r, 0)),
            pl.BlockSpec((factors, step), lambda r: (0, r)),
            pl.BlockSpec((1, factors), lambda r: (0, 0)),
        ],
        out_shape=[
            jax.ShapeDtypeStruct((rows, factors), jnp.bfloat16),
            jax.ShapeDtypeStruct((rows, 1), jnp.float32),
            jax.ShapeDtypeStruct((factors, rows), jnp.bfloat16),
            jax.ShapeDtypeStruct((1, factors), jnp.float32),
        ],
        compiler_params=pltpu.CompilerParams(vmem_limit_bytes=VMEM_BYTES),
        cost_estimate=pl.CostEstimate(
            flops=40 * rows * factors, bytes_accessed=12 * rows * factors, transcendentals=4 * rows * factors
        ),
    )(in_hbm(user_shape), in_hbm(user_rate), heads)


def pick_kernel(per_owner, seat_ref, head_ref, gain_ref, picked_ref, sent):
    edge = gain_ref.shape[1]
    copies = []
    for device in range(head_ref.shape[0]):
        for place in range(per_owner):
            block = head_ref[device, 0, place * LANES + seat_ref[0]].astype(jnp.int32)
            copies.append(
                pltpu.make_async_copy(
                    gain_ref.at[block],
                    picked_ref.at[device, pl.ds(place * edge, edge)],
                    sent.at[device * per_owner + place],
                )
            )
            copies[-1].start()
    for copy in copies:
        copy.wait()


def pick(seat, heads, item_gain, edge, per_owner):
    items, factors = item_gain.shape
    devices = heads.shape[0]
    return pl.pallas_call(
        functools.partial(pick_kernel, per_owner),
        in_specs=[IN_SMEM, IN_SMEM, IN_VMEM],
        out_specs=IN_PLACE,
        scratch_shapes=[pltpu.SemaphoreType.DMA((devices * per_owner,))],
        out_shape=pltpu.HBM((devices, per_owner * edge, factors), jnp.bfloat16),
        compiler_params=pltpu.CompilerParams(vmem_limit_bytes=VMEM_BYTES),
        cost_estimate=pl.CostEstimate(
            flops=0, bytes_accessed=2 * items * factors + 2 * devices * per_owner * edge * factors, transcendentals=0
        ),
    )(seat, heads, item_gain.reshape(items // edge, edge, factors))


def dense_kernel(user_of, slot_of, live_ref, counts_ref, after_ref, dense_ref, held_ref, arrived):
    depth, group = held_ref.shape[:2]
    live = live_ref[0]
    groups = (live + group - 1) // group

    def fetch(index):
        place = lax.rem(index, depth)
        return pltpu.make_async_copy(
            counts_ref.at[pl.ds(index * group, group)], held_ref.at[place], arrived.at[place]
        )

    for index in range(depth):

        @pl.when(index < groups)
        def _():
            fetch(index).start()

    def clear(slot, carry):
        dense_ref[slot] = jnp.zeros(dense_ref.shape[1:], dense_ref.dtype)
        return carry

    lax.fori_loop(0, dense_ref.shape[0], clear, 0)

    def add_group(index, carry):
        fetch(index).wait()
        place = lax.rem(index, depth)
        for offset in range(group):
            tile = index * group + offset

            @pl.when(tile < live)
            def _():
                user, slot = user_of[tile], slot_of[tile]
                dense_ref[slot, user] += held_ref[place, offset].astype(jnp.float32).astype(jnp.bfloat16)

        @pl.when(index + depth < groups)
        def _():
            fetch(index + depth).start()

        return carry

    lax.fori_loop(0, groups, add_group, 0)


def dense_counts(counts, tile_user, tile_slot, live_tiles, slot_count, user_blocks, after):
    tiles, edge, _ = counts.shape
    group = 8
    depth = min(8, tiles // group)
    return pl.pallas_call(
        dense_kernel,
        in_specs=[IN_SMEM, IN_SMEM, IN_SMEM, IN_PLACE, IN_VMEM],
        out_specs=IN_VMEM,
        scratch_shapes=[
            pltpu.VMEM((depth, group, edge, edge), jnp.int32),
            pltpu.SemaphoreType.DMA((depth,)),
        ],
        out_shape=jax.ShapeDtypeStruct((slot_count, user_blocks, edge, edge), jnp.bfloat16),
        compiler_params=pltpu.CompilerParams(vmem_limit_bytes=VMEM_BYTES),
        cost_estimate=pl.CostEstimate(
            flops=tiles * edge * edge, bytes_accessed=4 * counts.size + 2 * slot_count * user_blocks * edge * edge,
            transcendentals=0,
        ),
    )(tile_user, tile_slot, live_tiles, in_hbm(counts), after)


def split_rows(value, rows):
    high = value.astype(jnp.bfloat16).astype(jnp.float32)
    middle = (value - high).astype(jnp.bfloat16).astype(jnp.float32)
    low = value - high - middle
    row = lax.broadcasted_iota(jnp.int32, (rows, value.shape[1]), 0)
    block = jnp.where(row == 0, high, jnp.where(row == 1, middle, jnp.where(row == 2, low, 0.0)))
    return block.astype(jnp.bfloat16)


def sweep_kernel(
    prior_share, place_ref, dense_ref, items_ref, gain_ref, turned_ref, level_ref, total_ref, item_ref, *rest
):
    user_refs, (acc_ref, early_ref, late_ref, sums_ref, extra_ref, sent) = rest[:-6], rest[-6:]
    owners, touched_rows, factors = items_ref.shape
    slots, user_blocks, edge, _ = dense_ref.shape
    users = user_blocks * edge
    per_owner = slots // owners
    pair = 2
    chunk = users // 2
    last = owners // pair - 1

    def items_of(index):
        return items_ref[pl.ds(index * pair, pair)].reshape(pair * touched_rows, factors)

    def denominators(index):
        turned_items = items_of(index).T
        return [
            jnp.dot(gain_ref[pl.ds(first, chunk), :], turned_items, preferred_element_type=jnp.float32)
            for first in range(0, users, chunk)
        ]

    def put_ratios(index, parts, ratio_ref):
        for place, denominator in enumerate(parts):
            blocks = pl.ds(place * (chunk // edge), chunk // edge)
            counted = jnp.concatenate(
                [
                    dense_ref[index * pair * per_owner + slot, blocks].reshape(chunk, edge)
                    for slot in range(pair * per_owner)
                ],
                axis=1,
            ).astype(jnp.float32)
            inverse = pl.reciprocal(denominator, approx=True)
            inverse *= 2.0 - denominator * inverse
            ratio_ref[pl.ds(place * chunk, chunk), :] = (counted * inverse).astype(jnp.bfloat16)

    def copy_of(index):
        return pltpu.make_async_copy(
            sums_ref.at[pl.ds(index * pair, pair)],
            item_ref.at[pl.ds(index * pair, pair), pl.ds(0, touched_rows)],
            sent.at[index],
        )

    def add_products(index, ratio_ref):
        items = items_of(index)
        for first in range(0, users, chunk):
            rows = pl.ds(first, chunk)
            acc_ref[rows, :] += jnp.dot(ratio_ref[rows, :], items, preferred_element_type=jnp.float32)
        sums = jnp.dot(turned_ref[...], ratio_ref[...], preferred_element_type=jnp.float32)
        sums_ref[pl.ds(index * pair, pair)] = sums.astype(jnp.bfloat16).T.reshape(pair, touched_rows, factors)
        copy_of(index).start()

    acc_ref[...] = jnp.zeros_like(acc_ref)
    put_ratios(0, denominators(0), early_ref)

    def turn(step, carry):
        first, second, third = 2 * step, 2 * step + 1, jnp.minimum(2 * step + 2, last)
        late = denominators(second)
        add_products(first, early_ref)
        put_ratios(second, late, late_ref)
        early = denominators(third)
        add_products(second, late_ref)
        put_ratios(third, early, early_ref)
        return carry

    lax.fori_loop(0, (last + 1) // 2, turn, 0)

    own = users // len(user_refs)
    part = jnp.zeros((1, factors), jnp.float32)
    for ahead, user_ref in enumerate(user_refs):
        target = (place_ref[0] + ahead) % len(user_refs)
        rows = pl.ds(pl.multiple_of(target * own, own), own)
        user_sums = acc_ref[rows, :]
        user_ref[...] = user_sums.astype(jnp.bfloat16)
        shape_share = prior_share + gain_ref[rows, :].astype(jnp.float32) * user_sums
        part += jnp.sum(shape_share / (level_ref[rows, :] + total_ref[...]), axis=0, keepdims=True)
    extra_ref[...] = jnp.broadcast_to(split_rows(part, EXTRA)[None], extra_ref.shape)
    extra_copy = pltpu.make_async_copy(
        extra_ref, item_ref.at[:, pl.ds(touched_rows, EXTRA)], sent.at[last + 1]
    )
    extra_copy.start()
    for index in range(last + 1):
        copy_of(index).wait()
    extra_copy.wait()


def sweep(place, dense, items, user_gain, turned_gain, user_level, item_total, parts):
    owners, touched_rows, factors = items.shape
    users = user_gain.shape[0]
    own = users // parts
    pair = 2
    out = pl.pallas_call(
        functools.partial(sweep_kernel, user_prior / parts),
        in_specs=[IN_SMEM] + [IN_VMEM] * 6,
        out_specs=[IN_PLACE] + [IN_VMEM] * parts,
        scratch_shapes=[
            pltpu.VMEM((users, factors), jnp.float32),
            pltpu.VMEM((users, pair * touched_rows), jnp.bfloat16),
            pltpu.VMEM((users, pair * touched_rows), jnp.bfloat16),
            pltpu.VMEM((owners, touched_rows, factors), jnp.bfloat16),
            pltpu.VMEM((owners, EXTRA, factors), jnp.bfloat16),
            pltpu.SemaphoreType.DMA((owners // pair + 1,)),
        ],
        out_shape=[pltpu.HBM((owners, touched_rows + EXTRA, factors), jnp.bfloat16)]
        + [jax.ShapeDtypeStruct((own, factors), jnp.bfloat16)] * parts,
        compiler_params=pltpu.CompilerParams(vmem_limit_bytes=SWEEP_BYTES),
        cost_estimate=pl.CostEstimate(
            flops=6 * owners * touched_rows * users * factors,
            bytes_accessed=2 * dense.size + 4 * items.size + 4 * users * factors,
            transcendentals=owners * touched_rows * users,
        ),
    )(place, dense, items, user_gain, turned_gain, user_level, item_total)
    return out[0], out[1:]


def own_kernel(place_ref, gain_ref, *rest):
    sums_refs, sum_ref = rest[:-1], rest[-1]
    own = sum_ref.shape[0]
    sums = jnp.zeros(sum_ref.shape, jnp.float32)
    for sums_ref in sums_refs:
        sums += sums_ref[...].astype(jnp.float32)
    gain = gain_ref[pl.ds(pl.multiple_of(place_ref[0] * own, own), own), :]
    sum_ref[...] = (gain.astype(jnp.float32) * sums).astype(jnp.bfloat16)


def own_users(place, sums, user_gain):
    own, factors = sums[0].shape
    return pl.pallas_call(
        own_kernel,
        in_specs=[IN_SMEM] + [IN_VMEM] * (len(sums) + 1),
        out_specs=IN_VMEM,
        out_shape=jax.ShapeDtypeStruct((own, factors), jnp.bfloat16),
        compiler_params=pltpu.CompilerParams(vmem_limit_bytes=VMEM_BYTES),
        cost_estimate=pl.CostEstimate(
            flops=2 * len(sums) * own * factors, bytes_accessed=2 * len(sums) * own * factors, transcendentals=0
        ),
    )(place, user_gain, *sums)


def fold_kernel(sums_ref, after_ref, part_ref):
    extra = sums_ref[0].astype(jnp.float32)
    for sender in range(1, sums_ref.shape[0]):
        extra += sums_ref[sender].astype(jnp.float32)
    part_ref[...] = jnp.broadcast_to(jnp.sum(extra, axis=0).reshape(1, 1, -1), part_ref.shape)


def fold(sums, copies, after):
    senders, extended, factors = sums.shape
    return pl.pallas_call(
        fold_kernel,
        grid=(1,),
        in_specs=[pl.BlockSpec((senders, EXTRA, factors), lambda step: (0, extended // EXTRA - 1, 0)), IN_PLACE],
        out_specs=pl.BlockSpec((copies, 1, factors), lambda step: (0, 0, 0)),
        out_shape=jax.ShapeDtypeStruct((copies, 1, factors), jnp.float32),
        compiler_params=pltpu.CompilerParams(vmem_limit_bytes=VMEM_BYTES),
        cost_estimate=pl.CostEstimate(flops=0, bytes_accessed=2 * senders * EXTRA * factors, transcendentals=0),
    )(sums, after)


def shape_kernel(per_owner, seat_ref, head_ref, sums_ref, gain_ref, shape_ref, digamma_ref, acc_ref):
    edge = acc_ref.shape[1]
    acc_ref[...] = jnp.zeros_like(acc_ref)
    for sender in range(sums_ref.shape[0]):
        for place in range(per_owner):
            block = head_ref[sender, 0, place * LANES + seat_ref[0]].astype(jnp.int32)
            acc_ref[block] += sums_ref[sender, pl.ds(place * edge, edge), :].astype(jnp.float32)
    for block in range(acc_ref.shape[0]):
        rows = pl.ds(block * edge, edge)
        shape_new = item_prior + gain_ref[rows, :].astype(jnp.float32) * acc_ref[block]
        shape_ref[rows, :] = shape_new
        digamma_ref[rows, :] = digamma(shape_new)


def item_shapes(seat, heads, sums, item_gain, edge, per_owner):
    items, factors = item_gain.shape
    whole = lambda step, seat_ref: (0, 0)
    return pl.pallas_call(
        functools.partial(shape_kernel, per_owner),
        grid_spec=pltpu.PrefetchScalarGridSpec(
            num_scalar_prefetch=1,
            grid=(1,),
            in_specs=[
                pl.BlockSpec(heads.shape, lambda step, seat_ref: (0, 0, 0), memory_space=pltpu.SMEM),
                pl.BlockSpec(sums.shape, lambda step, seat_ref: (0, 0, 0)),
                pl.BlockSpec((items, factors), whole),
            ],
            out_specs=[pl.BlockSpec((items, factors), whole)] * 2,
            scratch_shapes=[pltpu.VMEM((items // edge, edge, factors), jnp.float32)],
        ),
        out_shape=[jax.ShapeDtypeStruct((items, factors), jnp.float32)] * 2,
        compiler_params=pltpu.CompilerParams(vmem_limit_bytes=VMEM_BYTES),
        cost_estimate=pl.CostEstimate(
            flops=40 * items * factors, bytes_accessed=2 * sums.size + 10 * items * factors,
            transcendentals=3 * items * factors,
        ),
    )(seat, heads, sums, item_gain)


def elog_kernel(digamma_ref, level_ref, parts_ref, elog_ref):
    user_total = jnp.sum(parts_ref[...], axis=0)
    elog_ref[...] = digamma_ref[...] - jnp.log(level_ref[...] + user_total)


def item_elogs(digammas, item_level, user_parts):
    items, factors = digammas.shape
    step = items // 2
    row_spec = pl.BlockSpec((step, factors), lambda r: (r, 0))
    return pl.pallas_call(
        elog_kernel,
        grid=(items // step,),
        in_specs=[
            row_spec,
            pl.BlockSpec((step, 1), lambda r: (r, 0)),
            pl.BlockSpec(user_parts.shape, lambda r: (0, 0, 0)),
        ],
        out_specs=row_spec,
        out_shape=jax.ShapeDtypeStruct((items, factors), jnp.float32),
        compiler_params=pltpu.CompilerParams(vmem_limit_bytes=VMEM_BYTES),
        cost_estimate=pl.CostEstimate(
            flops=2 * items * factors, bytes_accessed=8 * items * factors, transcendentals=items * factors
        ),
    )(digammas, item_level, user_parts)


def shards(
    counts, tile_user, tile_slot, live_tiles, touched, user_shape, user_rate, item_shape, item_rate
):
    edge = counts.shape[1]
    users, factors = user_shape.shape
    user_blocks = users // edge
    owners, per_owner = touched.shape
    columns = lax.axis_size("item")
    place = lax.axis_index("item").astype(jnp.int32).reshape(1)
    seat = lax.axis_index("user").astype(jnp.int32).reshape(1)
    item_gain, item_level, heads = item_gains(touched, item_shape, item_rate)
    heads = lax.all_to_all(heads, "user", 0, 0)
    item_rows = lax.all_to_all(pick(seat, heads, item_gain, edge, per_owner), "user", 0, 0)
    user_gain, user_level, turned_gain, column_total = user_gains(user_shape, user_rate, heads)
    item_total = jnp.sum(lax.all_gather(column_total, "item", axis=0, tiled=True), axis=0, keepdims=True)
    dense = dense_counts(
        counts, tile_user, tile_slot, live_tiles, owners * per_owner, user_blocks, item_total
    )
    item_sums, user_sums = sweep(
        place, dense, item_rows, user_gain, turned_gain, user_level, item_total, columns
    )
    item_sums = lax.all_to_all(item_sums, "user", 0, 0)
    user_sums = [user_sums[0]] + [
        lax.ppermute(user_sums[k], "item", [(j, (j + k) % columns) for j in range(columns)])
        for k in range(1, columns)
    ]
    user_sum = lax.all_gather(own_users(place, user_sums, user_gain), "item", axis=0, tiled=True)
    user_shape_new = user_prior + user_sum.astype(jnp.float32)
    user_rate_new = user_level + item_total
    user_parts = lax.all_to_all(fold(item_sums, columns, user_shape_new), "item", 0, 0)
    item_shape_new, digammas = item_shapes(seat, heads, item_sums, item_gain, edge, per_owner)
    item_elog = item_elogs(digammas, item_level, user_parts)
    return (user_shape_new, user_rate_new, item_shape_new, item_elog)


def solution(mesh):
    return jax.shard_map(
        shards,
        mesh=mesh,
        in_specs=(
            P(("user", "item"), None, None),
            P(("user", "item")),
            P(("user", "item")),
            P(("user", "item")),
            P(("user", "item"), None),
            P("user", None),
            P("user", None),
            P(("user", "item"), None),
            P(("user", "item"), None),
        ),
        out_specs=(
            P("user", None),
            P("user", None),
            P(("user", "item"), None),
            P(("user", "item"), None),
        ),
        check_vma=False,
    )
```

```python
import functools

import jax
import jax.numpy as jnp
from jax import lax
from jax.experimental import pallas as pl
from jax.experimental.pallas import tpu as pltpu
from jax.sharding import PartitionSpec as P

user_prior = 0.3
activity_prior = 0.3
activity_scale = 1.0
item_prior = 0.3
popularity_prior = 0.3
popularity_scale = 1.0

VMEM_BYTES = 24 << 20
SWEEP_BYTES = 36 << 20
EXTRA = 16
LANES = 128
IN_VMEM = pl.BlockSpec(memory_space=pltpu.VMEM)
IN_SMEM = pl.BlockSpec(memory_space=pltpu.SMEM)
IN_PLACE = pl.BlockSpec(memory_space=pl.ANY)


def in_hbm(array):
    return pltpu.with_memory_space_constraint(array, pltpu.HBM)


def digamma_rest(x):
    w = x * (x + 3.0)
    steps = (2.0 * x + 3.0) * (2.0 * w + 2.0) / (w * (w + 2.0))
    inverse = 1.0 / (x + 4.0)
    z = inverse * inverse
    series = z * (1.0 / 12.0 - z * (1.0 / 120.0 - z * (1.0 / 252.0 - z * (1.0 / 240.0))))
    return steps + 0.5 * inverse + series


def digamma(x):
    return jnp.log(x + 4.0) - digamma_rest(x)


def gains_of(shape_values, rate_values, prior, strength):
    inverse_rate = 1.0 / rate_values
    gain = (shape_values + 4.0) * jnp.exp(-digamma_rest(shape_values)) * inverse_rate
    mean = shape_values * inverse_rate
    return gain.astype(jnp.bfloat16), strength / (prior + jnp.sum(mean, axis=1, keepdims=True)), mean


def head_kernel(touched_ref, shape_from, rate_from, head_ref, shape_ref, rate_ref, arrived):
    per_owner, devices = touched_ref.shape
    rows, factors = shape_ref.shape
    parts = arrived.shape[1]
    step = rows // parts

    def fetch(part):
        piece = pl.ds(part * step, step)
        return [
            pltpu.make_async_copy(shape_from.at[piece], shape_ref.at[piece], arrived.at[0, part]),
            pltpu.make_async_copy(rate_from.at[piece], rate_ref.at[piece], arrived.at[1, part]),
        ]

    for part in range(parts):
        for copy in fetch(part):
            copy.start()
    head_ref[...] = jnp.zeros_like(head_ref)
    for place in range(per_owner):
        blocks = touched_ref[pl.ds(place, 1), :].astype(jnp.float32).reshape(1, 1, devices)
        head_ref[:, :, pl.ds(place * LANES, devices)] = jnp.broadcast_to(blocks, (devices, 1, devices))
    total = jnp.zeros((1, factors), jnp.float32)
    for part in range(parts):
        for copy in fetch(part):
            copy.wait()
        piece = pl.ds(part * step, step)
        total += jnp.sum(shape_ref[piece, :] / rate_ref[piece, :], axis=0, keepdims=True)
    head_ref[:, :, pl.ds(per_owner * LANES, factors)] = jnp.broadcast_to(
        total.reshape(1, 1, factors), (devices, 1, factors)
    )


def head_of(touched, item_shape, item_rate):
    rows, factors = item_shape.shape
    devices, per_owner = touched.shape
    head_shape = (devices, 1, per_owner * LANES + factors)
    return pl.pallas_call(
        head_kernel,
        grid=(1,),
        in_specs=[pl.BlockSpec((per_owner, devices), lambda r: (0, 0)), IN_PLACE, IN_PLACE],
        out_specs=pl.BlockSpec(head_shape, lambda r: (0, 0, 0)),
        out_shape=pltpu.HBM(head_shape, jnp.float32),
        scratch_shapes=[
            pltpu.VMEM((rows, factors), jnp.float32),
            pltpu.VMEM((rows, factors), jnp.float32),
            pltpu.SemaphoreType.DMA((2, 4)),
        ],
        compiler_params=pltpu.CompilerParams(vmem_limit_bytes=VMEM_BYTES),
        cost_estimate=pl.CostEstimate(
            flops=4 * rows * factors, bytes_accessed=8 * rows * factors, transcendentals=rows * factors
        ),
    )(in_hbm(touched.T), in_hbm(item_shape), in_hbm(item_rate))


def item_gain_kernel(strength, shape_ref, rate_ref, gain_ref, level_ref):
    gain_ref[...], level_ref[...], _ = gains_of(
        shape_ref[...], rate_ref[...], popularity_prior / popularity_scale, strength
    )


def item_gains(item_shape, item_rate):
    rows, factors = item_shape.shape
    step = rows // 2
    row_spec = pl.BlockSpec((step, factors), lambda r: (r, 0))
    return pl.pallas_call(
        functools.partial(item_gain_kernel, popularity_prior + factors * item_prior),
        grid=(rows // step,),
        in_specs=[row_spec, row_spec],
        out_specs=[row_spec, pl.BlockSpec((step, 1), lambda r: (r, 0))],
        out_shape=[
            pltpu.HBM((rows, factors), jnp.bfloat16),
            pltpu.HBM((rows, 1), jnp.float32),
        ],
        compiler_params=pltpu.CompilerParams(vmem_limit_bytes=VMEM_BYTES),
        cost_estimate=pl.CostEstimate(
            flops=40 * rows * factors, bytes_accessed=10 * rows * factors, transcendentals=4 * rows * factors
        ),
    )(in_hbm(item_shape), in_hbm(item_rate))


def user_gain_kernel(strength, shape_ref, rate_ref, head_ref, gain_ref, level_ref, turned_ref, column_ref):
    gain, level_ref[...], _ = gains_of(shape_ref[...], rate_ref[...], activity_prior / activity_scale, strength)
    gain_ref[...] = gain
    turned_ref[...] = gain.T

    @pl.when(pl.program_id(0) == 0)
    def _():
        factors = gain.shape[1]
        means = head_ref[:, :, pl.ds(head_ref.shape[2] - factors, factors)]
        column_ref[...] = jnp.sum(means, axis=0).reshape(1, factors)


def user_gains(user_shape, user_rate, heads):
    rows, factors = user_shape.shape
    step = rows // 4
    row_spec = pl.BlockSpec((step, factors), lambda r: (r, 0))
    return pl.pallas_call(
        functools.partial(user_gain_kernel, activity_prior + factors * user_prior),
        grid=(rows // step,),
        in_specs=[row_spec, row_spec, pl.BlockSpec(heads.shape, lambda r: (0, 0, 0))],
        out_specs=[
            row_spec,
            pl.BlockSpec((step, 1), lambda r: (r, 0)),
            pl.BlockSpec((factors, step), lambda r: (0, r)),
            pl.BlockSpec((1, factors), lambda r: (0, 0)),
        ],
        out_shape=[
            pltpu.HBM((rows, factors), jnp.bfloat16),
            pltpu.HBM((rows, 1), jnp.float32),
            pltpu.HBM((factors, rows), jnp.bfloat16),
            pltpu.HBM((1, factors), jnp.float32),
        ],
        compiler_params=pltpu.CompilerParams(vmem_limit_bytes=VMEM_BYTES),
        cost_estimate=pl.CostEstimate(
            flops=40 * rows * factors, bytes_accessed=12 * rows * factors, transcendentals=4 * rows * factors
        ),
    )(in_hbm(user_shape), in_hbm(user_rate), heads)


def pick_kernel(per_owner, seat_ref, head_ref, gain_from, picked_ref, gain_ref, arrived, sent):
    blocks, edge, _ = gain_ref.shape
    fetches = [
        pltpu.make_async_copy(gain_from.at[block], gain_ref.at[block], arrived.at[block]) for block in range(blocks)
    ]
    for copy in fetches:
        copy.start()
    for copy in fetches:
        copy.wait()
    copies = []
    for device in range(head_ref.shape[0]):
        for place in range(per_owner):
            block = head_ref[device, 0, place * LANES + seat_ref[0]].astype(jnp.int32)
            copies.append(
                pltpu.make_async_copy(
                    gain_ref.at[block],
                    picked_ref.at[device, pl.ds(place * edge, edge)],
                    sent.at[device * per_owner + place],
                )
            )
            copies[-1].start()
    for copy in copies:
        copy.wait()


def pick(seat, heads, item_gain, edge, per_owner):
    items, factors = item_gain.shape
    devices = heads.shape[0]
    return pl.pallas_call(
        functools.partial(pick_kernel, per_owner),
        in_specs=[IN_SMEM, IN_SMEM, IN_PLACE],
        out_specs=IN_PLACE,
        scratch_shapes=[
            pltpu.VMEM((items // edge, edge, factors), jnp.bfloat16),
            pltpu.SemaphoreType.DMA((items // edge,)),
            pltpu.SemaphoreType.DMA((devices * per_owner,)),
        ],
        out_shape=pltpu.HBM((devices, per_owner * edge, factors), jnp.bfloat16),
        compiler_params=pltpu.CompilerParams(vmem_limit_bytes=VMEM_BYTES),
        cost_estimate=pl.CostEstimate(
            flops=0, bytes_accessed=2 * items * factors + 2 * devices * per_owner * edge * factors, transcendentals=0
        ),
    )(seat, heads, in_hbm(item_gain.reshape(items // edge, edge, factors)))


def dense_kernel(user_of, slot_of, live_ref, counts_ref, after_ref, out_ref, dense_ref, held_ref, arrived, sent):
    depth, group = held_ref.shape[:2]
    live = live_ref[0]
    groups = (live + group - 1) // group

    def fetch(index):
        place = lax.rem(index, depth)
        return pltpu.make_async_copy(
            counts_ref.at[pl.ds(index * group, group)], held_ref.at[place], arrived.at[place]
        )

    for index in range(depth):

        @pl.when(index < groups)
        def _():
            fetch(index).start()

    def clear(slot, carry):
        dense_ref[slot] = jnp.zeros(dense_ref.shape[1:], dense_ref.dtype)
        return carry

    lax.fori_loop(0, dense_ref.shape[0], clear, 0)

    def add_group(index, carry):
        fetch(index).wait()
        place = lax.rem(index, depth)
        for offset in range(group):
            tile = index * group + offset

            @pl.when(tile < live)
            def _():
                user, slot = user_of[tile], slot_of[tile]
                dense_ref[slot, user] += held_ref[place, offset].astype(jnp.float32).astype(jnp.bfloat16)

        @pl.when(index + depth < groups)
        def _():
            fetch(index + depth).start()

        return carry

    lax.fori_loop(0, groups, add_group, 0)
    slots = dense_ref.shape[0] // sent.shape[0]
    copies = [
        pltpu.make_async_copy(
            dense_ref.at[pl.ds(part * slots, slots)], out_ref.at[pl.ds(part * slots, slots)], sent.at[part]
        )
        for part in range(sent.shape[0])
    ]
    for copy in copies:
        copy.start()
    for copy in copies:
        copy.wait()


def dense_counts(counts, tile_user, tile_slot, live_tiles, slot_count, user_blocks, after):
    tiles, edge, _ = counts.shape
    group = 8
    depth = min(8, tiles // group)
    return pl.pallas_call(
        dense_kernel,
        in_specs=[IN_SMEM, IN_SMEM, IN_SMEM, IN_PLACE, IN_VMEM],
        out_specs=IN_PLACE,
        scratch_shapes=[
            pltpu.VMEM((slot_count, user_blocks, edge, edge), jnp.bfloat16),
            pltpu.VMEM((depth, group, edge, edge), jnp.int32),
            pltpu.SemaphoreType.DMA((depth,)),
            pltpu.SemaphoreType.DMA((16,)),
        ],
        out_shape=pltpu.HBM((slot_count, user_blocks, edge, edge), jnp.bfloat16),
        compiler_params=pltpu.CompilerParams(vmem_limit_bytes=VMEM_BYTES),
        cost_estimate=pl.CostEstimate(
            flops=tiles * edge * edge, bytes_accessed=4 * counts.size + 2 * slot_count * user_blocks * edge * edge,
            transcendentals=0,
        ),
    )(tile_user, tile_slot, live_tiles, in_hbm(counts), after)


def split_rows(value, rows):
    high = value.astype(jnp.bfloat16).astype(jnp.float32)
    middle = (value - high).astype(jnp.bfloat16).astype(jnp.float32)
    low = value - high - middle
    row = lax.broadcasted_iota(jnp.int32, (rows, value.shape[1]), 0)
    block = jnp.where(row == 0, high, jnp.where(row == 1, middle, jnp.where(row == 2, low, 0.0)))
    return block.astype(jnp.bfloat16)


def sweep_kernel(
    prior_share, place_ref, dense_from, items_ref, gain_from, turned_from, level_from, total_ref, item_ref, *rest
):
    user_outs, rest = rest[:-12], rest[-12:]
    dense_ref, gain_ref, turned_ref, level_ref, acc_ref, early_ref, late_ref, sums_ref, extra_ref, users_ref = rest[:10]
    arrived, sent = rest[10:]
    owners, touched_rows, factors = items_ref.shape
    slots, user_blocks, edge, _ = dense_ref.shape
    users = user_blocks * edge
    per_owner = slots // owners
    pair = 2
    chunk = users // 2
    last = owners // pair - 1

    def items_of(index):
        return items_ref[pl.ds(index * pair, pair)].reshape(pair * touched_rows, factors)

    def denominators(index):
        turned_items = items_of(index).T
        return [
            jnp.dot(gain_ref[pl.ds(first, chunk), :], turned_items, preferred_element_type=jnp.float32)
            for first in range(0, users, chunk)
        ]

    def put_ratios(index, parts, ratio_ref):
        for place, denominator in enumerate(parts):
            blocks = pl.ds(place * (chunk // edge), chunk // edge)
            counted = jnp.concatenate(
                [
                    dense_ref[index * pair * per_owner + slot, blocks].reshape(chunk, edge)
                    for slot in range(pair * per_owner)
                ],
                axis=1,
            ).astype(jnp.float32)
            inverse = pl.reciprocal(denominator, approx=True)
            inverse *= 2.0 - denominator * inverse
            ratio_ref[pl.ds(place * chunk, chunk), :] = (counted * inverse).astype(jnp.bfloat16)

    def copy_of(index):
        return pltpu.make_async_copy(
            sums_ref.at[pl.ds(index * pair, pair)],
            item_ref.at[pl.ds(index * pair, pair), pl.ds(0, touched_rows)],
            sent.at[index],
        )

    def add_products(index, ratio_ref):
        items = items_of(index)
        for first in range(0, users, chunk):
            rows = pl.ds(first, chunk)
            acc_ref[rows, :] += jnp.dot(ratio_ref[rows, :], items, preferred_element_type=jnp.float32)
        sums = jnp.dot(turned_ref[...], ratio_ref[...], preferred_element_type=jnp.float32)
        sums_ref[pl.ds(index * pair, pair)] = sums.astype(jnp.bfloat16).T.reshape(pair, touched_rows, factors)
        copy_of(index).start()

    def fetch(index):
        slots_of = pl.ds(index * pair * per_owner, pair * per_owner)
        return pltpu.make_async_copy(dense_from.at[slots_of], dense_ref.at[slots_of], arrived.at[index])

    gain_rows = [pl.ds(first, chunk) for first in range(0, users, chunk)]
    first_copies = [
        pltpu.make_async_copy(gain_from.at[rows], gain_ref.at[rows], arrived.at[last + 1 + place])
        for place, rows in enumerate(gain_rows)
    ]
    later_copies = [
        pltpu.make_async_copy(source, target, arrived.at[last + 3 + place])
        for place, (source, target) in enumerate(((turned_from, turned_ref), (level_from, level_ref)))
    ]
    first_copies[0].start()
    fetch(0).start()
    first_copies[1].start()
    acc_ref[...] = jnp.zeros_like(acc_ref)
    for copy in first_copies:
        copy.wait()
    later_copies[0].start()
    for index in range(1, last + 1):
        fetch(index).start()
    later_copies[1].start()
    fetch(0).wait()
    put_ratios(0, denominators(0), early_ref)
    later_copies[0].wait()

    def turn(step, carry):
        first, second, third = 2 * step, 2 * step + 1, jnp.minimum(2 * step + 2, last)
        fetch(second).wait()

        @pl.when(third > second)
        def _():
            fetch(third).wait()

        late = denominators(second)
        add_products(first, early_ref)
        put_ratios(second, late, late_ref)
        early = denominators(third)
        add_products(second, late_ref)
        put_ratios(third, early, early_ref)
        return carry

    lax.fori_loop(0, (last + 1) // 2, turn, 0)

    own = users // len(user_outs)
    copies = []
    for ahead, user_out in enumerate(user_outs):
        target = (place_ref[0] + ahead) % len(user_outs)
        rows = pl.ds(pl.multiple_of(target * own, own), own)
        users_ref[ahead] = acc_ref[rows, :].astype(jnp.bfloat16)
        copies.append(pltpu.make_async_copy(users_ref.at[ahead], user_out, sent.at[last + 2 + ahead]))
        copies[-1].start()
    later_copies[1].wait()
    part = jnp.zeros((1, factors), jnp.float32)
    for first in range(0, users, own):
        rows = pl.ds(first, own)
        shape_share = prior_share + gain_ref[rows, :].astype(jnp.float32) * acc_ref[rows, :]
        part += jnp.sum(shape_share / (level_ref[rows, :] + total_ref[...]), axis=0, keepdims=True)
    extra_ref[...] = jnp.broadcast_to(split_rows(part, EXTRA)[None], extra_ref.shape)
    copies.append(
        pltpu.make_async_copy(extra_ref, item_ref.at[:, pl.ds(touched_rows, EXTRA)], sent.at[last + 1])
    )
    copies[-1].start()
    for index in range(last + 1):
        copy_of(index).wait()
    for copy in copies:
        copy.wait()


def sweep(place, dense, items, user_gain, turned_gain, user_level, item_total, parts):
    owners, touched_rows, factors = items.shape
    users = user_gain.shape[0]
    own = users // parts
    pair = 2
    out = pl.pallas_call(
        functools.partial(sweep_kernel, user_prior / parts),
        in_specs=[IN_SMEM, IN_PLACE, IN_VMEM, IN_PLACE, IN_PLACE, IN_PLACE, IN_VMEM],
        out_specs=[IN_PLACE] * (parts + 1),
        scratch_shapes=[
            pltpu.VMEM(dense.shape, jnp.bfloat16),
            pltpu.VMEM((users, factors), jnp.bfloat16),
            pltpu.VMEM((factors, users), jnp.bfloat16),
            pltpu.VMEM((users, 1), jnp.float32),
            pltpu.VMEM((users, factors), jnp.float32),
            pltpu.VMEM((users, pair * touched_rows), jnp.bfloat16),
            pltpu.VMEM((users, pair * touched_rows), jnp.bfloat16),
            pltpu.VMEM((owners, touched_rows, factors), jnp.bfloat16),
            pltpu.VMEM((owners, EXTRA, factors), jnp.bfloat16),
            pltpu.VMEM((parts, own, factors), jnp.bfloat16),
            pltpu.SemaphoreType.DMA((owners // pair + 4,)),
            pltpu.SemaphoreType.DMA((owners // pair + 1 + parts,)),
        ],
        out_shape=[pltpu.HBM((owners, touched_rows + EXTRA, factors), jnp.bfloat16)]
        + [pltpu.HBM((own, factors), jnp.bfloat16)] * parts,
        compiler_params=pltpu.CompilerParams(vmem_limit_bytes=SWEEP_BYTES),
        cost_estimate=pl.CostEstimate(
            flops=6 * owners * touched_rows * users * factors,
            bytes_accessed=2 * dense.size + 4 * items.size + 4 * users * factors,
            transcendentals=owners * touched_rows * users,
        ),
    )(place, in_hbm(dense), items, in_hbm(user_gain), in_hbm(turned_gain), in_hbm(user_level), item_total)
    return out[0], out[1:]


def own_kernel(place_ref, gain_ref, *rest):
    sums_refs, sum_ref = rest[:-1], rest[-1]
    sums = jnp.zeros(sum_ref.shape, jnp.float32)
    for sums_ref in sums_refs:
        sums += sums_ref[...].astype(jnp.float32)
    sum_ref[...] = (gain_ref[...].astype(jnp.float32) * sums).astype(jnp.bfloat16)


def own_users(place, sums, user_gain):
    own, factors = sums[0].shape
    first = lambda step, place_ref: (0, 0)
    return pl.pallas_call(
        own_kernel,
        grid_spec=pltpu.PrefetchScalarGridSpec(
            num_scalar_prefetch=1,
            grid=(1,),
            in_specs=[pl.BlockSpec((own, factors), lambda step, place_ref: (place_ref[0], 0))]
            + [pl.BlockSpec((own, factors), first)] * len(sums),
            out_specs=pl.BlockSpec((own, factors), first),
        ),
        out_shape=pltpu.HBM((own, factors), jnp.bfloat16),
        compiler_params=pltpu.CompilerParams(vmem_limit_bytes=VMEM_BYTES),
        cost_estimate=pl.CostEstimate(
            flops=2 * len(sums) * own * factors, bytes_accessed=2 * len(sums) * own * factors, transcendentals=0
        ),
    )(place, in_hbm(user_gain), *sums)


def fold_kernel(sums_ref, shape_after_ref, rate_after_ref, part_ref):
    extra = sums_ref[0].astype(jnp.float32)
    for sender in range(1, sums_ref.shape[0]):
        extra += sums_ref[sender].astype(jnp.float32)
    part_ref[...] = jnp.broadcast_to(jnp.sum(extra, axis=0).reshape(1, 1, -1), part_ref.shape)


def fold(sums, copies, *after):
    senders, extended, factors = sums.shape
    return pl.pallas_call(
        fold_kernel,
        grid=(1,),
        in_specs=[pl.BlockSpec((senders, EXTRA, factors), lambda step: (0, extended // EXTRA - 1, 0)), IN_PLACE, IN_PLACE],
        out_specs=pl.BlockSpec((copies, 1, factors), lambda step: (0, 0, 0)),
        out_shape=pltpu.HBM((copies, 1, factors), jnp.float32),
        compiler_params=pltpu.CompilerParams(vmem_limit_bytes=VMEM_BYTES),
        cost_estimate=pl.CostEstimate(flops=0, bytes_accessed=2 * senders * EXTRA * factors, transcendentals=0),
    )(sums, *(in_hbm(array) for array in after))


def shape_kernel(
    per_owner, seat_ref, head_ref, sums_ref, gain_from, shape_out, digamma_ref, acc_ref, gain_ref, shape_ref, arrived, sent
):
    blocks, edge, _ = acc_ref.shape
    fetch = pltpu.make_async_copy(gain_from, gain_ref, arrived)
    fetch.start()
    acc_ref[...] = jnp.zeros_like(acc_ref)
    for sender in range(sums_ref.shape[0]):
        for place in range(per_owner):
            block = head_ref[sender, 0, place * LANES + seat_ref[0]].astype(jnp.int32)
            acc_ref[block] += sums_ref[sender, pl.ds(place * edge, edge), :].astype(jnp.float32)
    fetch.wait()
    copies = []
    for block in range(blocks):
        rows = pl.ds(block * edge, edge)
        shape_new = item_prior + gain_ref[rows, :].astype(jnp.float32) * acc_ref[block]
        shape_ref[rows, :] = shape_new
        copies.append(pltpu.make_async_copy(shape_ref.at[rows], shape_out.at[rows], sent.at[block]))
        copies[-1].start()
        digamma_ref[rows, :] = digamma(shape_new)
    for copy in copies:
        copy.wait()


def item_shapes(seat, heads, sums, item_gain, edge, per_owner):
    items, factors = item_gain.shape
    return pl.pallas_call(
        functools.partial(shape_kernel, per_owner),
        in_specs=[IN_SMEM, IN_SMEM, IN_VMEM, IN_PLACE],
        out_specs=[IN_PLACE, IN_VMEM],
        scratch_shapes=[
            pltpu.VMEM((items // edge, edge, factors), jnp.float32),
            pltpu.VMEM((items, factors), jnp.bfloat16),
            pltpu.VMEM((items, factors), jnp.float32),
            pltpu.SemaphoreType.DMA,
            pltpu.SemaphoreType.DMA((items // edge,)),
        ],
        out_shape=[pltpu.HBM((items, factors), jnp.float32), jax.ShapeDtypeStruct((items, factors), jnp.float32)],
        compiler_params=pltpu.CompilerParams(vmem_limit_bytes=VMEM_BYTES),
        cost_estimate=pl.CostEstimate(
            flops=40 * items * factors, bytes_accessed=2 * sums.size + 10 * items * factors,
            transcendentals=3 * items * factors,
        ),
    )(seat, heads, sums, in_hbm(item_gain))


def elog_kernel(digamma_ref, level_ref, parts_ref, elog_out, elog_ref, sent):
    user_total = jnp.sum(parts_ref[...], axis=0)
    step = elog_ref.shape[0] // sent.shape[0]
    copies = []
    for piece in range(sent.shape[0]):
        rows = pl.ds(piece * step, step)
        elog_ref[rows, :] = digamma_ref[rows, :] - jnp.log(level_ref[rows, :] + user_total)
        copies.append(pltpu.make_async_copy(elog_ref.at[rows], elog_out.at[rows], sent.at[piece]))
        copies[-1].start()
    for copy in copies:
        copy.wait()


def item_elogs(digammas, item_level, user_parts):
    items, factors = digammas.shape
    return pl.pallas_call(
        elog_kernel,
        in_specs=[IN_VMEM, IN_VMEM, IN_VMEM],
        out_specs=IN_PLACE,
        scratch_shapes=[pltpu.VMEM((items, factors), jnp.float32), pltpu.SemaphoreType.DMA((4,))],
        out_shape=pltpu.HBM((items, factors), jnp.float32),
        compiler_params=pltpu.CompilerParams(vmem_limit_bytes=VMEM_BYTES),
        cost_estimate=pl.CostEstimate(
            flops=2 * items * factors, bytes_accessed=8 * items * factors, transcendentals=items * factors
        ),
    )(digammas, item_level, user_parts)


def shards(
    counts, tile_user, tile_slot, live_tiles, touched, user_shape, user_rate, item_shape, item_rate
):
    edge = counts.shape[1]
    users, factors = user_shape.shape
    user_blocks = users // edge
    owners, per_owner = touched.shape
    columns = lax.axis_size("item")
    place = lax.axis_index("item").astype(jnp.int32).reshape(1)
    seat = lax.axis_index("user").astype(jnp.int32).reshape(1)
    heads = lax.all_to_all(head_of(touched, item_shape, item_rate), "user", 0, 0)
    item_gain, item_level = item_gains(item_shape, item_rate)
    item_rows = lax.all_to_all(pick(seat, heads, item_gain, edge, per_owner), "user", 0, 0)
    user_gain, user_level, turned_gain, column_total = user_gains(user_shape, user_rate, heads)
    item_total = jnp.sum(lax.all_gather(column_total, "item", axis=0, tiled=True), axis=0, keepdims=True)
    dense = dense_counts(
        counts, tile_user, tile_slot, live_tiles, owners * per_owner, user_blocks, item_total
    )
    item_sums, user_sums = sweep(
        place, dense, item_rows, user_gain, turned_gain, user_level, item_total, columns
    )
    item_sums = lax.all_to_all(item_sums, "user", 0, 0)
    user_sums = [user_sums[0]] + [
        lax.ppermute(user_sums[k], "item", [(j, (j + k) % columns) for j in range(columns)])
        for k in range(1, columns)
    ]
    user_sum = lax.all_gather(own_users(place, user_sums, user_gain), "item", axis=0, tiled=True)
    user_shape_new = user_prior + user_sum.astype(jnp.float32)
    user_rate_new = user_level + item_total
    user_parts = lax.all_to_all(fold(item_sums, columns, user_shape_new, user_rate_new), "item", 0, 0)
    item_shape_new, digammas = item_shapes(seat, heads, item_sums, item_gain, edge, per_owner)
    item_elog = item_elogs(digammas, item_level, user_parts)
    return (user_shape_new, user_rate_new, item_shape_new, item_elog)


def solution(mesh):
    return jax.shard_map(
        shards,
        mesh=mesh,
        in_specs=(
            P(("user", "item"), None, None),
            P(("user", "item")),
            P(("user", "item")),
            P(("user", "item")),
            P(("user", "item"), None),
            P("user", None),
            P("user", None),
            P(("user", "item"), None),
            P(("user", "item"), None),
        ),
        out_specs=(
            P("user", None),
            P("user", None),
            P(("user", "item"), None),
            P(("user", "item"), None),
        ),
        check_vma=False,
    )
```

```python
import functools

import jax
import jax.numpy as jnp
from jax import lax
from jax.experimental import pallas as pl
from jax.experimental.pallas import tpu as pltpu
from jax.sharding import PartitionSpec as P

user_prior = 0.3
activity_prior = 0.3
activity_scale = 1.0
item_prior = 0.3
popularity_prior = 0.3
popularity_scale = 1.0

VMEM_BYTES = 24 << 20
SWEEP_BYTES = 36 << 20
EXTRA = 16
LANES = 128
IN_VMEM = pl.BlockSpec(memory_space=pltpu.VMEM)
IN_SMEM = pl.BlockSpec(memory_space=pltpu.SMEM)
IN_PLACE = pl.BlockSpec(memory_space=pl.ANY)


def in_hbm(array):
    return pltpu.with_memory_space_constraint(array, pltpu.HBM)


def digamma_rest(x):
    w = x * (x + 3.0)
    steps = (2.0 * x + 3.0) * (2.0 * w + 2.0) / (w * (w + 2.0))
    inverse = 1.0 / (x + 4.0)
    z = inverse * inverse
    series = z * (1.0 / 12.0 - z * (1.0 / 120.0 - z * (1.0 / 252.0 - z * (1.0 / 240.0))))
    return steps + 0.5 * inverse + series


def digamma(x):
    return jnp.log(x + 4.0) - digamma_rest(x)


def gains_of(shape_values, rate_values, prior, strength):
    inverse_rate = 1.0 / rate_values
    gain = (shape_values + 4.0) * jnp.exp(-digamma_rest(shape_values)) * inverse_rate
    mean = shape_values * inverse_rate
    return gain.astype(jnp.bfloat16), strength / (prior + jnp.sum(mean, axis=1, keepdims=True)), mean


def head_kernel(touched_from, shape_from, rate_from, head_ref, touched_ref, shape_ref, rate_ref, arrived):
    per_owner, devices = touched_ref.shape
    rows, factors = shape_ref.shape
    parts = (arrived.shape[0] - 1) // 2
    step = rows // parts

    def fetch(part):
        piece = pl.ds(part * step, step)
        return [
            pltpu.make_async_copy(shape_from.at[piece], shape_ref.at[piece], arrived.at[2 * part]),
            pltpu.make_async_copy(rate_from.at[piece], rate_ref.at[piece], arrived.at[2 * part + 1]),
        ]

    table = pltpu.make_async_copy(touched_from, touched_ref, arrived.at[2 * parts])
    for part in range(parts):
        for copy in fetch(part):
            copy.start()
    table.start()
    total = jnp.zeros((1, factors), jnp.float32)
    for part in range(parts):
        for copy in fetch(part):
            copy.wait()
        piece = pl.ds(part * step, step)
        total += jnp.sum(shape_ref[piece, :] / rate_ref[piece, :], axis=0, keepdims=True)
    table.wait()
    blocks = touched_ref[...].astype(jnp.float32)
    row = jnp.concatenate(
        [blocks[place : place + 1] for place in range(per_owner)]
        + [jnp.zeros((1, LANES - per_owner * devices), jnp.float32), total],
        axis=1,
    )
    head_ref[...] = jnp.broadcast_to(row.reshape(1, 1, LANES + factors), head_ref.shape)


def head_of(touched, item_shape, item_rate):
    rows, factors = item_shape.shape
    devices, per_owner = touched.shape
    head_shape = (devices, 1, LANES + factors)
    return pl.pallas_call(
        head_kernel,
        grid=(1,),
        in_specs=[IN_PLACE, IN_PLACE, IN_PLACE],
        out_specs=pl.BlockSpec(head_shape, lambda r: (0, 0, 0)),
        out_shape=pltpu.HBM(head_shape, jnp.float32),
        scratch_shapes=[
            pltpu.VMEM((per_owner, devices), jnp.int32),
            pltpu.VMEM((rows, factors), jnp.float32),
            pltpu.VMEM((rows, factors), jnp.float32),
            pltpu.SemaphoreType.DMA((9,)),
        ],
        compiler_params=pltpu.CompilerParams(vmem_limit_bytes=VMEM_BYTES),
        cost_estimate=pl.CostEstimate(
            flops=4 * rows * factors, bytes_accessed=8 * rows * factors, transcendentals=rows * factors
        ),
    )(in_hbm(touched.T), in_hbm(item_shape), in_hbm(item_rate))


def item_gain_kernel(strength, shape_ref, rate_ref, gain_ref, level_ref):
    gain_ref[...], level_ref[...], _ = gains_of(
        shape_ref[...], rate_ref[...], popularity_prior / popularity_scale, strength
    )


def item_gains(item_shape, item_rate):
    rows, factors = item_shape.shape
    step = rows // 2
    row_spec = pl.BlockSpec((step, factors), lambda r: (r, 0))
    return pl.pallas_call(
        functools.partial(item_gain_kernel, popularity_prior + factors * item_prior),
        grid=(rows // step,),
        in_specs=[row_spec, row_spec],
        out_specs=[row_spec, pl.BlockSpec((step, 1), lambda r: (r, 0))],
        out_shape=[
            pltpu.HBM((rows, factors), jnp.bfloat16),
            pltpu.HBM((rows, 1), jnp.float32),
        ],
        compiler_params=pltpu.CompilerParams(vmem_limit_bytes=VMEM_BYTES),
        cost_estimate=pl.CostEstimate(
            flops=40 * rows * factors, bytes_accessed=10 * rows * factors, transcendentals=4 * rows * factors
        ),
    )(in_hbm(item_shape), in_hbm(item_rate))


def user_gain_kernel(strength, shape_ref, rate_ref, head_ref, gain_ref, level_ref, turned_ref, column_ref):
    gain, level_ref[...], _ = gains_of(shape_ref[...], rate_ref[...], activity_prior / activity_scale, strength)
    gain_ref[...] = gain
    turned_ref[...] = gain.T

    @pl.when(pl.program_id(0) == 0)
    def _():
        factors = gain.shape[1]
        means = head_ref[:, :, pl.ds(head_ref.shape[2] - factors, factors)]
        column_ref[...] = jnp.sum(means, axis=0).reshape(1, factors)


def user_gains(user_shape, user_rate, heads):
    rows, factors = user_shape.shape
    step = rows // 4
    row_spec = pl.BlockSpec((step, factors), lambda r: (r, 0))
    return pl.pallas_call(
        functools.partial(user_gain_kernel, activity_prior + factors * user_prior),
        grid=(rows // step,),
        in_specs=[row_spec, row_spec, pl.BlockSpec(heads.shape, lambda r: (0, 0, 0))],
        out_specs=[
            row_spec,
            pl.BlockSpec((step, 1), lambda r: (r, 0)),
            pl.BlockSpec((factors, step), lambda r: (0, r)),
            pl.BlockSpec((1, factors), lambda r: (0, 0)),
        ],
        out_shape=[
            pltpu.HBM((rows, factors), jnp.bfloat16),
            pltpu.HBM((rows, 1), jnp.float32),
            pltpu.HBM((factors, rows), jnp.bfloat16),
            pltpu.HBM((1, factors), jnp.float32),
        ],
        compiler_params=pltpu.CompilerParams(vmem_limit_bytes=VMEM_BYTES),
        cost_estimate=pl.CostEstimate(
            flops=40 * rows * factors, bytes_accessed=12 * rows * factors, transcendentals=4 * rows * factors
        ),
    )(in_hbm(user_shape), in_hbm(user_rate), heads)


def block_at(table_ref, device, place, seat):
    return table_ref[device, 0, place * table_ref.shape[0] + seat].astype(jnp.int32)


def pick_kernel(per_owner, seat_ref, head_from, gain_from, picked_out, table_ref, gain_ref, picked_ref, arrived, sent):
    blocks, edge, _ = gain_ref.shape
    devices = table_ref.shape[0]
    fetches = [pltpu.make_async_copy(head_from.at[:, :, pl.ds(0, LANES)], table_ref, arrived.at[blocks])] + [
        pltpu.make_async_copy(gain_from.at[block], gain_ref.at[block], arrived.at[block]) for block in range(blocks)
    ]
    for copy in fetches:
        copy.start()
    for copy in fetches:
        copy.wait()
    per_copy = devices // sent.shape[0]
    copies = []
    for part in range(sent.shape[0]):
        for device in range(part * per_copy, (part + 1) * per_copy):
            for place in range(per_owner):
                block = block_at(table_ref, device, place, seat_ref[0])
                picked_ref[device, pl.ds(place * edge, edge), :] = gain_ref[block]
        piece = pl.ds(part * per_copy, per_copy)
        copies.append(pltpu.make_async_copy(picked_ref.at[piece], picked_out.at[piece], sent.at[part]))
        copies[-1].start()
    for copy in copies:
        copy.wait()


def pick(seat, heads, item_gain, edge, per_owner):
    items, factors = item_gain.shape
    devices = heads.shape[0]
    return pl.pallas_call(
        functools.partial(pick_kernel, per_owner),
        in_specs=[IN_SMEM, IN_PLACE, IN_PLACE],
        out_specs=IN_PLACE,
        scratch_shapes=[
            pltpu.SMEM((devices, 1, LANES), jnp.float32),
            pltpu.VMEM((items // edge, edge, factors), jnp.bfloat16),
            pltpu.VMEM((devices, per_owner * edge, factors), jnp.bfloat16),
            pltpu.SemaphoreType.DMA((items // edge + 1,)),
            pltpu.SemaphoreType.DMA((min(8, devices),)),
        ],
        out_shape=pltpu.HBM((devices, per_owner * edge, factors), jnp.bfloat16),
        compiler_params=pltpu.CompilerParams(vmem_limit_bytes=VMEM_BYTES),
        cost_estimate=pl.CostEstimate(
            flops=0, bytes_accessed=2 * items * factors + 2 * devices * per_owner * edge * factors, transcendentals=0
        ),
    )(seat, heads, in_hbm(item_gain.reshape(items // edge, edge, factors)))


def dense_kernel(user_of, slot_of, live_ref, counts_ref, after_ref, out_ref, dense_ref, held_ref, arrived, sent):
    depth, group = held_ref.shape[:2]
    live = live_ref[0]
    groups = (live + group - 1) // group

    def fetch(index):
        place = lax.rem(index, depth)
        return pltpu.make_async_copy(
            counts_ref.at[pl.ds(index * group, group)], held_ref.at[place], arrived.at[place]
        )

    for index in range(depth):

        @pl.when(index < groups)
        def _():
            fetch(index).start()

    def clear(slot, carry):
        dense_ref[slot] = jnp.zeros(dense_ref.shape[1:], dense_ref.dtype)
        return carry

    lax.fori_loop(0, dense_ref.shape[0], clear, 0)

    def add_group(index, carry):
        fetch(index).wait()
        place = lax.rem(index, depth)
        for offset in range(group):
            tile = index * group + offset

            @pl.when(tile < live)
            def _():
                user, slot = user_of[tile], slot_of[tile]
                dense_ref[slot, user] += held_ref[place, offset].astype(jnp.float32).astype(jnp.bfloat16)

        @pl.when(index + depth < groups)
        def _():
            fetch(index + depth).start()

        return carry

    lax.fori_loop(0, groups, add_group, 0)
    slots = dense_ref.shape[0] // sent.shape[0]
    copies = [
        pltpu.make_async_copy(
            dense_ref.at[pl.ds(part * slots, slots)], out_ref.at[pl.ds(part * slots, slots)], sent.at[part]
        )
        for part in range(sent.shape[0])
    ]
    for copy in copies:
        copy.start()
    for copy in copies:
        copy.wait()


def dense_counts(counts, tile_user, tile_slot, live_tiles, slot_count, user_blocks, after):
    tiles, edge, _ = counts.shape
    group = 8
    depth = min(8, tiles // group)
    return pl.pallas_call(
        dense_kernel,
        in_specs=[IN_SMEM, IN_SMEM, IN_SMEM, IN_PLACE, IN_VMEM],
        out_specs=IN_PLACE,
        scratch_shapes=[
            pltpu.VMEM((slot_count, user_blocks, edge, edge), jnp.bfloat16),
            pltpu.VMEM((depth, group, edge, edge), jnp.int32),
            pltpu.SemaphoreType.DMA((depth,)),
            pltpu.SemaphoreType.DMA((16,)),
        ],
        out_shape=pltpu.HBM((slot_count, user_blocks, edge, edge), jnp.bfloat16),
        compiler_params=pltpu.CompilerParams(vmem_limit_bytes=VMEM_BYTES),
        cost_estimate=pl.CostEstimate(
            flops=tiles * edge * edge, bytes_accessed=4 * counts.size + 2 * slot_count * user_blocks * edge * edge,
            transcendentals=0,
        ),
    )(tile_user, tile_slot, live_tiles, in_hbm(counts), after)


def split_rows(value, rows):
    high = value.astype(jnp.bfloat16).astype(jnp.float32)
    middle = (value - high).astype(jnp.bfloat16).astype(jnp.float32)
    low = value - high - middle
    row = lax.broadcasted_iota(jnp.int32, (rows, value.shape[1]), 0)
    block = jnp.where(row == 0, high, jnp.where(row == 1, middle, jnp.where(row == 2, low, 0.0)))
    return block.astype(jnp.bfloat16)


def sweep_kernel(
    prior_share, place_ref, dense_from, items_ref, gain_from, turned_from, level_from, total_ref, item_ref, *rest
):
    user_outs, rest = rest[:-12], rest[-12:]
    dense_ref, gain_ref, turned_ref, level_ref, acc_ref, early_ref, late_ref, sums_ref, extra_ref, users_ref = rest[:10]
    arrived, sent = rest[10:]
    owners, touched_rows, factors = items_ref.shape
    slots, user_blocks, edge, _ = dense_ref.shape
    users = user_blocks * edge
    per_owner = slots // owners
    pair = 2
    chunk = users // 2
    last = owners // pair - 1

    def items_of(index):
        return items_ref[pl.ds(index * pair, pair)].reshape(pair * touched_rows, factors)

    def denominators(index):
        turned_items = items_of(index).T
        return [
            jnp.dot(gain_ref[pl.ds(first, chunk), :], turned_items, preferred_element_type=jnp.float32)
            for first in range(0, users, chunk)
        ]

    def put_ratios(index, parts, ratio_ref):
        for place, denominator in enumerate(parts):
            blocks = pl.ds(place * (chunk // edge), chunk // edge)
            counted = jnp.concatenate(
                [
                    dense_ref[index * pair * per_owner + slot, blocks].reshape(chunk, edge)
                    for slot in range(pair * per_owner)
                ],
                axis=1,
            ).astype(jnp.float32)
            ratio_ref[pl.ds(place * chunk, chunk), :] = (counted * pl.reciprocal(denominator, approx=True)).astype(
                jnp.bfloat16
            )

    def copy_of(index):
        return pltpu.make_async_copy(
            sums_ref.at[pl.ds(index * pair, pair)],
            item_ref.at[pl.ds(index * pair, pair), pl.ds(0, touched_rows)],
            sent.at[index],
        )

    def add_products(index, ratio_ref):
        items = items_of(index)
        for first in range(0, users, chunk):
            rows = pl.ds(first, chunk)
            acc_ref[rows, :] += jnp.dot(ratio_ref[rows, :], items, preferred_element_type=jnp.float32)
        sums = jnp.dot(turned_ref[...], ratio_ref[...], preferred_element_type=jnp.float32)
        sums_ref[pl.ds(index * pair, pair)] = sums.astype(jnp.bfloat16).T.reshape(pair, touched_rows, factors)
        copy_of(index).start()

    def fetch(index):
        slots_of = pl.ds(index * pair * per_owner, pair * per_owner)
        return pltpu.make_async_copy(dense_from.at[slots_of], dense_ref.at[slots_of], arrived.at[index])

    gain_rows = [pl.ds(first, chunk) for first in range(0, users, chunk)]
    first_copies = [
        pltpu.make_async_copy(gain_from.at[rows], gain_ref.at[rows], arrived.at[last + 1 + place])
        for place, rows in enumerate(gain_rows)
    ]
    later_copies = [
        pltpu.make_async_copy(source, target, arrived.at[last + 3 + place])
        for place, (source, target) in enumerate(((turned_from, turned_ref), (level_from, level_ref)))
    ]
    first_copies[0].start()
    fetch(0).start()
    first_copies[1].start()
    acc_ref[...] = jnp.zeros_like(acc_ref)
    for copy in first_copies:
        copy.wait()
    later_copies[0].start()
    for index in range(1, last + 1):
        fetch(index).start()
    later_copies[1].start()
    fetch(0).wait()
    put_ratios(0, denominators(0), early_ref)
    later_copies[0].wait()

    def turn(step, carry):
        first, second, third = 2 * step, 2 * step + 1, jnp.minimum(2 * step + 2, last)
        fetch(second).wait()

        @pl.when(third > second)
        def _():
            fetch(third).wait()

        late = denominators(second)
        add_products(first, early_ref)
        put_ratios(second, late, late_ref)
        early = denominators(third)
        add_products(second, late_ref)
        put_ratios(third, early, early_ref)
        return carry

    lax.fori_loop(0, (last + 1) // 2, turn, 0)

    own = users // len(user_outs)
    copies = []
    for ahead, user_out in enumerate(user_outs):
        target = (place_ref[0] + ahead) % len(user_outs)
        rows = pl.ds(pl.multiple_of(target * own, own), own)
        users_ref[ahead] = acc_ref[rows, :].astype(jnp.bfloat16)
        copies.append(pltpu.make_async_copy(users_ref.at[ahead], user_out, sent.at[last + 2 + ahead]))
        copies[-1].start()
    later_copies[1].wait()
    part = jnp.zeros((1, factors), jnp.float32)
    for first in range(0, users, own):
        rows = pl.ds(first, own)
        shape_share = prior_share + gain_ref[rows, :].astype(jnp.float32) * acc_ref[rows, :]
        inverse_rate = pl.reciprocal(level_ref[rows, :] + total_ref[...], approx=True)
        part += jnp.sum(shape_share * inverse_rate, axis=0, keepdims=True)
    extra_ref[...] = jnp.broadcast_to(split_rows(part, EXTRA)[None], extra_ref.shape)
    copies.append(
        pltpu.make_async_copy(extra_ref, item_ref.at[:, pl.ds(touched_rows, EXTRA)], sent.at[last + 1])
    )
    copies[-1].start()
    for index in range(last + 1):
        copy_of(index).wait()
    for copy in copies:
        copy.wait()


def sweep(place, dense, items, user_gain, turned_gain, user_level, item_total, parts):
    owners, touched_rows, factors = items.shape
    users = user_gain.shape[0]
    own = users // parts
    pair = 2
    out = pl.pallas_call(
        functools.partial(sweep_kernel, user_prior / parts),
        in_specs=[IN_SMEM, IN_PLACE, IN_VMEM, IN_PLACE, IN_PLACE, IN_PLACE, IN_VMEM],
        out_specs=[IN_PLACE] * (parts + 1),
        scratch_shapes=[
            pltpu.VMEM(dense.shape, jnp.bfloat16),
            pltpu.VMEM((users, factors), jnp.bfloat16),
            pltpu.VMEM((factors, users), jnp.bfloat16),
            pltpu.VMEM((users, 1), jnp.float32),
            pltpu.VMEM((users, factors), jnp.float32),
            pltpu.VMEM((users, pair * touched_rows), jnp.bfloat16),
            pltpu.VMEM((users, pair * touched_rows), jnp.bfloat16),
            pltpu.VMEM((owners, touched_rows, factors), jnp.bfloat16),
            pltpu.VMEM((owners, EXTRA, factors), jnp.bfloat16),
            pltpu.VMEM((parts, own, factors), jnp.bfloat16),
            pltpu.SemaphoreType.DMA((owners // pair + 4,)),
            pltpu.SemaphoreType.DMA((owners // pair + 1 + parts,)),
        ],
        out_shape=[pltpu.HBM((owners, touched_rows + EXTRA, factors), jnp.bfloat16)]
        + [pltpu.HBM((own, factors), jnp.bfloat16)] * parts,
        compiler_params=pltpu.CompilerParams(vmem_limit_bytes=SWEEP_BYTES),
        cost_estimate=pl.CostEstimate(
            flops=6 * owners * touched_rows * users * factors,
            bytes_accessed=2 * dense.size + 4 * items.size + 4 * users * factors,
            transcendentals=owners * touched_rows * users,
        ),
    )(place, in_hbm(dense), items, in_hbm(user_gain), in_hbm(turned_gain), in_hbm(user_level), item_total)
    return out[0], out[1:]


def own_kernel(place_ref, gain_ref, *rest):
    sums_refs, sum_ref = rest[:-1], rest[-1]
    sums = jnp.zeros(sum_ref.shape, jnp.float32)
    for sums_ref in sums_refs:
        sums += sums_ref[...].astype(jnp.float32)
    sum_ref[...] = (gain_ref[...].astype(jnp.float32) * sums).astype(jnp.bfloat16)


def own_users(place, sums, user_gain):
    own, factors = sums[0].shape
    first = lambda step, place_ref: (0, 0)
    return pl.pallas_call(
        own_kernel,
        grid_spec=pltpu.PrefetchScalarGridSpec(
            num_scalar_prefetch=1,
            grid=(1,),
            in_specs=[pl.BlockSpec((own, factors), lambda step, place_ref: (place_ref[0], 0))]
            + [pl.BlockSpec((own, factors), first)] * len(sums),
            out_specs=pl.BlockSpec((own, factors), first),
        ),
        out_shape=pltpu.HBM((own, factors), jnp.bfloat16),
        compiler_params=pltpu.CompilerParams(vmem_limit_bytes=VMEM_BYTES),
        cost_estimate=pl.CostEstimate(
            flops=2 * len(sums) * own * factors, bytes_accessed=2 * len(sums) * own * factors, transcendentals=0
        ),
    )(place, in_hbm(user_gain), *sums)


def fold_kernel(sums_ref, shape_after_ref, rate_after_ref, part_ref):
    extra = sums_ref[0].astype(jnp.float32)
    for sender in range(1, sums_ref.shape[0]):
        extra += sums_ref[sender].astype(jnp.float32)
    part_ref[...] = jnp.broadcast_to(jnp.sum(extra, axis=0).reshape(1, 1, -1), part_ref.shape)


def fold(sums, copies, *after):
    senders, extended, factors = sums.shape
    return pl.pallas_call(
        fold_kernel,
        grid=(1,),
        in_specs=[pl.BlockSpec((senders, EXTRA, factors), lambda step: (0, extended // EXTRA - 1, 0)), IN_PLACE, IN_PLACE],
        out_specs=pl.BlockSpec((copies, 1, factors), lambda step: (0, 0, 0)),
        out_shape=pltpu.HBM((copies, 1, factors), jnp.float32),
        compiler_params=pltpu.CompilerParams(vmem_limit_bytes=VMEM_BYTES),
        cost_estimate=pl.CostEstimate(flops=0, bytes_accessed=2 * senders * EXTRA * factors, transcendentals=0),
    )(sums, *(in_hbm(array) for array in after))


def shape_kernel(
    per_owner, seat_ref, head_from, sums_ref, gain_from, shape_out, digamma_ref, table_ref, acc_ref, gain_ref, shape_ref,
    arrived, sent,
):
    blocks, edge, _ = acc_ref.shape
    table = pltpu.make_async_copy(head_from.at[:, :, pl.ds(0, LANES)], table_ref, arrived.at[0])
    gains = pltpu.make_async_copy(gain_from, gain_ref, arrived.at[1])
    table.start()
    gains.start()
    acc_ref[...] = jnp.zeros_like(acc_ref)
    table.wait()
    for sender in range(sums_ref.shape[0]):
        for place in range(per_owner):
            block = block_at(table_ref, sender, place, seat_ref[0])
            acc_ref[block] += sums_ref[sender, pl.ds(place * edge, edge), :].astype(jnp.float32)
    gains.wait()
    copies = []
    for block in range(blocks):
        rows = pl.ds(block * edge, edge)
        shape_new = item_prior + gain_ref[rows, :].astype(jnp.float32) * acc_ref[block]
        shape_ref[rows, :] = shape_new
        copies.append(pltpu.make_async_copy(shape_ref.at[rows], shape_out.at[rows], sent.at[block]))
        copies[-1].start()
        digamma_ref[rows, :] = digamma(shape_new)
    for copy in copies:
        copy.wait()


def item_shapes(seat, heads, sums, item_gain, edge, per_owner):
    items, factors = item_gain.shape
    return pl.pallas_call(
        functools.partial(shape_kernel, per_owner),
        in_specs=[IN_SMEM, IN_PLACE, IN_VMEM, IN_PLACE],
        out_specs=[IN_PLACE, IN_VMEM],
        scratch_shapes=[
            pltpu.SMEM((heads.shape[0], 1, LANES), jnp.float32),
            pltpu.VMEM((items // edge, edge, factors), jnp.float32),
            pltpu.VMEM((items, factors), jnp.bfloat16),
            pltpu.VMEM((items, factors), jnp.float32),
            pltpu.SemaphoreType.DMA((2,)),
            pltpu.SemaphoreType.DMA((items // edge,)),
        ],
        out_shape=[pltpu.HBM((items, factors), jnp.float32), jax.ShapeDtypeStruct((items, factors), jnp.float32)],
        compiler_params=pltpu.CompilerParams(vmem_limit_bytes=VMEM_BYTES),
        cost_estimate=pl.CostEstimate(
            flops=40 * items * factors, bytes_accessed=2 * sums.size + 10 * items * factors,
            transcendentals=3 * items * factors,
        ),
    )(seat, heads, sums, in_hbm(item_gain))


def elog_kernel(digamma_ref, level_ref, parts_ref, elog_out, elog_ref, sent):
    user_total = jnp.sum(parts_ref[...], axis=0)
    step = elog_ref.shape[0] // sent.shape[0]
    copies = []
    for piece in range(sent.shape[0]):
        rows = pl.ds(piece * step, step)
        elog_ref[rows, :] = digamma_ref[rows, :] - jnp.log(level_ref[rows, :] + user_total)
        copies.append(pltpu.make_async_copy(elog_ref.at[rows], elog_out.at[rows], sent.at[piece]))
        copies[-1].start()
    for copy in copies:
        copy.wait()


def item_elogs(digammas, item_level, user_parts):
    items, factors = digammas.shape
    return pl.pallas_call(
        elog_kernel,
        in_specs=[IN_VMEM, IN_VMEM, IN_VMEM],
        out_specs=IN_PLACE,
        scratch_shapes=[pltpu.VMEM((items, factors), jnp.float32), pltpu.SemaphoreType.DMA((4,))],
        out_shape=pltpu.HBM((items, factors), jnp.float32),
        compiler_params=pltpu.CompilerParams(vmem_limit_bytes=VMEM_BYTES),
        cost_estimate=pl.CostEstimate(
            flops=2 * items * factors, bytes_accessed=8 * items * factors, transcendentals=items * factors
        ),
    )(digammas, item_level, user_parts)


def shards(
    counts, tile_user, tile_slot, live_tiles, touched, user_shape, user_rate, item_shape, item_rate
):
    edge = counts.shape[1]
    users, factors = user_shape.shape
    user_blocks = users // edge
    owners, per_owner = touched.shape
    columns = lax.axis_size("item")
    place = lax.axis_index("item").astype(jnp.int32).reshape(1)
    seat = lax.axis_index("user").astype(jnp.int32).reshape(1)
    heads = lax.all_to_all(head_of(touched, item_shape, item_rate), "user", 0, 0)
    item_gain, item_level = item_gains(item_shape, item_rate)
    item_rows = lax.all_to_all(pick(seat, heads, item_gain, edge, per_owner), "user", 0, 0)
    user_gain, user_level, turned_gain, column_total = user_gains(user_shape, user_rate, heads)
    item_total = jnp.sum(lax.all_gather(column_total, "item", axis=0, tiled=True), axis=0, keepdims=True)
    dense = dense_counts(
        counts, tile_user, tile_slot, live_tiles, owners * per_owner, user_blocks, item_total
    )
    item_sums, user_sums = sweep(
        place, dense, item_rows, user_gain, turned_gain, user_level, item_total, columns
    )
    item_sums = lax.all_to_all(item_sums, "user", 0, 0)
    user_sums = [user_sums[0]] + [
        lax.ppermute(user_sums[k], "item", [(j, (j + k) % columns) for j in range(columns)])
        for k in range(1, columns)
    ]
    user_sum = lax.all_gather(own_users(place, user_sums, user_gain), "item", axis=0, tiled=True)
    user_shape_new = user_prior + user_sum.astype(jnp.float32)
    user_rate_new = user_level + item_total
    user_parts = lax.all_to_all(fold(item_sums, columns, user_shape_new, user_rate_new), "item", 0, 0)
    item_shape_new, digammas = item_shapes(seat, heads, item_sums, item_gain, edge, per_owner)
    item_elog = item_elogs(digammas, item_level, user_parts)
    return (user_shape_new, user_rate_new, item_shape_new, item_elog)


def solution(mesh):
    return jax.shard_map(
        shards,
        mesh=mesh,
        in_specs=(
            P(("user", "item"), None, None),
            P(("user", "item")),
            P(("user", "item")),
            P(("user", "item")),
            P(("user", "item"), None),
            P("user", None),
            P("user", None),
            P(("user", "item"), None),
            P(("user", "item"), None),
        ),
        out_specs=(
            P("user", None),
            P("user", None),
            P(("user", "item"), None),
            P(("user", "item"), None),
        ),
        check_vma=False,
    )
```

```python
import functools

import jax
import jax.numpy as jnp
from jax import lax
from jax.experimental import pallas as pl
from jax.experimental.pallas import tpu as pltpu
from jax.sharding import PartitionSpec as P

user_prior = 0.3
activity_prior = 0.3
activity_scale = 1.0
item_prior = 0.3
popularity_prior = 0.3
popularity_scale = 1.0

VMEM_BYTES = 24 << 20
SWEEP_BYTES = 36 << 20
LANES = 128
IN_VMEM = pl.BlockSpec(memory_space=pltpu.VMEM)
IN_SMEM = pl.BlockSpec(memory_space=pltpu.SMEM)
IN_PLACE = pl.BlockSpec(memory_space=pl.ANY)


def in_hbm(array):
    return pltpu.with_memory_space_constraint(array, pltpu.HBM)


def digamma_rest(x):
    w = x * (x + 3.0)
    steps = (2.0 * x + 3.0) * (2.0 * w + 2.0) / (w * (w + 2.0))
    inverse = 1.0 / (x + 4.0)
    z = inverse * inverse
    series = z * (1.0 / 12.0 - z * (1.0 / 120.0 - z * (1.0 / 252.0 - z * (1.0 / 240.0))))
    return steps + 0.5 * inverse + series


def digamma(x):
    return jnp.log(x + 4.0) - digamma_rest(x)


def gains_of(shape_values, rate_values, prior, strength):
    inverse_rate = 1.0 / rate_values
    gain = (shape_values + 4.0) * jnp.exp(-digamma_rest(shape_values)) * inverse_rate
    mean = shape_values * inverse_rate
    return gain.astype(jnp.bfloat16), strength / (prior + jnp.sum(mean, axis=1, keepdims=True)), mean


def head_kernel(touched_from, shape_from, rate_from, head_ref, touched_ref, shape_ref, rate_ref, arrived):
    per_owner, devices = touched_ref.shape
    rows, factors = shape_ref.shape
    parts = (arrived.shape[0] - 1) // 2
    step = rows // parts

    def fetch(part):
        piece = pl.ds(part * step, step)
        return [
            pltpu.make_async_copy(shape_from.at[piece], shape_ref.at[piece], arrived.at[2 * part]),
            pltpu.make_async_copy(rate_from.at[piece], rate_ref.at[piece], arrived.at[2 * part + 1]),
        ]

    table = pltpu.make_async_copy(touched_from, touched_ref, arrived.at[2 * parts])
    for part in range(parts):
        for copy in fetch(part):
            copy.start()
    table.start()
    total = jnp.zeros((1, factors), jnp.float32)
    for part in range(parts):
        for copy in fetch(part):
            copy.wait()
        piece = pl.ds(part * step, step)
        total += jnp.sum(shape_ref[piece, :] / rate_ref[piece, :], axis=0, keepdims=True)
    table.wait()
    blocks = touched_ref[...].astype(jnp.float32)
    row = jnp.concatenate(
        [blocks[place : place + 1] for place in range(per_owner)]
        + [jnp.zeros((1, LANES - per_owner * devices), jnp.float32), total],
        axis=1,
    )
    head_ref[...] = jnp.broadcast_to(row.reshape(1, 1, LANES + factors), head_ref.shape)


def head_of(touched, item_shape, item_rate):
    rows, factors = item_shape.shape
    devices, per_owner = touched.shape
    head_shape = (devices, 1, LANES + factors)
    return pl.pallas_call(
        head_kernel,
        grid=(1,),
        in_specs=[IN_PLACE, IN_PLACE, IN_PLACE],
        out_specs=pl.BlockSpec(head_shape, lambda r: (0, 0, 0)),
        out_shape=pltpu.HBM(head_shape, jnp.float32),
        scratch_shapes=[
            pltpu.VMEM((per_owner, devices), jnp.int32),
            pltpu.VMEM((rows, factors), jnp.float32),
            pltpu.VMEM((rows, factors), jnp.float32),
            pltpu.SemaphoreType.DMA((9,)),
        ],
        compiler_params=pltpu.CompilerParams(vmem_limit_bytes=VMEM_BYTES),
        cost_estimate=pl.CostEstimate(
            flops=4 * rows * factors, bytes_accessed=8 * rows * factors, transcendentals=rows * factors
        ),
    )(in_hbm(touched.T), in_hbm(item_shape), in_hbm(item_rate))


def item_gain_kernel(strength, shape_ref, rate_ref, gain_ref, level_ref):
    gain_ref[...], level_ref[...], _ = gains_of(
        shape_ref[...], rate_ref[...], popularity_prior / popularity_scale, strength
    )


def item_gains(item_shape, item_rate):
    rows, factors = item_shape.shape
    step = rows // 2
    row_spec = pl.BlockSpec((step, factors), lambda r: (r, 0))
    return pl.pallas_call(
        functools.partial(item_gain_kernel, popularity_prior + factors * item_prior),
        grid=(rows // step,),
        in_specs=[row_spec, row_spec],
        out_specs=[row_spec, pl.BlockSpec((step, 1), lambda r: (r, 0))],
        out_shape=[
            pltpu.HBM((rows, factors), jnp.bfloat16),
            pltpu.HBM((rows, 1), jnp.float32),
        ],
        compiler_params=pltpu.CompilerParams(vmem_limit_bytes=VMEM_BYTES),
        cost_estimate=pl.CostEstimate(
            flops=40 * rows * factors, bytes_accessed=10 * rows * factors, transcendentals=4 * rows * factors
        ),
    )(in_hbm(item_shape), in_hbm(item_rate))


def user_gain_kernel(strength, shape_ref, rate_ref, head_ref, gain_ref, level_ref, turned_ref, column_ref):
    gain, level_ref[...], _ = gains_of(shape_ref[...], rate_ref[...], activity_prior / activity_scale, strength)
    gain_ref[...] = gain
    turned_ref[...] = gain.T

    @pl.when(pl.program_id(0) == 0)
    def _():
        factors = gain.shape[1]
        means = head_ref[:, :, pl.ds(head_ref.shape[2] - factors, factors)]
        column_ref[...] = jnp.sum(means, axis=0).reshape(1, factors)


def user_gains(user_shape, user_rate, heads):
    rows, factors = user_shape.shape
    step = rows // 4
    row_spec = pl.BlockSpec((step, factors), lambda r: (r, 0))
    return pl.pallas_call(
        functools.partial(user_gain_kernel, activity_prior + factors * user_prior),
        grid=(rows // step,),
        in_specs=[row_spec, row_spec, pl.BlockSpec(heads.shape, lambda r: (0, 0, 0))],
        out_specs=[
            row_spec,
            pl.BlockSpec((step, 1), lambda r: (r, 0)),
            pl.BlockSpec((factors, step), lambda r: (0, r)),
            pl.BlockSpec((1, factors), lambda r: (0, 0)),
        ],
        out_shape=[
            pltpu.HBM((rows, factors), jnp.bfloat16),
            pltpu.HBM((rows, 1), jnp.float32),
            pltpu.HBM((factors, rows), jnp.bfloat16),
            pltpu.HBM((1, factors), jnp.float32),
        ],
        compiler_params=pltpu.CompilerParams(vmem_limit_bytes=VMEM_BYTES),
        cost_estimate=pl.CostEstimate(
            flops=40 * rows * factors, bytes_accessed=12 * rows * factors, transcendentals=4 * rows * factors
        ),
    )(in_hbm(user_shape), in_hbm(user_rate), heads)


def block_at(table_ref, device, place, seat):
    return table_ref[device, 0, place * table_ref.shape[0] + seat].astype(jnp.int32)


def pick_kernel(per_owner, seat_ref, head_from, gain_from, picked_out, table_ref, gain_ref, picked_ref, arrived, sent):
    blocks, edge, _ = gain_ref.shape
    devices = table_ref.shape[0]
    fetches = [pltpu.make_async_copy(head_from.at[:, :, pl.ds(0, LANES)], table_ref, arrived.at[blocks])] + [
        pltpu.make_async_copy(gain_from.at[block], gain_ref.at[block], arrived.at[block]) for block in range(blocks)
    ]
    for copy in fetches:
        copy.start()
    for copy in fetches:
        copy.wait()
    per_copy = devices // sent.shape[0]
    copies = []
    for part in range(sent.shape[0]):
        for device in range(part * per_copy, (part + 1) * per_copy):
            for place in range(per_owner):
                block = block_at(table_ref, device, place, seat_ref[0])
                picked_ref[device, pl.ds(place * edge, edge), :] = gain_ref[block]
        piece = pl.ds(part * per_copy, per_copy)
        copies.append(pltpu.make_async_copy(picked_ref.at[piece], picked_out.at[piece], sent.at[part]))
        copies[-1].start()
    for copy in copies:
        copy.wait()


def pick(seat, heads, item_gain, edge, per_owner):
    items, factors = item_gain.shape
    devices = heads.shape[0]
    return pl.pallas_call(
        functools.partial(pick_kernel, per_owner),
        in_specs=[IN_SMEM, IN_PLACE, IN_PLACE],
        out_specs=IN_PLACE,
        scratch_shapes=[
            pltpu.SMEM((devices, 1, LANES), jnp.float32),
            pltpu.VMEM((items // edge, edge, factors), jnp.bfloat16),
            pltpu.VMEM((devices, per_owner * edge, factors), jnp.bfloat16),
            pltpu.SemaphoreType.DMA((items // edge + 1,)),
            pltpu.SemaphoreType.DMA((min(8, devices),)),
        ],
        out_shape=pltpu.HBM((devices, per_owner * edge, factors), jnp.bfloat16),
        compiler_params=pltpu.CompilerParams(vmem_limit_bytes=VMEM_BYTES),
        cost_estimate=pl.CostEstimate(
            flops=0, bytes_accessed=2 * items * factors + 2 * devices * per_owner * edge * factors, transcendentals=0
        ),
    )(seat, heads, in_hbm(item_gain.reshape(items // edge, edge, factors)))


def dense_kernel(user_of, slot_of, live_ref, counts_ref, after_ref, out_ref, dense_ref, held_ref, arrived, sent):
    depth, group = held_ref.shape[:2]
    live = live_ref[0]
    groups = (live + group - 1) // group

    def fetch(index):
        place = lax.rem(index, depth)
        return pltpu.make_async_copy(
            counts_ref.at[pl.ds(index * group, group)], held_ref.at[place], arrived.at[place]
        )

    for index in range(depth):

        @pl.when(index < groups)
        def _():
            fetch(index).start()

    def clear(slot, carry):
        dense_ref[slot] = jnp.zeros(dense_ref.shape[1:], dense_ref.dtype)
        return carry

    lax.fori_loop(0, dense_ref.shape[0], clear, 0)

    def add_group(index, carry):
        fetch(index).wait()
        place = lax.rem(index, depth)
        for offset in range(group):
            tile = index * group + offset

            @pl.when(tile < live)
            def _():
                user, slot = user_of[tile], slot_of[tile]
                dense_ref[slot, user] += held_ref[place, offset].astype(jnp.float32).astype(jnp.bfloat16)

        @pl.when(index + depth < groups)
        def _():
            fetch(index + depth).start()

        return carry

    lax.fori_loop(0, groups, add_group, 0)
    slots = dense_ref.shape[0] // sent.shape[0]
    copies = [
        pltpu.make_async_copy(
            dense_ref.at[pl.ds(part * slots, slots)], out_ref.at[pl.ds(part * slots, slots)], sent.at[part]
        )
        for part in range(sent.shape[0])
    ]
    for copy in copies:
        copy.start()
    for copy in copies:
        copy.wait()


def dense_counts(counts, tile_user, tile_slot, live_tiles, slot_count, user_blocks, after):
    tiles, edge, _ = counts.shape
    group = 8
    depth = min(8, tiles // group)
    return pl.pallas_call(
        dense_kernel,
        in_specs=[IN_SMEM, IN_SMEM, IN_SMEM, IN_PLACE, IN_VMEM],
        out_specs=IN_PLACE,
        scratch_shapes=[
            pltpu.VMEM((slot_count, user_blocks, edge, edge), jnp.bfloat16),
            pltpu.VMEM((depth, group, edge, edge), jnp.int32),
            pltpu.SemaphoreType.DMA((depth,)),
            pltpu.SemaphoreType.DMA((16,)),
        ],
        out_shape=pltpu.HBM((slot_count, user_blocks, edge, edge), jnp.bfloat16),
        compiler_params=pltpu.CompilerParams(vmem_limit_bytes=VMEM_BYTES),
        cost_estimate=pl.CostEstimate(
            flops=tiles * edge * edge, bytes_accessed=4 * counts.size + 2 * slot_count * user_blocks * edge * edge,
            transcendentals=0,
        ),
    )(tile_user, tile_slot, live_tiles, in_hbm(counts), after)


def sweep_kernel(
    prior_share, place_ref, dense_from, items_ref, gain_from, turned_from, level_from, total_ref,
    item_ref, kept_out, given_out, part_out,
    dense_ref, gain_ref, turned_ref, level_ref, acc_ref, early_ref, late_ref, sums_ref, given_ref, part_ref,
    arrived, sent,
):
    owners, touched_rows, factors = items_ref.shape
    slots, user_blocks, edge, _ = dense_ref.shape
    users = user_blocks * edge
    per_owner = slots // owners
    pair = 2
    chunk = users // 2
    last = owners // pair - 1

    def items_of(index):
        return items_ref[pl.ds(index * pair, pair)].reshape(pair * touched_rows, factors)

    def denominators(index):
        turned_items = items_of(index).T
        return [
            jnp.dot(gain_ref[pl.ds(first, chunk), :], turned_items, preferred_element_type=jnp.float32)
            for first in range(0, users, chunk)
        ]

    def put_ratios(index, parts, ratio_ref):
        for place, denominator in enumerate(parts):
            blocks = pl.ds(place * (chunk // edge), chunk // edge)
            counted = jnp.concatenate(
                [
                    dense_ref[index * pair * per_owner + slot, blocks].reshape(chunk, edge)
                    for slot in range(pair * per_owner)
                ],
                axis=1,
            ).astype(jnp.float32)
            ratio_ref[pl.ds(place * chunk, chunk), :] = (counted * pl.reciprocal(denominator, approx=True)).astype(
                jnp.bfloat16
            )

    def copy_of(index):
        return pltpu.make_async_copy(
            sums_ref.at[pl.ds(index * pair, pair)],
            item_ref.at[pl.ds(index * pair, pair), pl.ds(0, touched_rows)],
            sent.at[index],
        )

    def add_products(index, ratio_ref):
        items = items_of(index)
        for first in range(0, users, chunk):
            rows = pl.ds(first, chunk)
            acc_ref[rows, :] += jnp.dot(ratio_ref[rows, :], items, preferred_element_type=jnp.float32)
        sums = jnp.dot(turned_ref[...], ratio_ref[...], preferred_element_type=jnp.float32)
        sums_ref[pl.ds(index * pair, pair)] = sums.astype(jnp.bfloat16).T.reshape(pair, touched_rows, factors)
        copy_of(index).start()

    def fetch(index):
        slots_of = pl.ds(index * pair * per_owner, pair * per_owner)
        return pltpu.make_async_copy(dense_from.at[slots_of], dense_ref.at[slots_of], arrived.at[index])

    gain_rows = [pl.ds(first, chunk) for first in range(0, users, chunk)]
    first_copies = [
        pltpu.make_async_copy(gain_from.at[rows], gain_ref.at[rows], arrived.at[last + 1 + place])
        for place, rows in enumerate(gain_rows)
    ]
    later_copies = [
        pltpu.make_async_copy(source, target, arrived.at[last + 3 + place])
        for place, (source, target) in enumerate(((turned_from, turned_ref), (level_from, level_ref)))
    ]
    first_copies[0].start()
    fetch(0).start()
    first_copies[1].start()
    acc_ref[...] = jnp.zeros_like(acc_ref)
    for copy in first_copies:
        copy.wait()
    later_copies[0].start()
    for index in range(1, last + 1):
        fetch(index).start()
    later_copies[1].start()
    fetch(0).wait()
    put_ratios(0, denominators(0), early_ref)
    later_copies[0].wait()

    def turn(step, carry):
        first, second, third = 2 * step, 2 * step + 1, jnp.minimum(2 * step + 2, last)
        fetch(second).wait()

        @pl.when(third > second)
        def _():
            fetch(third).wait()

        late = denominators(second)
        add_products(first, early_ref)
        put_ratios(second, late, late_ref)
        early = denominators(third)
        add_products(second, late_ref)
        put_ratios(third, early, early_ref)
        return carry

    lax.fori_loop(0, (last + 1) // 2, turn, 0)

    half = users // 2
    step = half // 2
    core = lax.rem(place_ref[0], 2)
    copies = []
    for index in range(2):
        kept = pl.ds(pl.multiple_of(core * half + index * step, step), step)
        given = pl.ds(pl.multiple_of((1 - core) * half + index * step, step), step)
        rows = pl.ds(index * step, step)
        given_ref[rows, :] = acc_ref[given, :].astype(jnp.bfloat16)
        copies.append(pltpu.make_async_copy(acc_ref.at[kept], kept_out.at[rows], sent.at[last + 1 + 2 * index]))
        copies.append(pltpu.make_async_copy(given_ref.at[rows], given_out.at[rows], sent.at[last + 2 + 2 * index]))
    for copy in copies:
        copy.start()
    later_copies[1].wait()
    part = jnp.zeros((1, factors), jnp.float32)
    for first in range(0, users, step):
        rows = pl.ds(first, step)
        shape_share = prior_share + gain_ref[rows, :].astype(jnp.float32) * acc_ref[rows, :]
        inverse_rate = pl.reciprocal(level_ref[rows, :] + total_ref[...], approx=True)
        part += jnp.sum(shape_share * inverse_rate, axis=0, keepdims=True)
    part_ref[...] = part
    copies.append(pltpu.make_async_copy(part_ref, part_out, sent.at[last + 5]))
    copies[-1].start()
    for index in range(last + 1):
        copy_of(index).wait()
    for copy in copies:
        copy.wait()


def sweep(place, dense, items, user_gain, turned_gain, user_level, item_total, columns):
    owners, touched_rows, factors = items.shape
    users = user_gain.shape[0]
    pair = 2
    return pl.pallas_call(
        functools.partial(sweep_kernel, user_prior / columns),
        in_specs=[IN_SMEM, IN_PLACE, IN_VMEM, IN_PLACE, IN_PLACE, IN_PLACE, IN_VMEM],
        out_specs=[IN_PLACE] * 4,
        scratch_shapes=[
            pltpu.VMEM(dense.shape, jnp.bfloat16),
            pltpu.VMEM((users, factors), jnp.bfloat16),
            pltpu.VMEM((factors, users), jnp.bfloat16),
            pltpu.VMEM((users, 1), jnp.float32),
            pltpu.VMEM((users, factors), jnp.float32),
            pltpu.VMEM((users, pair * touched_rows), jnp.bfloat16),
            pltpu.VMEM((users, pair * touched_rows), jnp.bfloat16),
            pltpu.VMEM((owners, touched_rows, factors), jnp.bfloat16),
            pltpu.VMEM((users // 2, factors), jnp.bfloat16),
            pltpu.VMEM((1, factors), jnp.float32),
            pltpu.SemaphoreType.DMA((owners // pair + 4,)),
            pltpu.SemaphoreType.DMA((owners // pair + 5,)),
        ],
        out_shape=[
            pltpu.HBM((owners, touched_rows, factors), jnp.bfloat16),
            pltpu.HBM((users // 2, factors), jnp.float32),
            pltpu.HBM((users // 2, factors), jnp.bfloat16),
            pltpu.HBM((1, factors), jnp.float32),
        ],
        compiler_params=pltpu.CompilerParams(vmem_limit_bytes=SWEEP_BYTES),
        cost_estimate=pl.CostEstimate(
            flops=6 * owners * touched_rows * users * factors,
            bytes_accessed=2 * dense.size + 4 * items.size + 4 * users * factors,
            transcendentals=owners * touched_rows * users,
        ),
    )(place, in_hbm(dense), items, in_hbm(user_gain), in_hbm(turned_gain), in_hbm(user_level), item_total)


def chip_kernel(kept_ref, got_ref, sum_ref):
    sum_ref[...] = (kept_ref[...] + got_ref[...].astype(jnp.float32)).astype(jnp.bfloat16)


def chip_sums(kept, got):
    rows, factors = kept.shape
    spec = pl.BlockSpec((rows // 2, factors), lambda r: (r, 0))
    return pl.pallas_call(
        chip_kernel,
        grid=(2,),
        in_specs=[spec, spec],
        out_specs=spec,
        out_shape=pltpu.HBM((rows, factors), jnp.bfloat16),
        compiler_params=pltpu.CompilerParams(vmem_limit_bytes=VMEM_BYTES),
        cost_estimate=pl.CostEstimate(flops=rows * factors, bytes_accessed=8 * rows * factors, transcendentals=0),
    )(kept, got)


def slab_kernel(place_ref, gain_ref, *rest):
    sums_refs, shape_ref = rest[:-1], rest[-1]
    parts = [ref[...].astype(jnp.float32) for ref in sums_refs]
    while len(parts) > 1:
        apart = len(parts) // 2
        parts = [parts[k] + parts[k + apart] for k in range(apart)]
    shape_ref[...] = user_prior + gain_ref[...].astype(jnp.float32) * parts[0]


def slab_shapes(place, sums, user_gain):
    rows, factors = sums[0].shape
    spec = pl.BlockSpec((rows // 2, factors), lambda r, place_ref: (r, 0))
    return pl.pallas_call(
        slab_kernel,
        grid_spec=pltpu.PrefetchScalarGridSpec(
            num_scalar_prefetch=1,
            grid=(2,),
            in_specs=[pl.BlockSpec((rows // 2, factors), lambda r, place_ref: (lax.rem(place_ref[0], 2) * 2 + r, 0))]
            + [spec] * len(sums),
            out_specs=spec,
        ),
        out_shape=pltpu.HBM((rows, factors), jnp.float32),
        compiler_params=pltpu.CompilerParams(vmem_limit_bytes=VMEM_BYTES),
        cost_estimate=pl.CostEstimate(
            flops=len(sums) * rows * factors, bytes_accessed=2 * (len(sums) + 3) * rows * factors, transcendentals=0
        ),
    )(place, in_hbm(user_gain), *sums)


def item_kernel(
    per_owner, seat_ref, head_from, sums_ref, gain_from, level_from, total_ref, shape_out, elog_out,
    table_ref, acc_ref, gain_ref, level_ref, shape_ref, elog_ref, arrived, sent,
):
    blocks, edge, _ = acc_ref.shape
    fetches = [
        pltpu.make_async_copy(source, target, arrived.at[place])
        for place, (source, target) in enumerate(
            ((head_from.at[:, :, pl.ds(0, LANES)], table_ref), (gain_from, gain_ref), (level_from, level_ref))
        )
    ]
    for copy in fetches:
        copy.start()
    acc_ref[...] = jnp.zeros_like(acc_ref)
    fetches[0].wait()
    for sender in range(sums_ref.shape[0]):
        for place in range(per_owner):
            block = block_at(table_ref, sender, place, seat_ref[0])
            acc_ref[block] += sums_ref[sender, pl.ds(place * edge, edge), :].astype(jnp.float32)
    for copy in fetches[1:]:
        copy.wait()
    copies = []
    for block in range(blocks):
        rows = pl.ds(block * edge, edge)
        shape_new = item_prior + gain_ref[rows, :].astype(jnp.float32) * acc_ref[block]
        shape_ref[rows, :] = shape_new
        elog_ref[rows, :] = digamma(shape_new) - jnp.log(level_ref[rows, :] + total_ref[...])
        copies.append(pltpu.make_async_copy(shape_ref.at[rows], shape_out.at[rows], sent.at[2 * block]))
        copies.append(pltpu.make_async_copy(elog_ref.at[rows], elog_out.at[rows], sent.at[2 * block + 1]))
        for copy in copies[-2:]:
            copy.start()
    for copy in copies:
        copy.wait()


def item_update(seat, heads, sums, item_gain, item_level, user_total, edge, per_owner):
    items, factors = item_gain.shape
    return pl.pallas_call(
        functools.partial(item_kernel, per_owner),
        in_specs=[IN_SMEM, IN_PLACE, IN_VMEM, IN_PLACE, IN_PLACE, IN_VMEM],
        out_specs=[IN_PLACE, IN_PLACE],
        scratch_shapes=[
            pltpu.SMEM((heads.shape[0], 1, LANES), jnp.float32),
            pltpu.VMEM((items // edge, edge, factors), jnp.float32),
            pltpu.VMEM((items, factors), jnp.bfloat16),
            pltpu.VMEM((items, 1), jnp.float32),
            pltpu.VMEM((items, factors), jnp.float32),
            pltpu.VMEM((items, factors), jnp.float32),
            pltpu.SemaphoreType.DMA((3,)),
            pltpu.SemaphoreType.DMA((2 * (items // edge),)),
        ],
        out_shape=[pltpu.HBM((items, factors), jnp.float32)] * 2,
        compiler_params=pltpu.CompilerParams(vmem_limit_bytes=VMEM_BYTES),
        cost_estimate=pl.CostEstimate(
            flops=40 * items * factors, bytes_accessed=2 * sums.size + 10 * items * factors,
            transcendentals=4 * items * factors,
        ),
    )(seat, heads, sums, in_hbm(item_gain), in_hbm(item_level), user_total)


def ahead(array, axis, count):
    size = lax.axis_size(axis)
    return lax.ppermute(array, axis, [(j, (j + count) % size) for j in range(size)])


def across(array, axis, bit):
    return lax.ppermute(array, axis, [(j, j ^ bit) for j in range(lax.axis_size(axis))])


def shards(
    counts, tile_user, tile_slot, live_tiles, touched, user_shape, user_rate, item_shape, item_rate
):
    edge = counts.shape[1]
    users, factors = user_shape.shape
    user_blocks = users // edge
    owners, per_owner = touched.shape
    columns = lax.axis_size("item")
    place = lax.axis_index("item").astype(jnp.int32).reshape(1)
    seat = lax.axis_index("user").astype(jnp.int32).reshape(1)
    heads = lax.all_to_all(head_of(touched, item_shape, item_rate), "user", 0, 0)
    item_gain, item_level = item_gains(item_shape, item_rate)
    item_rows = lax.all_to_all(pick(seat, heads, item_gain, edge, per_owner), "user", 0, 0)
    user_gain, user_level, turned_gain, column_total = user_gains(user_shape, user_rate, heads)
    item_total = jnp.sum(lax.all_gather(column_total, "item", axis=0, tiled=True), axis=0, keepdims=True)
    dense = dense_counts(
        counts, tile_user, tile_slot, live_tiles, owners * per_owner, user_blocks, item_total
    )
    item_sums, kept, given, user_total = sweep(
        place, dense, item_rows, user_gain, turned_gain, user_level, item_total, columns
    )
    item_sums = lax.all_to_all(item_sums, "user", 0, 0)
    user_total = jnp.sum(lax.all_gather(user_total, "item", axis=0, tiled=True), axis=0, keepdims=True)
    bit = 1
    while bit < owners:
        user_total = user_total + across(user_total, "user", bit)
        bit *= 2
    chip = chip_sums(kept, across(given, "item", 1))
    own_shapes = slab_shapes(place, [chip] + [ahead(chip, "item", count) for count in range(2, columns, 2)], user_gain)
    other_shapes = across(own_shapes, "item", 1)
    user_shape_new = jnp.where(
        place[0] % 2 == 0,
        jnp.concatenate([own_shapes, other_shapes], axis=0),
        jnp.concatenate([other_shapes, own_shapes], axis=0),
    )
    user_rate_new = user_level + item_total
    item_shape_new, item_elog = item_update(
        seat, heads, item_sums, item_gain, item_level, user_total, edge, per_owner
    )
    return (user_shape_new, user_rate_new, item_shape_new, item_elog)


def solution(mesh):
    return jax.shard_map(
        shards,
        mesh=mesh,
        in_specs=(
            P(("user", "item"), None, None),
            P(("user", "item")),
            P(("user", "item")),
            P(("user", "item")),
            P(("user", "item"), None),
            P("user", None),
            P("user", None),
            P(("user", "item"), None),
            P(("user", "item"), None),
        ),
        out_specs=(
            P("user", None),
            P("user", None),
            P(("user", "item"), None),
            P(("user", "item"), None),
        ),
        check_vma=False,
    )
```

```python
import functools

import jax
import jax.numpy as jnp
from jax import lax
from jax.experimental import pallas as pl
from jax.experimental.pallas import tpu as pltpu
from jax.sharding import PartitionSpec as P

user_prior = 0.3
activity_prior = 0.3
activity_scale = 1.0
item_prior = 0.3
popularity_prior = 0.3
popularity_scale = 1.0

VMEM_BYTES = 24 << 20
SWEEP_BYTES = 36 << 20
LANES = 128
IN_VMEM = pl.BlockSpec(memory_space=pltpu.VMEM)
IN_SMEM = pl.BlockSpec(memory_space=pltpu.SMEM)
IN_PLACE = pl.BlockSpec(memory_space=pl.ANY)


def in_hbm(array):
    return pltpu.with_memory_space_constraint(array, pltpu.HBM)


def digamma_rest(x):
    w = x * (x + 3.0)
    steps = (2.0 * x + 3.0) * (2.0 * w + 2.0) / (w * (w + 2.0))
    inverse = 1.0 / (x + 4.0)
    z = inverse * inverse
    series = z * (1.0 / 12.0 - z * (1.0 / 120.0 - z * (1.0 / 252.0 - z * (1.0 / 240.0))))
    return steps + 0.5 * inverse + series


def digamma(x):
    return jnp.log(x + 4.0) - digamma_rest(x)


def gains_of(shape_values, rate_values, prior, strength):
    inverse_rate = 1.0 / rate_values
    gain = (shape_values + 4.0) * jnp.exp(-digamma_rest(shape_values)) * inverse_rate
    mean = shape_values * inverse_rate
    return gain.astype(jnp.bfloat16), strength / (prior + jnp.sum(mean, axis=1, keepdims=True)), mean


def head_kernel(touched_from, shape_from, rate_from, head_ref, touched_ref, shape_ref, rate_ref, arrived):
    per_owner, devices = touched_ref.shape
    rows, factors = shape_ref.shape
    parts = (arrived.shape[0] - 1) // 2
    step = rows // parts

    def fetch(part):
        piece = pl.ds(part * step, step)
        return [
            pltpu.make_async_copy(shape_from.at[piece], shape_ref.at[piece], arrived.at[2 * part]),
            pltpu.make_async_copy(rate_from.at[piece], rate_ref.at[piece], arrived.at[2 * part + 1]),
        ]

    table = pltpu.make_async_copy(touched_from, touched_ref, arrived.at[2 * parts])
    for part in range(parts):
        for copy in fetch(part):
            copy.start()
    table.start()
    total = jnp.zeros((1, factors), jnp.float32)
    for part in range(parts):
        for copy in fetch(part):
            copy.wait()
        piece = pl.ds(part * step, step)
        total += jnp.sum(shape_ref[piece, :] / rate_ref[piece, :], axis=0, keepdims=True)
    table.wait()
    blocks = touched_ref[...].astype(jnp.float32)
    row = jnp.concatenate(
        [blocks[place : place + 1] for place in range(per_owner)]
        + [jnp.zeros((1, LANES - per_owner * devices), jnp.float32), total],
        axis=1,
    )
    head_ref[...] = jnp.broadcast_to(row.reshape(1, 1, LANES + factors), head_ref.shape)


def head_of(touched, item_shape, item_rate):
    rows, factors = item_shape.shape
    devices, per_owner = touched.shape
    head_shape = (devices, 1, LANES + factors)
    return pl.pallas_call(
        head_kernel,
        grid=(1,),
        in_specs=[IN_PLACE, IN_PLACE, IN_PLACE],
        out_specs=pl.BlockSpec(head_shape, lambda r: (0, 0, 0)),
        out_shape=pltpu.HBM(head_shape, jnp.float32),
        scratch_shapes=[
            pltpu.VMEM((per_owner, devices), jnp.int32),
            pltpu.VMEM((rows, factors), jnp.float32),
            pltpu.VMEM((rows, factors), jnp.float32),
            pltpu.SemaphoreType.DMA((9,)),
        ],
        compiler_params=pltpu.CompilerParams(vmem_limit_bytes=VMEM_BYTES),
        cost_estimate=pl.CostEstimate(
            flops=4 * rows * factors, bytes_accessed=8 * rows * factors, transcendentals=rows * factors
        ),
    )(in_hbm(touched.T), in_hbm(item_shape), in_hbm(item_rate))


def item_gain_kernel(strength, shape_ref, rate_ref, gain_ref, level_ref):
    gain_ref[...], level_ref[...], _ = gains_of(
        shape_ref[...], rate_ref[...], popularity_prior / popularity_scale, strength
    )


def item_gains(item_shape, item_rate):
    rows, factors = item_shape.shape
    step = rows // 2
    row_spec = pl.BlockSpec((step, factors), lambda r: (r, 0))
    return pl.pallas_call(
        functools.partial(item_gain_kernel, popularity_prior + factors * item_prior),
        grid=(rows // step,),
        in_specs=[row_spec, row_spec],
        out_specs=[row_spec, pl.BlockSpec((step, 1), lambda r: (r, 0))],
        out_shape=[
            pltpu.HBM((rows, factors), jnp.bfloat16),
            pltpu.HBM((rows, 1), jnp.float32),
        ],
        compiler_params=pltpu.CompilerParams(vmem_limit_bytes=VMEM_BYTES),
        cost_estimate=pl.CostEstimate(
            flops=40 * rows * factors, bytes_accessed=10 * rows * factors, transcendentals=4 * rows * factors
        ),
    )(in_hbm(item_shape), in_hbm(item_rate))


def user_gain_kernel(strength, shape_ref, rate_ref, head_ref, gain_ref, level_ref, turned_ref, column_ref):
    gain, level_ref[...], _ = gains_of(shape_ref[...], rate_ref[...], activity_prior / activity_scale, strength)
    gain_ref[...] = gain
    turned_ref[...] = gain.T

    @pl.when(pl.program_id(0) == 0)
    def _():
        factors = gain.shape[1]
        means = head_ref[:, :, pl.ds(head_ref.shape[2] - factors, factors)]
        column_ref[...] = jnp.sum(means, axis=0).reshape(1, factors)


def user_gains(user_shape, user_rate, heads):
    rows, factors = user_shape.shape
    step = rows // 4
    row_spec = pl.BlockSpec((step, factors), lambda r: (r, 0))
    return pl.pallas_call(
        functools.partial(user_gain_kernel, activity_prior + factors * user_prior),
        grid=(rows // step,),
        in_specs=[row_spec, row_spec, pl.BlockSpec(heads.shape, lambda r: (0, 0, 0))],
        out_specs=[
            row_spec,
            pl.BlockSpec((step, 1), lambda r: (r, 0)),
            pl.BlockSpec((factors, step), lambda r: (0, r)),
            pl.BlockSpec((1, factors), lambda r: (0, 0)),
        ],
        out_shape=[
            pltpu.HBM((rows, factors), jnp.bfloat16),
            pltpu.HBM((rows, 1), jnp.float32),
            pltpu.HBM((factors, rows), jnp.bfloat16),
            pltpu.HBM((1, factors), jnp.float32),
        ],
        compiler_params=pltpu.CompilerParams(vmem_limit_bytes=VMEM_BYTES),
        cost_estimate=pl.CostEstimate(
            flops=40 * rows * factors, bytes_accessed=12 * rows * factors, transcendentals=4 * rows * factors
        ),
    )(in_hbm(user_shape), in_hbm(user_rate), heads)


def block_at(table_ref, device, place, seat):
    return table_ref[device, 0, place * table_ref.shape[0] + seat].astype(jnp.int32)


def pick_kernel(per_owner, seat_ref, head_from, gain_from, picked_out, table_ref, gain_ref, picked_ref, arrived, sent):
    blocks, edge, _ = gain_ref.shape
    devices = table_ref.shape[0]
    fetches = [pltpu.make_async_copy(head_from.at[:, :, pl.ds(0, LANES)], table_ref, arrived.at[blocks])] + [
        pltpu.make_async_copy(gain_from.at[block], gain_ref.at[block], arrived.at[block]) for block in range(blocks)
    ]
    for copy in fetches:
        copy.start()
    for copy in fetches:
        copy.wait()
    per_copy = devices // sent.shape[0]
    copies = []
    for part in range(sent.shape[0]):
        for device in range(part * per_copy, (part + 1) * per_copy):
            for place in range(per_owner):
                block = block_at(table_ref, device, place, seat_ref[0])
                picked_ref[device, pl.ds(place * edge, edge), :] = gain_ref[block]
        piece = pl.ds(part * per_copy, per_copy)
        copies.append(pltpu.make_async_copy(picked_ref.at[piece], picked_out.at[piece], sent.at[part]))
        copies[-1].start()
    for copy in copies:
        copy.wait()


def pick(seat, heads, item_gain, edge, per_owner):
    items, factors = item_gain.shape
    devices = heads.shape[0]
    return pl.pallas_call(
        functools.partial(pick_kernel, per_owner),
        in_specs=[IN_SMEM, IN_PLACE, IN_PLACE],
        out_specs=IN_PLACE,
        scratch_shapes=[
            pltpu.SMEM((devices, 1, LANES), jnp.float32),
            pltpu.VMEM((items // edge, edge, factors), jnp.bfloat16),
            pltpu.VMEM((devices, per_owner * edge, factors), jnp.bfloat16),
            pltpu.SemaphoreType.DMA((items // edge + 1,)),
            pltpu.SemaphoreType.DMA((min(8, devices),)),
        ],
        out_shape=pltpu.HBM((devices, per_owner * edge, factors), jnp.bfloat16),
        compiler_params=pltpu.CompilerParams(vmem_limit_bytes=VMEM_BYTES),
        cost_estimate=pl.CostEstimate(
            flops=0, bytes_accessed=2 * items * factors + 2 * devices * per_owner * edge * factors, transcendentals=0
        ),
    )(seat, heads, in_hbm(item_gain.reshape(items // edge, edge, factors)))


def dense_kernel(user_of, slot_of, live_ref, counts_ref, after_ref, out_ref, dense_ref, held_ref, arrived, sent):
    depth, group = held_ref.shape[:2]
    live = live_ref[0]
    groups = (live + group - 1) // group

    def fetch(index):
        place = lax.rem(index, depth)
        return pltpu.make_async_copy(
            counts_ref.at[pl.ds(index * group, group)], held_ref.at[place], arrived.at[place]
        )

    for index in range(depth):

        @pl.when(index < groups)
        def _():
            fetch(index).start()

    def clear(slot, carry):
        dense_ref[slot] = jnp.zeros(dense_ref.shape[1:], dense_ref.dtype)
        return carry

    lax.fori_loop(0, dense_ref.shape[0], clear, 0)

    def add_group(index, carry):
        fetch(index).wait()
        place = lax.rem(index, depth)
        for offset in range(group):
            tile = index * group + offset

            @pl.when(tile < live)
            def _():
                user, slot = user_of[tile], slot_of[tile]
                dense_ref[slot, user] += held_ref[place, offset].astype(jnp.float32).astype(jnp.bfloat16)

        @pl.when(index + depth < groups)
        def _():
            fetch(index + depth).start()

        return carry

    lax.fori_loop(0, groups, add_group, 0)
    slots = dense_ref.shape[0] // sent.shape[0]
    copies = [
        pltpu.make_async_copy(
            dense_ref.at[pl.ds(part * slots, slots)], out_ref.at[pl.ds(part * slots, slots)], sent.at[part]
        )
        for part in range(sent.shape[0])
    ]
    for copy in copies:
        copy.start()
    for copy in copies:
        copy.wait()


def dense_counts(counts, tile_user, tile_slot, live_tiles, slot_count, user_blocks, after):
    tiles, edge, _ = counts.shape
    group = 8
    depth = min(8, tiles // group)
    return pl.pallas_call(
        dense_kernel,
        in_specs=[IN_SMEM, IN_SMEM, IN_SMEM, IN_PLACE, IN_VMEM],
        out_specs=IN_PLACE,
        scratch_shapes=[
            pltpu.VMEM((slot_count, user_blocks, edge, edge), jnp.bfloat16),
            pltpu.VMEM((depth, group, edge, edge), jnp.int32),
            pltpu.SemaphoreType.DMA((depth,)),
            pltpu.SemaphoreType.DMA((min(16, slot_count),)),
        ],
        out_shape=pltpu.HBM((slot_count, user_blocks, edge, edge), jnp.bfloat16),
        compiler_params=pltpu.CompilerParams(vmem_limit_bytes=VMEM_BYTES),
        cost_estimate=pl.CostEstimate(
            flops=tiles * edge * edge, bytes_accessed=4 * counts.size + 2 * slot_count * user_blocks * edge * edge,
            transcendentals=0,
        ),
    )(tile_user, tile_slot, live_tiles, in_hbm(counts), after)


def sweep_kernel(
    prior_share, place_ref, dense_from, items_ref, gain_from, turned_from, level_from, total_ref,
    item_ref, kept_out, given_out, part_out,
    dense_ref, gain_ref, turned_ref, level_ref, acc_ref, early_ref, late_ref, sums_ref, given_ref, part_ref,
    arrived, sent,
):
    owners, touched_rows, factors = items_ref.shape
    slots, user_blocks, edge, _ = dense_ref.shape
    users = user_blocks * edge
    per_owner = slots // owners
    pair = 2
    chunk = users // 2
    last = owners // pair - 1

    def items_of(index):
        return items_ref[pl.ds(index * pair, pair)].reshape(pair * touched_rows, factors)

    def denominators(index):
        turned_items = items_of(index).T
        return [
            jnp.dot(gain_ref[pl.ds(first, chunk), :], turned_items, preferred_element_type=jnp.float32)
            for first in range(0, users, chunk)
        ]

    def put_ratios(index, parts, ratio_ref):
        for place, denominator in enumerate(parts):
            blocks = pl.ds(place * (chunk // edge), chunk // edge)
            counted = jnp.concatenate(
                [
                    dense_ref[index * pair * per_owner + slot, blocks].reshape(chunk, edge)
                    for slot in range(pair * per_owner)
                ],
                axis=1,
            ).astype(jnp.float32)
            ratio_ref[pl.ds(place * chunk, chunk), :] = (counted * pl.reciprocal(denominator, approx=True)).astype(
                jnp.bfloat16
            )

    def copy_of(index):
        return pltpu.make_async_copy(
            sums_ref.at[pl.ds(index * pair, pair)],
            item_ref.at[pl.ds(index * pair, pair), pl.ds(0, touched_rows)],
            sent.at[index],
        )

    def add_products(index, ratio_ref):
        items = items_of(index)
        for first in range(0, users, chunk):
            rows = pl.ds(first, chunk)
            acc_ref[rows, :] += jnp.dot(ratio_ref[rows, :], items, preferred_element_type=jnp.float32)
        sums = jnp.dot(turned_ref[...], ratio_ref[...], preferred_element_type=jnp.float32)
        sums_ref[pl.ds(index * pair, pair)] = sums.astype(jnp.bfloat16).T.reshape(pair, touched_rows, factors)
        copy_of(index).start()

    def fetch(index):
        slots_of = pl.ds(index * pair * per_owner, pair * per_owner)
        return pltpu.make_async_copy(dense_from.at[slots_of], dense_ref.at[slots_of], arrived.at[index])

    gain_rows = [pl.ds(first, chunk) for first in range(0, users, chunk)]
    first_copies = [
        pltpu.make_async_copy(gain_from.at[rows], gain_ref.at[rows], arrived.at[last + 1 + place])
        for place, rows in enumerate(gain_rows)
    ]
    later_copies = [
        pltpu.make_async_copy(source, target, arrived.at[last + 3 + place])
        for place, (source, target) in enumerate(((turned_from, turned_ref), (level_from, level_ref)))
    ]
    first_copies[0].start()
    fetch(0).start()
    first_copies[1].start()
    acc_ref[...] = jnp.zeros_like(acc_ref)
    for copy in first_copies:
        copy.wait()
    later_copies[0].start()
    for index in range(1, last + 1):
        fetch(index).start()
    later_copies[1].start()
    fetch(0).wait()
    put_ratios(0, denominators(0), early_ref)
    later_copies[0].wait()

    def turn(step, carry):
        first, second, third = 2 * step, 2 * step + 1, jnp.minimum(2 * step + 2, last)
        fetch(second).wait()

        @pl.when(third > second)
        def _():
            fetch(third).wait()

        late = denominators(second)
        add_products(first, early_ref)
        put_ratios(second, late, late_ref)
        early = denominators(third)
        add_products(second, late_ref)
        put_ratios(third, early, early_ref)
        return carry

    lax.fori_loop(0, (last + 1) // 2, turn, 0)

    half = users // 2
    step = half // 2
    core = lax.rem(place_ref[0], 2)
    copies = []
    for index in range(2):
        kept = pl.ds(pl.multiple_of(core * half + index * step, step), step)
        given = pl.ds(pl.multiple_of((1 - core) * half + index * step, step), step)
        rows = pl.ds(index * step, step)
        given_ref[rows, :] = acc_ref[given, :].astype(jnp.bfloat16)
        copies.append(pltpu.make_async_copy(acc_ref.at[kept], kept_out.at[rows], sent.at[last + 1 + 2 * index]))
        copies.append(pltpu.make_async_copy(given_ref.at[rows], given_out.at[rows], sent.at[last + 2 + 2 * index]))
    for copy in copies:
        copy.start()
    later_copies[1].wait()
    part = jnp.zeros((1, factors), jnp.float32)
    for first in range(0, users, step):
        rows = pl.ds(first, step)
        shape_share = prior_share + gain_ref[rows, :].astype(jnp.float32) * acc_ref[rows, :]
        inverse_rate = pl.reciprocal(level_ref[rows, :] + total_ref[...], approx=True)
        part += jnp.sum(shape_share * inverse_rate, axis=0, keepdims=True)
    part_ref[...] = part
    copies.append(pltpu.make_async_copy(part_ref, part_out, sent.at[last + 5]))
    copies[-1].start()
    for index in range(last + 1):
        copy_of(index).wait()
    for copy in copies:
        copy.wait()


def sweep(place, dense, items, user_gain, turned_gain, user_level, item_total, columns):
    owners, touched_rows, factors = items.shape
    users = user_gain.shape[0]
    pair = 2
    return pl.pallas_call(
        functools.partial(sweep_kernel, user_prior / columns),
        in_specs=[IN_SMEM, IN_PLACE, IN_VMEM, IN_PLACE, IN_PLACE, IN_PLACE, IN_VMEM],
        out_specs=[IN_PLACE] * 4,
        scratch_shapes=[
            pltpu.VMEM(dense.shape, jnp.bfloat16),
            pltpu.VMEM((users, factors), jnp.bfloat16),
            pltpu.VMEM((factors, users), jnp.bfloat16),
            pltpu.VMEM((users, 1), jnp.float32),
            pltpu.VMEM((users, factors), jnp.float32),
            pltpu.VMEM((users, pair * touched_rows), jnp.bfloat16),
            pltpu.VMEM((users, pair * touched_rows), jnp.bfloat16),
            pltpu.VMEM((owners, touched_rows, factors), jnp.bfloat16),
            pltpu.VMEM((users // 2, factors), jnp.bfloat16),
            pltpu.VMEM((1, factors), jnp.float32),
            pltpu.SemaphoreType.DMA((owners // pair + 4,)),
            pltpu.SemaphoreType.DMA((owners // pair + 5,)),
        ],
        out_shape=[
            pltpu.HBM((owners, touched_rows, factors), jnp.bfloat16),
            pltpu.HBM((users // 2, factors), jnp.float32),
            pltpu.HBM((users // 2, factors), jnp.bfloat16),
            pltpu.HBM((1, factors), jnp.float32),
        ],
        compiler_params=pltpu.CompilerParams(vmem_limit_bytes=SWEEP_BYTES),
        cost_estimate=pl.CostEstimate(
            flops=6 * owners * touched_rows * users * factors,
            bytes_accessed=2 * dense.size + 4 * items.size + 4 * users * factors,
            transcendentals=owners * touched_rows * users,
        ),
    )(place, in_hbm(dense), items, in_hbm(user_gain), in_hbm(turned_gain), in_hbm(user_level), item_total)


def chip_kernel(kept_ref, got_ref, sum_ref):
    sum_ref[...] = (kept_ref[...] + got_ref[...].astype(jnp.float32)).astype(jnp.bfloat16)


def chip_sums(kept, got):
    rows, factors = kept.shape
    spec = pl.BlockSpec((rows // 2, factors), lambda r: (r, 0))
    return pl.pallas_call(
        chip_kernel,
        grid=(2,),
        in_specs=[spec, spec],
        out_specs=spec,
        out_shape=pltpu.HBM((rows, factors), jnp.bfloat16),
        compiler_params=pltpu.CompilerParams(vmem_limit_bytes=VMEM_BYTES),
        cost_estimate=pl.CostEstimate(flops=rows * factors, bytes_accessed=8 * rows * factors, transcendentals=0),
    )(kept, got)


def slab_kernel(place_ref, after_ref, gain_ref, *rest):
    sums_refs, shape_ref = rest[:-1], rest[-1]
    parts = [ref[...].astype(jnp.float32) for ref in sums_refs]
    while len(parts) > 1:
        apart = len(parts) // 2
        parts = [parts[k] + parts[k + apart] for k in range(apart)]
    shape_ref[...] = user_prior + gain_ref[...].astype(jnp.float32) * parts[0]


def slab_shapes(place, sums, user_gain, after):
    rows, factors = sums[0].shape
    spec = pl.BlockSpec((rows // 2, factors), lambda r, place_ref: (r, 0))
    return pl.pallas_call(
        slab_kernel,
        grid_spec=pltpu.PrefetchScalarGridSpec(
            num_scalar_prefetch=1,
            grid=(2,),
            in_specs=[
                IN_PLACE,
                pl.BlockSpec((rows // 2, factors), lambda r, place_ref: (lax.rem(place_ref[0], 2) * 2 + r, 0)),
            ]
            + [spec] * len(sums),
            out_specs=spec,
        ),
        out_shape=pltpu.HBM((rows, factors), jnp.float32),
        compiler_params=pltpu.CompilerParams(vmem_limit_bytes=VMEM_BYTES),
        cost_estimate=pl.CostEstimate(
            flops=len(sums) * rows * factors, bytes_accessed=2 * (len(sums) + 3) * rows * factors, transcendentals=0
        ),
    )(place, after, in_hbm(user_gain), in_hbm(sums[0]), *sums[1:])


def item_kernel(
    per_owner, seat_ref, head_from, sums_ref, gain_from, level_from, near_ref, far_ref, shape_out, elog_out,
    table_ref, acc_ref, gain_ref, level_ref, shape_ref, elog_ref, arrived, sent,
):
    blocks, edge, _ = acc_ref.shape
    fetches = [
        pltpu.make_async_copy(source, target, arrived.at[place])
        for place, (source, target) in enumerate(
            ((head_from.at[:, :, pl.ds(0, LANES)], table_ref), (gain_from, gain_ref), (level_from, level_ref))
        )
    ]
    for copy in fetches:
        copy.start()
    acc_ref[...] = jnp.zeros_like(acc_ref)
    fetches[0].wait()
    for sender in range(sums_ref.shape[0]):
        for place in range(per_owner):
            block = block_at(table_ref, sender, place, seat_ref[0])
            acc_ref[block] += sums_ref[sender, pl.ds(place * edge, edge), :].astype(jnp.float32)
    for copy in fetches[1:]:
        copy.wait()
    user_total = near_ref[...] + far_ref[...]
    copies = []
    for block in range(blocks):
        rows = pl.ds(block * edge, edge)
        shape_new = item_prior + gain_ref[rows, :].astype(jnp.float32) * acc_ref[block]
        shape_ref[rows, :] = shape_new
        elog_ref[rows, :] = digamma(shape_new) - jnp.log(level_ref[rows, :] + user_total)
        copies.append(pltpu.make_async_copy(shape_ref.at[rows], shape_out.at[rows], sent.at[2 * block]))
        copies.append(pltpu.make_async_copy(elog_ref.at[rows], elog_out.at[rows], sent.at[2 * block + 1]))
        for copy in copies[-2:]:
            copy.start()
    for copy in copies:
        copy.wait()


def item_update(seat, heads, sums, item_gain, item_level, near, far, edge, per_owner):
    items, factors = item_gain.shape
    return pl.pallas_call(
        functools.partial(item_kernel, per_owner),
        in_specs=[IN_SMEM, IN_PLACE, IN_VMEM, IN_PLACE, IN_PLACE, IN_VMEM, IN_VMEM],
        out_specs=[IN_PLACE, IN_PLACE],
        scratch_shapes=[
            pltpu.SMEM((heads.shape[0], 1, LANES), jnp.float32),
            pltpu.VMEM((items // edge, edge, factors), jnp.float32),
            pltpu.VMEM((items, factors), jnp.bfloat16),
            pltpu.VMEM((items, 1), jnp.float32),
            pltpu.VMEM((items, factors), jnp.float32),
            pltpu.VMEM((items, factors), jnp.float32),
            pltpu.SemaphoreType.DMA((3,)),
            pltpu.SemaphoreType.DMA((2 * (items // edge),)),
        ],
        out_shape=[pltpu.HBM((items, factors), jnp.float32)] * 2,
        compiler_params=pltpu.CompilerParams(vmem_limit_bytes=VMEM_BYTES),
        cost_estimate=pl.CostEstimate(
            flops=40 * items * factors, bytes_accessed=2 * sums.size + 10 * items * factors,
            transcendentals=4 * items * factors,
        ),
    )(seat, heads, sums, in_hbm(item_gain), in_hbm(item_level), near, far)


def ahead(array, axis, count):
    size = lax.axis_size(axis)
    return lax.ppermute(array, axis, [(j, (j + count) % size) for j in range(size)])


def across(array, axis, bit):
    return lax.ppermute(array, axis, [(j, j ^ bit) for j in range(lax.axis_size(axis))])


def shards(
    counts, tile_user, tile_slot, live_tiles, touched, user_shape, user_rate, item_shape, item_rate
):
    edge = counts.shape[1]
    users, factors = user_shape.shape
    user_blocks = users // edge
    owners, per_owner = touched.shape
    columns = lax.axis_size("item")
    place = lax.axis_index("item").astype(jnp.int32).reshape(1)
    seat = lax.axis_index("user").astype(jnp.int32).reshape(1)
    heads = lax.all_to_all(head_of(touched, item_shape, item_rate), "user", 0, 0)
    item_gain, item_level = item_gains(item_shape, item_rate)
    item_rows = lax.all_to_all(pick(seat, heads, item_gain, edge, per_owner), "user", 0, 0)
    user_gain, user_level, turned_gain, column_total = user_gains(user_shape, user_rate, heads)
    item_total = jnp.sum(lax.all_gather(column_total, "item", axis=0, tiled=True), axis=0, keepdims=True)
    dense = dense_counts(
        counts, tile_user, tile_slot, live_tiles, owners * per_owner, user_blocks, item_total
    )
    item_sums, kept, given, user_total = sweep(
        place, dense, item_rows, user_gain, turned_gain, user_level, item_total, columns
    )
    item_sums = lax.all_to_all(item_sums, "user", 0, 0)
    user_total = jnp.sum(lax.all_gather(user_total, "item", axis=0, tiled=True), axis=0, keepdims=True)
    bits = [1 << step for step in range(owners.bit_length() - 1)]
    for bit in bits[:2]:
        user_total = user_total + across(user_total, "user", bit)
    chip = chip_sums(kept, across(given, "item", 1))
    own_shapes = slab_shapes(
        place, [chip] + [ahead(chip, "item", count) for count in range(2, columns, 2)], user_gain, user_total
    )
    for bit in bits[2:-1]:
        user_total = user_total + across(user_total, "user", bit)
    far_total = across(user_total, "user", bits[-1])
    other_shapes = across(own_shapes, "item", 1)
    user_shape_new = jnp.where(
        place[0] % 2 == 0,
        jnp.concatenate([own_shapes, other_shapes], axis=0),
        jnp.concatenate([other_shapes, own_shapes], axis=0),
    )
    user_rate_new = user_level + item_total
    item_shape_new, item_elog = item_update(
        seat, heads, item_sums, item_gain, item_level, user_total, far_total, edge, per_owner
    )
    return (user_shape_new, user_rate_new, item_shape_new, item_elog)


def solution(mesh):
    return jax.shard_map(
        shards,
        mesh=mesh,
        in_specs=(
            P(("user", "item"), None, None),
            P(("user", "item")),
            P(("user", "item")),
            P(("user", "item")),
            P(("user", "item"), None),
            P("user", None),
            P("user", None),
            P(("user", "item"), None),
            P(("user", "item"), None),
        ),
        out_specs=(
            P("user", None),
            P("user", None),
            P(("user", "item"), None),
            P(("user", "item"), None),
        ),
        check_vma=False,
    )
```

```python
import functools

import jax
import jax.numpy as jnp
from jax import lax
from jax.experimental import pallas as pl
from jax.experimental.pallas import tpu as pltpu
from jax.sharding import PartitionSpec as P

user_prior = 0.3
activity_prior = 0.3
activity_scale = 1.0
item_prior = 0.3
popularity_prior = 0.3
popularity_scale = 1.0

VMEM_BYTES = 24 << 20
SWEEP_BYTES = 36 << 20
LANES = 128
IN_VMEM = pl.BlockSpec(memory_space=pltpu.VMEM)
IN_SMEM = pl.BlockSpec(memory_space=pltpu.SMEM)
IN_PLACE = pl.BlockSpec(memory_space=pl.ANY)


def in_hbm(array):
    return pltpu.with_memory_space_constraint(array, pltpu.HBM)


def digamma_rest(x):
    w = x * (x + 3.0)
    steps = (2.0 * x + 3.0) * (2.0 * w + 2.0) / (w * (w + 2.0))
    inverse = 1.0 / (x + 4.0)
    z = inverse * inverse
    series = z * (1.0 / 12.0 - z * (1.0 / 120.0 - z * (1.0 / 252.0 - z * (1.0 / 240.0))))
    return steps + 0.5 * inverse + series


def digamma(x):
    return jnp.log(x + 4.0) - digamma_rest(x)


def gains_of(shape_values, rate_values, prior, strength):
    inverse_rate = 1.0 / rate_values
    gain = (shape_values + 4.0) * jnp.exp(-digamma_rest(shape_values)) * inverse_rate
    mean = shape_values * inverse_rate
    return gain.astype(jnp.bfloat16), strength / (prior + jnp.sum(mean, axis=1, keepdims=True)), mean


def head_kernel(touched_from, shape_from, rate_from, head_ref, touched_ref, shape_ref, rate_ref, arrived):
    per_owner, devices = touched_ref.shape
    rows, factors = shape_ref.shape
    parts = (arrived.shape[0] - 1) // 2
    step = rows // parts

    def fetch(part):
        piece = pl.ds(part * step, step)
        return [
            pltpu.make_async_copy(shape_from.at[piece], shape_ref.at[piece], arrived.at[2 * part]),
            pltpu.make_async_copy(rate_from.at[piece], rate_ref.at[piece], arrived.at[2 * part + 1]),
        ]

    table = pltpu.make_async_copy(touched_from, touched_ref, arrived.at[2 * parts])
    for part in range(parts):
        for copy in fetch(part):
            copy.start()
    table.start()
    total = jnp.zeros((1, factors), jnp.float32)
    for part in range(parts):
        for copy in fetch(part):
            copy.wait()
        piece = pl.ds(part * step, step)
        total += jnp.sum(shape_ref[piece, :] / rate_ref[piece, :], axis=0, keepdims=True)
    table.wait()
    blocks = touched_ref[...].astype(jnp.float32)
    row = jnp.concatenate(
        [blocks[place : place + 1] for place in range(per_owner)]
        + [jnp.zeros((1, LANES - per_owner * devices), jnp.float32), total],
        axis=1,
    )
    head_ref[...] = jnp.broadcast_to(row.reshape(1, 1, LANES + factors), head_ref.shape)


def head_of(touched, item_shape, item_rate):
    rows, factors = item_shape.shape
    devices, per_owner = touched.shape
    head_shape = (devices, 1, LANES + factors)
    return pl.pallas_call(
        head_kernel,
        grid=(1,),
        in_specs=[IN_PLACE, IN_PLACE, IN_PLACE],
        out_specs=pl.BlockSpec(head_shape, lambda r: (0, 0, 0)),
        out_shape=pltpu.HBM(head_shape, jnp.float32),
        scratch_shapes=[
            pltpu.VMEM((per_owner, devices), jnp.int32),
            pltpu.VMEM((rows, factors), jnp.float32),
            pltpu.VMEM((rows, factors), jnp.float32),
            pltpu.SemaphoreType.DMA((9,)),
        ],
        compiler_params=pltpu.CompilerParams(vmem_limit_bytes=VMEM_BYTES),
        cost_estimate=pl.CostEstimate(
            flops=4 * rows * factors, bytes_accessed=8 * rows * factors, transcendentals=rows * factors
        ),
    )(in_hbm(touched.T), in_hbm(item_shape), in_hbm(item_rate))


def item_gain_kernel(strength, shape_ref, rate_ref, gain_ref, level_ref):
    gain_ref[...], level_ref[...], _ = gains_of(
        shape_ref[...], rate_ref[...], popularity_prior / popularity_scale, strength
    )


def item_gains(item_shape, item_rate):
    rows, factors = item_shape.shape
    step = rows // 2
    row_spec = pl.BlockSpec((step, factors), lambda r: (r, 0))
    return pl.pallas_call(
        functools.partial(item_gain_kernel, popularity_prior + factors * item_prior),
        grid=(rows // step,),
        in_specs=[row_spec, row_spec],
        out_specs=[row_spec, pl.BlockSpec((step, 1), lambda r: (r, 0))],
        out_shape=[
            pltpu.HBM((rows, factors), jnp.bfloat16),
            pltpu.HBM((rows, 1), jnp.float32),
        ],
        compiler_params=pltpu.CompilerParams(vmem_limit_bytes=VMEM_BYTES),
        cost_estimate=pl.CostEstimate(
            flops=40 * rows * factors, bytes_accessed=10 * rows * factors, transcendentals=4 * rows * factors
        ),
    )(in_hbm(item_shape), in_hbm(item_rate))


def user_gain_kernel(strength, shape_ref, rate_ref, head_ref, gain_ref, level_ref, turned_ref, column_ref):
    gain, level_ref[...], _ = gains_of(shape_ref[...], rate_ref[...], activity_prior / activity_scale, strength)
    gain_ref[...] = gain
    turned_ref[...] = gain.T

    @pl.when(pl.program_id(0) == 0)
    def _():
        factors = gain.shape[1]
        means = head_ref[:, :, pl.ds(head_ref.shape[2] - factors, factors)]
        column_ref[...] = jnp.sum(means, axis=0).reshape(1, factors)


def user_gains(user_shape, user_rate, heads):
    rows, factors = user_shape.shape
    step = rows // 4
    row_spec = pl.BlockSpec((step, factors), lambda r: (r, 0))
    return pl.pallas_call(
        functools.partial(user_gain_kernel, activity_prior + factors * user_prior),
        grid=(rows // step,),
        in_specs=[row_spec, row_spec, pl.BlockSpec(heads.shape, lambda r: (0, 0, 0))],
        out_specs=[
            row_spec,
            pl.BlockSpec((step, 1), lambda r: (r, 0)),
            pl.BlockSpec((factors, step), lambda r: (0, r)),
            pl.BlockSpec((1, factors), lambda r: (0, 0)),
        ],
        out_shape=[
            pltpu.HBM((rows, factors), jnp.bfloat16),
            pltpu.HBM((rows, 1), jnp.float32),
            pltpu.HBM((factors, rows), jnp.bfloat16),
            pltpu.HBM((1, factors), jnp.float32),
        ],
        compiler_params=pltpu.CompilerParams(vmem_limit_bytes=VMEM_BYTES),
        cost_estimate=pl.CostEstimate(
            flops=40 * rows * factors, bytes_accessed=12 * rows * factors, transcendentals=4 * rows * factors
        ),
    )(in_hbm(user_shape), in_hbm(user_rate), heads)


def block_at(table_ref, device, place, seat):
    return table_ref[device, 0, place * table_ref.shape[0] + seat].astype(jnp.int32)


def pick_kernel(per_owner, seat_ref, head_from, gain_from, picked_out, table_ref, gain_ref, picked_ref, arrived, sent):
    blocks, edge, _ = gain_ref.shape
    devices = table_ref.shape[0]
    fetches = [pltpu.make_async_copy(head_from.at[:, :, pl.ds(0, LANES)], table_ref, arrived.at[blocks])] + [
        pltpu.make_async_copy(gain_from.at[block], gain_ref.at[block], arrived.at[block]) for block in range(blocks)
    ]
    for copy in fetches:
        copy.start()
    for copy in fetches:
        copy.wait()
    per_copy = devices // sent.shape[0]
    copies = []
    for part in range(sent.shape[0]):
        for device in range(part * per_copy, (part + 1) * per_copy):
            for place in range(per_owner):
                block = block_at(table_ref, device, place, seat_ref[0])
                picked_ref[device, pl.ds(place * edge, edge), :] = gain_ref[block]
        piece = pl.ds(part * per_copy, per_copy)
        copies.append(pltpu.make_async_copy(picked_ref.at[piece], picked_out.at[piece], sent.at[part]))
        copies[-1].start()
    for copy in copies:
        copy.wait()


def pick(seat, heads, item_gain, edge, per_owner):
    items, factors = item_gain.shape
    devices = heads.shape[0]
    return pl.pallas_call(
        functools.partial(pick_kernel, per_owner),
        in_specs=[IN_SMEM, IN_PLACE, IN_PLACE],
        out_specs=IN_PLACE,
        scratch_shapes=[
            pltpu.SMEM((devices, 1, LANES), jnp.float32),
            pltpu.VMEM((items // edge, edge, factors), jnp.bfloat16),
            pltpu.VMEM((devices, per_owner * edge, factors), jnp.bfloat16),
            pltpu.SemaphoreType.DMA((items // edge + 1,)),
            pltpu.SemaphoreType.DMA((min(8, devices),)),
        ],
        out_shape=pltpu.HBM((devices, per_owner * edge, factors), jnp.bfloat16),
        compiler_params=pltpu.CompilerParams(vmem_limit_bytes=VMEM_BYTES),
        cost_estimate=pl.CostEstimate(
            flops=0, bytes_accessed=2 * items * factors + 2 * devices * per_owner * edge * factors, transcendentals=0
        ),
    )(seat, heads, in_hbm(item_gain.reshape(items // edge, edge, factors)))


def dense_kernel(user_of, slot_of, live_ref, counts_ref, after_ref, out_ref, dense_ref, held_ref, arrived, sent):
    depth, group = held_ref.shape[:2]
    live = live_ref[0]
    groups = (live + group - 1) // group

    def fetch(index):
        place = lax.rem(index, depth)
        return pltpu.make_async_copy(
            counts_ref.at[pl.ds(index * group, group)], held_ref.at[place], arrived.at[place]
        )

    for index in range(depth):

        @pl.when(index < groups)
        def _():
            fetch(index).start()

    def clear(slot, carry):
        dense_ref[slot] = jnp.zeros(dense_ref.shape[1:], dense_ref.dtype)
        return carry

    lax.fori_loop(0, dense_ref.shape[0], clear, 0)

    def add_group(index, carry):
        fetch(index).wait()
        place = lax.rem(index, depth)
        for offset in range(group):
            tile = index * group + offset

            @pl.when(tile < live)
            def _():
                user, slot = user_of[tile], slot_of[tile]
                dense_ref[slot, user] += held_ref[place, offset].astype(jnp.float32).astype(jnp.bfloat16)

        @pl.when(index + depth < groups)
        def _():
            fetch(index + depth).start()

        return carry

    lax.fori_loop(0, groups, add_group, 0)
    slots = dense_ref.shape[0] // sent.shape[0]
    copies = [
        pltpu.make_async_copy(
            dense_ref.at[pl.ds(part * slots, slots)], out_ref.at[pl.ds(part * slots, slots)], sent.at[part]
        )
        for part in range(sent.shape[0])
    ]
    for copy in copies:
        copy.start()
    for copy in copies:
        copy.wait()


def dense_counts(counts, tile_user, tile_slot, live_tiles, slot_count, user_blocks, after):
    tiles, edge, _ = counts.shape
    group = 8
    depth = min(8, tiles // group)
    return pl.pallas_call(
        dense_kernel,
        in_specs=[IN_SMEM, IN_SMEM, IN_SMEM, IN_PLACE, IN_VMEM],
        out_specs=IN_PLACE,
        scratch_shapes=[
            pltpu.VMEM((slot_count, user_blocks, edge, edge), jnp.bfloat16),
            pltpu.VMEM((depth, group, edge, edge), jnp.int32),
            pltpu.SemaphoreType.DMA((depth,)),
            pltpu.SemaphoreType.DMA((min(16, slot_count),)),
        ],
        out_shape=pltpu.HBM((slot_count, user_blocks, edge, edge), jnp.bfloat16),
        compiler_params=pltpu.CompilerParams(vmem_limit_bytes=VMEM_BYTES),
        cost_estimate=pl.CostEstimate(
            flops=tiles * edge * edge, bytes_accessed=4 * counts.size + 2 * slot_count * user_blocks * edge * edge,
            transcendentals=0,
        ),
    )(tile_user, tile_slot, live_tiles, in_hbm(counts), after)


def sweep_kernel(
    prior_share, place_ref, dense_from, items_ref, gain_from, turned_from, level_from, total_ref,
    item_ref, kept_out, given_out, part_out,
    dense_ref, gain_ref, turned_ref, level_ref, acc_ref, early_ref, late_ref, sums_ref, given_ref, part_ref,
    arrived, sent,
):
    owners, touched_rows, factors = items_ref.shape
    slots, user_blocks, edge, _ = dense_ref.shape
    users = user_blocks * edge
    per_owner = slots // owners
    pair = 2
    chunk = users // 2
    last = owners // pair - 1

    def items_of(index):
        return items_ref[pl.ds(index * pair, pair)].reshape(pair * touched_rows, factors)

    def denominators(index):
        turned_items = items_of(index).T
        return [
            jnp.dot(gain_ref[pl.ds(first, chunk), :], turned_items, preferred_element_type=jnp.float32)
            for first in range(0, users, chunk)
        ]

    def put_ratios(index, parts, ratio_ref):
        for place, denominator in enumerate(parts):
            blocks = pl.ds(place * (chunk // edge), chunk // edge)
            counted = jnp.concatenate(
                [
                    dense_ref[index * pair * per_owner + slot, blocks].reshape(chunk, edge)
                    for slot in range(pair * per_owner)
                ],
                axis=1,
            ).astype(jnp.float32)
            ratio_ref[pl.ds(place * chunk, chunk), :] = (counted * pl.reciprocal(denominator, approx=True)).astype(
                jnp.bfloat16
            )

    def copy_of(index):
        return pltpu.make_async_copy(
            sums_ref.at[pl.ds(index * pair, pair)],
            item_ref.at[pl.ds(index * pair, pair), pl.ds(0, touched_rows)],
            sent.at[index],
        )

    def add_products(index, ratio_ref):
        items = items_of(index)
        for first in range(0, users, chunk):
            rows = pl.ds(first, chunk)
            acc_ref[rows, :] += jnp.dot(ratio_ref[rows, :], items, preferred_element_type=jnp.float32)
        sums = jnp.dot(turned_ref[...], ratio_ref[...], preferred_element_type=jnp.float32)
        sums_ref[pl.ds(index * pair, pair)] = sums.astype(jnp.bfloat16).T.reshape(pair, touched_rows, factors)
        copy_of(index).start()

    def fetch(index):
        slots_of = pl.ds(index * pair * per_owner, pair * per_owner)
        return pltpu.make_async_copy(dense_from.at[slots_of], dense_ref.at[slots_of], arrived.at[index])

    gain_rows = [pl.ds(first, chunk) for first in range(0, users, chunk)]
    first_copies = [
        pltpu.make_async_copy(gain_from.at[rows], gain_ref.at[rows], arrived.at[last + 1 + place])
        for place, rows in enumerate(gain_rows)
    ]
    later_copies = [
        pltpu.make_async_copy(source, target, arrived.at[last + 3 + place])
        for place, (source, target) in enumerate(((turned_from, turned_ref), (level_from, level_ref)))
    ]
    first_copies[0].start()
    fetch(0).start()
    first_copies[1].start()
    acc_ref[...] = jnp.zeros_like(acc_ref)
    for copy in first_copies:
        copy.wait()
    later_copies[0].start()
    for index in range(1, last + 1):
        fetch(index).start()
    later_copies[1].start()
    fetch(0).wait()
    put_ratios(0, denominators(0), early_ref)
    later_copies[0].wait()

    def turn(step, carry):
        first, second, third = 2 * step, 2 * step + 1, jnp.minimum(2 * step + 2, last)
        fetch(second).wait()

        @pl.when(third > second)
        def _():
            fetch(third).wait()

        late = denominators(second)
        add_products(first, early_ref)
        put_ratios(second, late, late_ref)
        early = denominators(third)
        add_products(second, late_ref)
        put_ratios(third, early, early_ref)
        return carry

    lax.fori_loop(0, (last + 1) // 2, turn, 0)

    half = users // 2
    step = half // 2
    core = lax.rem(place_ref[0], 2)
    copies = []
    for index in range(2):
        kept = pl.ds(pl.multiple_of(core * half + index * step, step), step)
        given = pl.ds(pl.multiple_of((1 - core) * half + index * step, step), step)
        rows = pl.ds(index * step, step)
        given_ref[rows, :] = acc_ref[given, :].astype(jnp.bfloat16)
        copies.append(pltpu.make_async_copy(acc_ref.at[kept], kept_out.at[rows], sent.at[last + 1 + 2 * index]))
        copies.append(pltpu.make_async_copy(given_ref.at[rows], given_out.at[rows], sent.at[last + 2 + 2 * index]))
    for copy in copies:
        copy.start()
    later_copies[1].wait()
    part = jnp.zeros((1, factors), jnp.float32)
    for first in range(0, users, step):
        rows = pl.ds(first, step)
        shape_share = prior_share + gain_ref[rows, :].astype(jnp.float32) * acc_ref[rows, :]
        inverse_rate = pl.reciprocal(level_ref[rows, :] + total_ref[...], approx=True)
        part += jnp.sum(shape_share * inverse_rate, axis=0, keepdims=True)
    part_ref[...] = part
    copies.append(pltpu.make_async_copy(part_ref, part_out, sent.at[last + 5]))
    copies[-1].start()
    for index in range(last + 1):
        copy_of(index).wait()
    for copy in copies:
        copy.wait()


def sweep(place, dense, items, user_gain, turned_gain, user_level, item_total, columns):
    owners, touched_rows, factors = items.shape
    users = user_gain.shape[0]
    pair = 2
    return pl.pallas_call(
        functools.partial(sweep_kernel, user_prior / columns),
        in_specs=[IN_SMEM, IN_PLACE, IN_VMEM, IN_PLACE, IN_PLACE, IN_PLACE, IN_VMEM],
        out_specs=[IN_PLACE] * 4,
        scratch_shapes=[
            pltpu.VMEM(dense.shape, jnp.bfloat16),
            pltpu.VMEM((users, factors), jnp.bfloat16),
            pltpu.VMEM((factors, users), jnp.bfloat16),
            pltpu.VMEM((users, 1), jnp.float32),
            pltpu.VMEM((users, factors), jnp.float32),
            pltpu.VMEM((users, pair * touched_rows), jnp.bfloat16),
            pltpu.VMEM((users, pair * touched_rows), jnp.bfloat16),
            pltpu.VMEM((owners, touched_rows, factors), jnp.bfloat16),
            pltpu.VMEM((users // 2, factors), jnp.bfloat16),
            pltpu.VMEM((1, factors), jnp.float32),
            pltpu.SemaphoreType.DMA((owners // pair + 4,)),
            pltpu.SemaphoreType.DMA((owners // pair + 5,)),
        ],
        out_shape=[
            pltpu.HBM((owners, touched_rows, factors), jnp.bfloat16),
            pltpu.HBM((users // 2, factors), jnp.float32),
            pltpu.HBM((users // 2, factors), jnp.bfloat16),
            pltpu.HBM((1, factors), jnp.float32),
        ],
        compiler_params=pltpu.CompilerParams(vmem_limit_bytes=SWEEP_BYTES),
        cost_estimate=pl.CostEstimate(
            flops=6 * owners * touched_rows * users * factors,
            bytes_accessed=2 * dense.size + 4 * items.size + 4 * users * factors,
            transcendentals=owners * touched_rows * users,
        ),
    )(place, in_hbm(dense), items, in_hbm(user_gain), in_hbm(turned_gain), in_hbm(user_level), item_total)


def chip_kernel(after_ref, kept_ref, got_ref, sum_ref):
    sum_ref[...] = (kept_ref[...] + got_ref[...].astype(jnp.float32)).astype(jnp.bfloat16)


def chip_sums(kept, got, after):
    rows, factors = kept.shape
    spec = pl.BlockSpec((rows // 2, factors), lambda r: (r, 0))
    return pl.pallas_call(
        chip_kernel,
        grid=(2,),
        in_specs=[IN_PLACE, spec, spec],
        out_specs=spec,
        out_shape=pltpu.HBM((rows, factors), jnp.bfloat16),
        compiler_params=pltpu.CompilerParams(vmem_limit_bytes=VMEM_BYTES),
        cost_estimate=pl.CostEstimate(flops=rows * factors, bytes_accessed=8 * rows * factors, transcendentals=0),
    )(after, in_hbm(kept), got)


def slab_kernel(place_ref, after_ref, gain_ref, *rest):
    sums_refs, shape_ref = rest[:-1], rest[-1]
    parts = [ref[...].astype(jnp.float32) for ref in sums_refs]
    while len(parts) > 1:
        apart = len(parts) // 2
        parts = [parts[k] + parts[k + apart] for k in range(apart)]
    shape_ref[...] = user_prior + gain_ref[...].astype(jnp.float32) * parts[0]


def slab_shapes(place, sums, user_gain, after):
    rows, factors = sums[0].shape
    spec = pl.BlockSpec((rows // 2, factors), lambda r, place_ref: (r, 0))
    return pl.pallas_call(
        slab_kernel,
        grid_spec=pltpu.PrefetchScalarGridSpec(
            num_scalar_prefetch=1,
            grid=(2,),
            in_specs=[
                IN_PLACE,
                pl.BlockSpec((rows // 2, factors), lambda r, place_ref: (lax.rem(place_ref[0], 2) * 2 + r, 0)),
            ]
            + [spec] * len(sums),
            out_specs=spec,
        ),
        out_shape=pltpu.HBM((rows, factors), jnp.float32),
        compiler_params=pltpu.CompilerParams(vmem_limit_bytes=VMEM_BYTES),
        cost_estimate=pl.CostEstimate(
            flops=len(sums) * rows * factors, bytes_accessed=2 * (len(sums) + 3) * rows * factors, transcendentals=0
        ),
    )(place, after, in_hbm(user_gain), in_hbm(sums[0]), *sums[1:])


def item_kernel(
    per_owner, seat_ref, head_from, sums_ref, gain_from, level_from, near_ref, far_ref, shape_out, elog_out,
    table_ref, acc_ref, gain_ref, level_ref, shape_ref, elog_ref, arrived, sent,
):
    blocks, edge, _ = acc_ref.shape
    fetches = [
        pltpu.make_async_copy(source, target, arrived.at[place])
        for place, (source, target) in enumerate(
            ((head_from.at[:, :, pl.ds(0, LANES)], table_ref), (gain_from, gain_ref), (level_from, level_ref))
        )
    ]
    for copy in fetches:
        copy.start()
    acc_ref[...] = jnp.zeros_like(acc_ref)
    fetches[0].wait()
    for sender in range(sums_ref.shape[0]):
        for place in range(per_owner):
            block = block_at(table_ref, sender, place, seat_ref[0])
            acc_ref[block] += sums_ref[sender, pl.ds(place * edge, edge), :].astype(jnp.float32)
    for copy in fetches[1:]:
        copy.wait()
    user_total = near_ref[...] + far_ref[...]
    copies = []
    for block in range(blocks):
        rows = pl.ds(block * edge, edge)
        shape_new = item_prior + gain_ref[rows, :].astype(jnp.float32) * acc_ref[block]
        shape_ref[rows, :] = shape_new
        elog_ref[rows, :] = digamma(shape_new) - jnp.log(level_ref[rows, :] + user_total)
        copies.append(pltpu.make_async_copy(shape_ref.at[rows], shape_out.at[rows], sent.at[2 * block]))
        copies.append(pltpu.make_async_copy(elog_ref.at[rows], elog_out.at[rows], sent.at[2 * block + 1]))
        for copy in copies[-2:]:
            copy.start()
    for copy in copies:
        copy.wait()


def item_update(seat, heads, sums, item_gain, item_level, near, far, edge, per_owner):
    items, factors = item_gain.shape
    return pl.pallas_call(
        functools.partial(item_kernel, per_owner),
        in_specs=[IN_SMEM, IN_PLACE, IN_VMEM, IN_PLACE, IN_PLACE, IN_VMEM, IN_VMEM],
        out_specs=[IN_PLACE, IN_PLACE],
        scratch_shapes=[
            pltpu.SMEM((heads.shape[0], 1, LANES), jnp.float32),
            pltpu.VMEM((items // edge, edge, factors), jnp.float32),
            pltpu.VMEM((items, factors), jnp.bfloat16),
            pltpu.VMEM((items, 1), jnp.float32),
            pltpu.VMEM((items, factors), jnp.float32),
            pltpu.VMEM((items, factors), jnp.float32),
            pltpu.SemaphoreType.DMA((3,)),
            pltpu.SemaphoreType.DMA((2 * (items // edge),)),
        ],
        out_shape=[pltpu.HBM((items, factors), jnp.float32)] * 2,
        compiler_params=pltpu.CompilerParams(vmem_limit_bytes=VMEM_BYTES),
        cost_estimate=pl.CostEstimate(
            flops=40 * items * factors, bytes_accessed=2 * sums.size + 10 * items * factors,
            transcendentals=4 * items * factors,
        ),
    )(seat, heads, sums, in_hbm(item_gain), in_hbm(item_level), near, far)


def ahead(array, axis, count):
    size = lax.axis_size(axis)
    return lax.ppermute(array, axis, [(j, (j + count) % size) for j in range(size)])


def across(array, axis, bit):
    return lax.ppermute(array, axis, [(j, j ^ bit) for j in range(lax.axis_size(axis))])


def shards(
    counts, tile_user, tile_slot, live_tiles, touched, user_shape, user_rate, item_shape, item_rate
):
    edge = counts.shape[1]
    users, factors = user_shape.shape
    user_blocks = users // edge
    owners, per_owner = touched.shape
    columns = lax.axis_size("item")
    place = lax.axis_index("item").astype(jnp.int32).reshape(1)
    seat = lax.axis_index("user").astype(jnp.int32).reshape(1)
    heads = lax.all_to_all(head_of(touched, item_shape, item_rate), "user", 0, 0)
    item_gain, item_level = item_gains(item_shape, item_rate)
    item_rows = lax.all_to_all(pick(seat, heads, item_gain, edge, per_owner), "user", 0, 0)
    user_gain, user_level, turned_gain, column_total = user_gains(user_shape, user_rate, heads)
    item_total = jnp.sum(lax.all_gather(column_total, "item", axis=0, tiled=True), axis=0, keepdims=True)
    dense = dense_counts(
        counts, tile_user, tile_slot, live_tiles, owners * per_owner, user_blocks, item_total
    )
    item_sums, kept, given, user_total = sweep(
        place, dense, item_rows, user_gain, turned_gain, user_level, item_total, columns
    )
    item_sums = lax.all_to_all(item_sums, "user", 0, 0)
    user_total = jnp.sum(lax.all_gather(user_total, "item", axis=0, tiled=True), axis=0, keepdims=True)
    chip = chip_sums(kept, across(given, "item", 1), user_total)
    bits = [1 << step for step in range(owners.bit_length() - 1)]
    for bit in bits[:-1]:
        user_total = user_total + across(user_total, "user", bit)
    far_total = across(user_total, "user", bits[-1])
    own_shapes = slab_shapes(
        place, [chip] + [ahead(chip, "item", count) for count in range(2, columns, 2)], user_gain, far_total
    )
    other_shapes = across(own_shapes, "item", 1)
    user_shape_new = jnp.where(
        place[0] % 2 == 0,
        jnp.concatenate([own_shapes, other_shapes], axis=0),
        jnp.concatenate([other_shapes, own_shapes], axis=0),
    )
    user_rate_new = user_level + item_total
    item_shape_new, item_elog = item_update(
        seat, heads, item_sums, item_gain, item_level, user_total, far_total, edge, per_owner
    )
    return (user_shape_new, user_rate_new, item_shape_new, item_elog)


def solution(mesh):
    return jax.shard_map(
        shards,
        mesh=mesh,
        in_specs=(
            P(("user", "item"), None, None),
            P(("user", "item")),
            P(("user", "item")),
            P(("user", "item")),
            P(("user", "item"), None),
            P("user", None),
            P("user", None),
            P(("user", "item"), None),
            P(("user", "item"), None),
        ),
        out_specs=(
            P("user", None),
            P("user", None),
            P(("user", "item"), None),
            P(("user", "item"), None),
        ),
        check_vma=False,
    )
```

```python
import functools

import jax
import jax.numpy as jnp
from jax import lax
from jax.experimental import pallas as pl
from jax.experimental.pallas import tpu as pltpu
from jax.sharding import PartitionSpec as P

user_prior = 0.3
activity_prior = 0.3
activity_scale = 1.0
item_prior = 0.3
popularity_prior = 0.3
popularity_scale = 1.0

VMEM_BYTES = 24 << 20
SWEEP_BYTES = 36 << 20
LANES = 128
EXTRA = 16
IN_VMEM = pl.BlockSpec(memory_space=pltpu.VMEM)
IN_SMEM = pl.BlockSpec(memory_space=pltpu.SMEM)
IN_PLACE = pl.BlockSpec(memory_space=pl.ANY)


def in_hbm(array):
    return pltpu.with_memory_space_constraint(array, pltpu.HBM)


def digamma_rest(x):
    w = x * (x + 3.0)
    steps = (2.0 * x + 3.0) * (2.0 * w + 2.0) / (w * (w + 2.0))
    inverse = 1.0 / (x + 4.0)
    z = inverse * inverse
    series = z * (1.0 / 12.0 - z * (1.0 / 120.0 - z * (1.0 / 252.0 - z * (1.0 / 240.0))))
    return steps + 0.5 * inverse + series


def digamma(x):
    return jnp.log(x + 4.0) - digamma_rest(x)


def gains_of(shape_values, rate_values, prior, strength):
    inverse_rate = 1.0 / rate_values
    gain = (shape_values + 4.0) * jnp.exp(-digamma_rest(shape_values)) * inverse_rate
    mean = shape_values * inverse_rate
    return gain.astype(jnp.bfloat16), strength / (prior + jnp.sum(mean, axis=1, keepdims=True)), mean


def head_kernel(touched_from, shape_from, rate_from, head_ref, touched_ref, shape_ref, rate_ref, arrived):
    per_owner, devices = touched_ref.shape
    rows, factors = shape_ref.shape
    parts = (arrived.shape[0] - 1) // 2
    step = rows // parts

    def fetch(part):
        piece = pl.ds(part * step, step)
        return [
            pltpu.make_async_copy(shape_from.at[piece], shape_ref.at[piece], arrived.at[2 * part]),
            pltpu.make_async_copy(rate_from.at[piece], rate_ref.at[piece], arrived.at[2 * part + 1]),
        ]

    table = pltpu.make_async_copy(touched_from, touched_ref, arrived.at[2 * parts])
    for part in range(parts):
        for copy in fetch(part):
            copy.start()
    table.start()
    total = jnp.zeros((1, factors), jnp.float32)
    for part in range(parts):
        for copy in fetch(part):
            copy.wait()
        piece = pl.ds(part * step, step)
        total += jnp.sum(shape_ref[piece, :] / rate_ref[piece, :], axis=0, keepdims=True)
    table.wait()
    blocks = touched_ref[...].astype(jnp.float32)
    row = jnp.concatenate(
        [blocks[place : place + 1] for place in range(per_owner)]
        + [jnp.zeros((1, LANES - per_owner * devices), jnp.float32), total],
        axis=1,
    )
    head_ref[...] = jnp.broadcast_to(row.reshape(1, 1, LANES + factors), head_ref.shape)


def head_of(touched, item_shape, item_rate):
    rows, factors = item_shape.shape
    devices, per_owner = touched.shape
    head_shape = (devices, 1, LANES + factors)
    return pl.pallas_call(
        head_kernel,
        grid=(1,),
        in_specs=[IN_PLACE, IN_PLACE, IN_PLACE],
        out_specs=pl.BlockSpec(head_shape, lambda r: (0, 0, 0)),
        out_shape=pltpu.HBM(head_shape, jnp.float32),
        scratch_shapes=[
            pltpu.VMEM((per_owner, devices), jnp.int32),
            pltpu.VMEM((rows, factors), jnp.float32),
            pltpu.VMEM((rows, factors), jnp.float32),
            pltpu.SemaphoreType.DMA((9,)),
        ],
        compiler_params=pltpu.CompilerParams(vmem_limit_bytes=VMEM_BYTES),
        cost_estimate=pl.CostEstimate(
            flops=4 * rows * factors, bytes_accessed=8 * rows * factors, transcendentals=rows * factors
        ),
    )(in_hbm(touched.T), in_hbm(item_shape), in_hbm(item_rate))


def item_gain_kernel(strength, shape_ref, rate_ref, gain_ref, level_ref):
    gain_ref[...], level_ref[...], _ = gains_of(
        shape_ref[...], rate_ref[...], popularity_prior / popularity_scale, strength
    )


def item_gains(item_shape, item_rate):
    rows, factors = item_shape.shape
    step = rows // 2
    row_spec = pl.BlockSpec((step, factors), lambda r: (r, 0))
    return pl.pallas_call(
        functools.partial(item_gain_kernel, popularity_prior + factors * item_prior),
        grid=(rows // step,),
        in_specs=[row_spec, row_spec],
        out_specs=[row_spec, pl.BlockSpec((step, 1), lambda r: (r, 0))],
        out_shape=[
            pltpu.HBM((rows, factors), jnp.bfloat16),
            pltpu.HBM((rows, 1), jnp.float32),
        ],
        compiler_params=pltpu.CompilerParams(vmem_limit_bytes=VMEM_BYTES),
        cost_estimate=pl.CostEstimate(
            flops=40 * rows * factors, bytes_accessed=10 * rows * factors, transcendentals=4 * rows * factors
        ),
    )(in_hbm(item_shape), in_hbm(item_rate))


def user_gain_kernel(strength, shape_ref, rate_ref, head_ref, gain_ref, level_ref, turned_ref, column_ref):
    gain, level_ref[...], _ = gains_of(shape_ref[...], rate_ref[...], activity_prior / activity_scale, strength)
    gain_ref[...] = gain
    turned_ref[...] = gain.T

    @pl.when(pl.program_id(0) == 0)
    def _():
        factors = gain.shape[1]
        means = head_ref[:, :, pl.ds(head_ref.shape[2] - factors, factors)]
        column_ref[...] = jnp.sum(means, axis=0).reshape(1, factors)


def user_gains(user_shape, user_rate, heads):
    rows, factors = user_shape.shape
    step = rows // 4
    row_spec = pl.BlockSpec((step, factors), lambda r: (r, 0))
    return pl.pallas_call(
        functools.partial(user_gain_kernel, activity_prior + factors * user_prior),
        grid=(rows // step,),
        in_specs=[row_spec, row_spec, pl.BlockSpec(heads.shape, lambda r: (0, 0, 0))],
        out_specs=[
            row_spec,
            pl.BlockSpec((step, 1), lambda r: (r, 0)),
            pl.BlockSpec((factors, step), lambda r: (0, r)),
            pl.BlockSpec((1, factors), lambda r: (0, 0)),
        ],
        out_shape=[
            pltpu.HBM((rows, factors), jnp.bfloat16),
            pltpu.HBM((rows, 1), jnp.float32),
            pltpu.HBM((factors, rows), jnp.bfloat16),
            pltpu.HBM((1, factors), jnp.float32),
        ],
        compiler_params=pltpu.CompilerParams(vmem_limit_bytes=VMEM_BYTES),
        cost_estimate=pl.CostEstimate(
            flops=40 * rows * factors, bytes_accessed=12 * rows * factors, transcendentals=4 * rows * factors
        ),
    )(in_hbm(user_shape), in_hbm(user_rate), heads)


def block_at(table_ref, device, place, seat):
    return table_ref[device, 0, place * table_ref.shape[0] + seat].astype(jnp.int32)


def pick_kernel(per_owner, seat_ref, head_from, gain_from, picked_out, table_ref, gain_ref, picked_ref, arrived, sent):
    blocks, edge, _ = gain_ref.shape
    devices = table_ref.shape[0]
    fetches = [pltpu.make_async_copy(head_from.at[:, :, pl.ds(0, LANES)], table_ref, arrived.at[blocks])] + [
        pltpu.make_async_copy(gain_from.at[block], gain_ref.at[block], arrived.at[block]) for block in range(blocks)
    ]
    for copy in fetches:
        copy.start()
    for copy in fetches:
        copy.wait()
    per_copy = devices // sent.shape[0]
    copies = []
    for part in range(sent.shape[0]):
        for device in range(part * per_copy, (part + 1) * per_copy):
            for place in range(per_owner):
                block = block_at(table_ref, device, place, seat_ref[0])
                picked_ref[device, pl.ds(place * edge, edge), :] = gain_ref[block]
        piece = pl.ds(part * per_copy, per_copy)
        copies.append(pltpu.make_async_copy(picked_ref.at[piece], picked_out.at[piece], sent.at[part]))
        copies[-1].start()
    for copy in copies:
        copy.wait()


def pick(seat, heads, item_gain, edge, per_owner):
    items, factors = item_gain.shape
    devices = heads.shape[0]
    return pl.pallas_call(
        functools.partial(pick_kernel, per_owner),
        in_specs=[IN_SMEM, IN_PLACE, IN_PLACE],
        out_specs=IN_PLACE,
        scratch_shapes=[
            pltpu.SMEM((devices, 1, LANES), jnp.float32),
            pltpu.VMEM((items // edge, edge, factors), jnp.bfloat16),
            pltpu.VMEM((devices, per_owner * edge, factors), jnp.bfloat16),
            pltpu.SemaphoreType.DMA((items // edge + 1,)),
            pltpu.SemaphoreType.DMA((min(8, devices),)),
        ],
        out_shape=pltpu.HBM((devices, per_owner * edge, factors), jnp.bfloat16),
        compiler_params=pltpu.CompilerParams(vmem_limit_bytes=VMEM_BYTES),
        cost_estimate=pl.CostEstimate(
            flops=0, bytes_accessed=2 * items * factors + 2 * devices * per_owner * edge * factors, transcendentals=0
        ),
    )(seat, heads, in_hbm(item_gain.reshape(items // edge, edge, factors)))


def dense_kernel(user_of, slot_of, live_ref, counts_ref, after_ref, out_ref, dense_ref, held_ref, arrived, sent):
    depth, group = held_ref.shape[:2]
    live = live_ref[0]
    groups = (live + group - 1) // group

    def fetch(index):
        place = lax.rem(index, depth)
        return pltpu.make_async_copy(
            counts_ref.at[pl.ds(index * group, group)], held_ref.at[place], arrived.at[place]
        )

    for index in range(depth):

        @pl.when(index < groups)
        def _():
            fetch(index).start()

    def clear(slot, carry):
        dense_ref[slot] = jnp.zeros(dense_ref.shape[1:], dense_ref.dtype)
        return carry

    lax.fori_loop(0, dense_ref.shape[0], clear, 0)

    def add_group(index, carry):
        fetch(index).wait()
        place = lax.rem(index, depth)
        for offset in range(group):
            tile = index * group + offset

            @pl.when(tile < live)
            def _():
                user, slot = user_of[tile], slot_of[tile]
                dense_ref[slot, user] += held_ref[place, offset].astype(jnp.float32).astype(jnp.bfloat16)

        @pl.when(index + depth < groups)
        def _():
            fetch(index + depth).start()

        return carry

    lax.fori_loop(0, groups, add_group, 0)
    slots = dense_ref.shape[0] // sent.shape[0]
    copies = [
        pltpu.make_async_copy(
            dense_ref.at[pl.ds(part * slots, slots)], out_ref.at[pl.ds(part * slots, slots)], sent.at[part]
        )
        for part in range(sent.shape[0])
    ]
    for copy in copies:
        copy.start()
    for copy in copies:
        copy.wait()


def dense_counts(counts, tile_user, tile_slot, live_tiles, slot_count, user_blocks, after):
    tiles, edge, _ = counts.shape
    group = 8
    depth = min(8, tiles // group)
    return pl.pallas_call(
        dense_kernel,
        in_specs=[IN_SMEM, IN_SMEM, IN_SMEM, IN_PLACE, IN_VMEM],
        out_specs=IN_PLACE,
        scratch_shapes=[
            pltpu.VMEM((slot_count, user_blocks, edge, edge), jnp.bfloat16),
            pltpu.VMEM((depth, group, edge, edge), jnp.int32),
            pltpu.SemaphoreType.DMA((depth,)),
            pltpu.SemaphoreType.DMA((min(16, slot_count),)),
        ],
        out_shape=pltpu.HBM((slot_count, user_blocks, edge, edge), jnp.bfloat16),
        compiler_params=pltpu.CompilerParams(vmem_limit_bytes=VMEM_BYTES),
        cost_estimate=pl.CostEstimate(
            flops=tiles * edge * edge, bytes_accessed=4 * counts.size + 2 * slot_count * user_blocks * edge * edge,
            transcendentals=0,
        ),
    )(tile_user, tile_slot, live_tiles, in_hbm(counts), after)


def sweep_kernel(
    prior_share, place_ref, dense_from, items_ref, gain_from, turned_from, level_from, total_ref,
    item_ref, kept_out, given_out, part_out,
    dense_ref, gain_ref, turned_ref, level_ref, acc_ref, early_ref, late_ref, sums_ref, given_ref, part_ref,
    arrived, sent,
):
    owners, touched_rows, factors = items_ref.shape
    slots, user_blocks, edge, _ = dense_ref.shape
    users = user_blocks * edge
    per_owner = slots // owners
    pair = 2
    chunk = users // 4
    last = owners // pair - 1

    def items_of(index):
        return items_ref[pl.ds(index * pair, pair)].reshape(pair * touched_rows, factors)

    def denominators(index):
        turned_items = items_of(index).T
        return [
            jnp.dot(gain_ref[pl.ds(first, chunk), :], turned_items, preferred_element_type=jnp.float32)
            for first in range(0, users, chunk)
        ]

    def put_ratios(index, parts, ratio_ref):
        for place, denominator in enumerate(parts):
            blocks = pl.ds(place * (chunk // edge), chunk // edge)
            counted = jnp.concatenate(
                [
                    dense_ref[index * pair * per_owner + slot, blocks].reshape(chunk, edge)
                    for slot in range(pair * per_owner)
                ],
                axis=1,
            ).astype(jnp.float32)
            ratio_ref[pl.ds(place * chunk, chunk), :] = (counted * pl.reciprocal(denominator, approx=True)).astype(
                jnp.bfloat16
            )

    def copy_of(index):
        return pltpu.make_async_copy(
            sums_ref.at[pl.ds(index * pair, pair)],
            item_ref.at[pl.ds(index * pair, pair), pl.ds(0, touched_rows)],
            sent.at[index],
        )

    def add_products(index, ratio_ref):
        items = items_of(index)
        for first in range(0, users, chunk):
            rows = pl.ds(first, chunk)
            acc_ref[rows, :] += jnp.dot(ratio_ref[rows, :], items, preferred_element_type=jnp.float32)
        sums = jnp.dot(turned_ref[...], ratio_ref[...], preferred_element_type=jnp.float32)
        sums_ref[pl.ds(index * pair, pair)] = sums.astype(jnp.bfloat16).T.reshape(pair, touched_rows, factors)
        copy_of(index).start()

    def fetch(index):
        slots_of = pl.ds(index * pair * per_owner, pair * per_owner)
        return pltpu.make_async_copy(dense_from.at[slots_of], dense_ref.at[slots_of], arrived.at[index])

    gain_rows = [pl.ds(first, users // 2) for first in (0, users // 2)]
    first_copies = [
        pltpu.make_async_copy(gain_from.at[rows], gain_ref.at[rows], arrived.at[last + 1 + place])
        for place, rows in enumerate(gain_rows)
    ]
    later_copies = [
        pltpu.make_async_copy(source, target, arrived.at[last + 3 + place])
        for place, (source, target) in enumerate(((turned_from, turned_ref), (level_from, level_ref)))
    ]
    first_copies[0].start()
    fetch(0).start()
    first_copies[1].start()
    acc_ref[...] = jnp.zeros_like(acc_ref)
    for copy in first_copies:
        copy.wait()
    later_copies[0].start()
    for index in range(1, last + 1):
        fetch(index).start()
    later_copies[1].start()
    fetch(0).wait()
    put_ratios(0, denominators(0), early_ref)
    later_copies[0].wait()

    def turn(step, carry):
        first, second, third = 2 * step, 2 * step + 1, jnp.minimum(2 * step + 2, last)
        fetch(second).wait()

        @pl.when(third > second)
        def _():
            fetch(third).wait()

        late = denominators(second)
        add_products(first, early_ref)
        put_ratios(second, late, late_ref)
        early = denominators(third)
        add_products(second, late_ref)
        put_ratios(third, early, early_ref)
        return carry

    lax.fori_loop(0, (last + 1) // 2, turn, 0)

    half = users // 2
    step = half // 2
    core = lax.rem(place_ref[0], 2)
    copies = []
    for index in range(2):
        kept = pl.ds(pl.multiple_of(core * half + index * step, step), step)
        given = pl.ds(pl.multiple_of((1 - core) * half + index * step, step), step)
        rows = pl.ds(index * step, step)
        given_ref[rows, :] = acc_ref[given, :].astype(jnp.bfloat16)
        copies.append(pltpu.make_async_copy(acc_ref.at[kept], kept_out.at[rows], sent.at[last + 1 + 2 * index]))
        copies.append(pltpu.make_async_copy(given_ref.at[rows], given_out.at[rows], sent.at[last + 2 + 2 * index]))
    for copy in copies:
        copy.start()
    later_copies[1].wait()
    part = jnp.zeros((1, factors), jnp.float32)
    for first in range(0, users, step):
        rows = pl.ds(first, step)
        shape_share = prior_share + gain_ref[rows, :].astype(jnp.float32) * acc_ref[rows, :]
        inverse_rate = pl.reciprocal(level_ref[rows, :] + total_ref[...], approx=True)
        part += jnp.sum(shape_share * inverse_rate, axis=0, keepdims=True)
    part_ref[...] = part
    copies.append(pltpu.make_async_copy(part_ref, part_out, sent.at[last + 5]))
    copies[-1].start()
    for index in range(last + 1):
        copy_of(index).wait()
    for copy in copies:
        copy.wait()


def sweep(place, dense, items, user_gain, turned_gain, user_level, item_total, columns):
    owners, touched_rows, factors = items.shape
    users = user_gain.shape[0]
    pair = 2
    return pl.pallas_call(
        functools.partial(sweep_kernel, user_prior / columns),
        in_specs=[IN_SMEM, IN_PLACE, IN_VMEM, IN_PLACE, IN_PLACE, IN_PLACE, IN_VMEM],
        out_specs=[IN_PLACE] * 4,
        scratch_shapes=[
            pltpu.VMEM(dense.shape, jnp.bfloat16),
            pltpu.VMEM((users, factors), jnp.bfloat16),
            pltpu.VMEM((factors, users), jnp.bfloat16),
            pltpu.VMEM((users, 1), jnp.float32),
            pltpu.VMEM((users, factors), jnp.float32),
            pltpu.VMEM((users, pair * touched_rows), jnp.bfloat16),
            pltpu.VMEM((users, pair * touched_rows), jnp.bfloat16),
            pltpu.VMEM((owners, touched_rows, factors), jnp.bfloat16),
            pltpu.VMEM((users // 2, factors), jnp.bfloat16),
            pltpu.VMEM((1, factors), jnp.float32),
            pltpu.SemaphoreType.DMA((owners // pair + 4,)),
            pltpu.SemaphoreType.DMA((owners // pair + 5,)),
        ],
        out_shape=[
            pltpu.HBM((owners, touched_rows + EXTRA, factors), jnp.bfloat16),
            pltpu.HBM((users // 2, factors), jnp.float32),
            pltpu.HBM((users // 2, factors), jnp.bfloat16),
            pltpu.HBM((1, factors), jnp.float32),
        ],
        compiler_params=pltpu.CompilerParams(vmem_limit_bytes=SWEEP_BYTES),
        cost_estimate=pl.CostEstimate(
            flops=6 * owners * touched_rows * users * factors,
            bytes_accessed=2 * dense.size + 4 * items.size + 4 * users * factors,
            transcendentals=owners * touched_rows * users,
        ),
    )(place, in_hbm(dense), items, in_hbm(user_gain), in_hbm(turned_gain), in_hbm(user_level), item_total)


def split_rows(value, rows):
    high = value.astype(jnp.bfloat16).astype(jnp.float32)
    middle = (value - high).astype(jnp.bfloat16).astype(jnp.float32)
    low = value - high - middle
    row = lax.broadcasted_iota(jnp.int32, (rows, value.shape[1]), 0)
    block = jnp.where(row == 0, high, jnp.where(row == 1, middle, jnp.where(row == 2, low, 0.0)))
    return block.astype(jnp.bfloat16)


def stamp_kernel(parts_ref, sums_ref, out_ref, extra_ref, sent):
    total = jnp.sum(parts_ref[...], axis=0)
    extra_ref[...] = jnp.broadcast_to(split_rows(total, EXTRA)[None], extra_ref.shape)
    rows = pl.ds(out_ref.shape[1] - EXTRA, EXTRA)
    copy = pltpu.make_async_copy(extra_ref, out_ref.at[:, rows], sent)
    copy.start()
    copy.wait()


def stamp(parts, sums):
    owners, _, factors = sums.shape
    return pl.pallas_call(
        stamp_kernel,
        in_specs=[IN_VMEM, IN_PLACE],
        out_specs=IN_PLACE,
        scratch_shapes=[pltpu.VMEM((owners, EXTRA, factors), jnp.bfloat16), pltpu.SemaphoreType.DMA],
        out_shape=pltpu.HBM(sums.shape, sums.dtype),
        input_output_aliases={1: 0},
        compiler_params=pltpu.CompilerParams(vmem_limit_bytes=VMEM_BYTES),
        cost_estimate=pl.CostEstimate(flops=0, bytes_accessed=2 * owners * EXTRA * factors, transcendentals=0),
    )(parts, in_hbm(sums))


def chip_kernel(after_ref, kept_ref, got_ref, sum_ref):
    sum_ref[...] = (kept_ref[...] + got_ref[...].astype(jnp.float32)).astype(jnp.bfloat16)


def chip_sums(kept, got, after):
    rows, factors = kept.shape
    spec = pl.BlockSpec((rows // 2, factors), lambda r: (r, 0))
    return pl.pallas_call(
        chip_kernel,
        grid=(2,),
        in_specs=[IN_PLACE, spec, spec],
        out_specs=spec,
        out_shape=pltpu.HBM((rows, factors), jnp.bfloat16),
        compiler_params=pltpu.CompilerParams(vmem_limit_bytes=VMEM_BYTES),
        cost_estimate=pl.CostEstimate(flops=rows * factors, bytes_accessed=8 * rows * factors, transcendentals=0),
    )(after, in_hbm(kept), got)


def slab_kernel(place_ref, gain_ref, *rest):
    sums_refs, shape_ref = rest[:-1], rest[-1]
    parts = [ref[...].astype(jnp.float32) for ref in sums_refs]
    while len(parts) > 1:
        apart = len(parts) // 2
        parts = [parts[k] + parts[k + apart] for k in range(apart)]
    shape_ref[...] = user_prior + gain_ref[...].astype(jnp.float32) * parts[0]


def slab_shapes(place, sums, user_gain):
    rows, factors = sums[0].shape
    spec = pl.BlockSpec((rows // 2, factors), lambda r, place_ref: (r, 0))
    return pl.pallas_call(
        slab_kernel,
        grid_spec=pltpu.PrefetchScalarGridSpec(
            num_scalar_prefetch=1,
            grid=(2,),
            in_specs=[pl.BlockSpec((rows // 2, factors), lambda r, place_ref: (lax.rem(place_ref[0], 2) * 2 + r, 0))]
            + [spec] * len(sums),
            out_specs=spec,
        ),
        out_shape=pltpu.HBM((rows, factors), jnp.float32),
        compiler_params=pltpu.CompilerParams(vmem_limit_bytes=VMEM_BYTES),
        cost_estimate=pl.CostEstimate(
            flops=len(sums) * rows * factors, bytes_accessed=2 * (len(sums) + 3) * rows * factors, transcendentals=0
        ),
    )(place, in_hbm(user_gain), in_hbm(sums[0]), *sums[1:])


def item_kernel(
    per_owner, seat_ref, head_from, sums_ref, gain_from, level_from, shape_out, elog_out,
    table_ref, acc_ref, gain_ref, level_ref, shape_ref, elog_ref, arrived, sent,
):
    blocks, edge, _ = acc_ref.shape
    fetches = [
        pltpu.make_async_copy(source, target, arrived.at[place])
        for place, (source, target) in enumerate(
            ((head_from.at[:, :, pl.ds(0, LANES)], table_ref), (gain_from, gain_ref), (level_from, level_ref))
        )
    ]
    for copy in fetches:
        copy.start()
    acc_ref[...] = jnp.zeros_like(acc_ref)
    below = pl.ds(sums_ref.shape[1] - EXTRA, EXTRA)
    extra = sums_ref[0, below, :].astype(jnp.float32)
    for sender in range(1, sums_ref.shape[0]):
        extra += sums_ref[sender, below, :].astype(jnp.float32)
    user_total = jnp.sum(extra, axis=0, keepdims=True)
    fetches[0].wait()
    for sender in range(sums_ref.shape[0]):
        for place in range(per_owner):
            block = block_at(table_ref, sender, place, seat_ref[0])
            acc_ref[block] += sums_ref[sender, pl.ds(place * edge, edge), :].astype(jnp.float32)
    for copy in fetches[1:]:
        copy.wait()
    copies = []
    for block in range(blocks):
        rows = pl.ds(block * edge, edge)
        shape_new = item_prior + gain_ref[rows, :].astype(jnp.float32) * acc_ref[block]
        shape_ref[rows, :] = shape_new
        elog_ref[rows, :] = digamma(shape_new) - jnp.log(level_ref[rows, :] + user_total)
        copies.append(pltpu.make_async_copy(shape_ref.at[rows], shape_out.at[rows], sent.at[2 * block]))
        copies.append(pltpu.make_async_copy(elog_ref.at[rows], elog_out.at[rows], sent.at[2 * block + 1]))
        for copy in copies[-2:]:
            copy.start()
    for copy in copies:
        copy.wait()


def item_update(seat, heads, sums, item_gain, item_level, edge, per_owner):
    items, factors = item_gain.shape
    return pl.pallas_call(
        functools.partial(item_kernel, per_owner),
        in_specs=[IN_SMEM, IN_PLACE, IN_VMEM, IN_PLACE, IN_PLACE],
        out_specs=[IN_PLACE, IN_PLACE],
        scratch_shapes=[
            pltpu.SMEM((heads.shape[0], 1, LANES), jnp.float32),
            pltpu.VMEM((items // edge, edge, factors), jnp.float32),
            pltpu.VMEM((items, factors), jnp.bfloat16),
            pltpu.VMEM((items, 1), jnp.float32),
            pltpu.VMEM((items, factors), jnp.float32),
            pltpu.VMEM((items, factors), jnp.float32),
            pltpu.SemaphoreType.DMA((3,)),
            pltpu.SemaphoreType.DMA((2 * (items // edge),)),
        ],
        out_shape=[pltpu.HBM((items, factors), jnp.float32)] * 2,
        compiler_params=pltpu.CompilerParams(vmem_limit_bytes=VMEM_BYTES),
        cost_estimate=pl.CostEstimate(
            flops=40 * items * factors, bytes_accessed=2 * sums.size + 10 * items * factors,
            transcendentals=4 * items * factors,
        ),
    )(seat, heads, sums, in_hbm(item_gain), in_hbm(item_level))


def ahead(array, axis, count):
    size = lax.axis_size(axis)
    return lax.ppermute(array, axis, [(j, (j + count) % size) for j in range(size)])


def across(array, axis, bit):
    return lax.ppermute(array, axis, [(j, j ^ bit) for j in range(lax.axis_size(axis))])


def shards(
    counts, tile_user, tile_slot, live_tiles, touched, user_shape, user_rate, item_shape, item_rate
):
    edge = counts.shape[1]
    users, factors = user_shape.shape
    user_blocks = users // edge
    owners, per_owner = touched.shape
    columns = lax.axis_size("item")
    place = lax.axis_index("item").astype(jnp.int32).reshape(1)
    seat = lax.axis_index("user").astype(jnp.int32).reshape(1)
    heads = lax.all_to_all(head_of(touched, item_shape, item_rate), "user", 0, 0)
    item_gain, item_level = item_gains(item_shape, item_rate)
    item_rows = lax.all_to_all(pick(seat, heads, item_gain, edge, per_owner), "user", 0, 0)
    user_gain, user_level, turned_gain, column_total = user_gains(user_shape, user_rate, heads)
    item_total = jnp.sum(lax.all_gather(column_total, "item", axis=0, tiled=True), axis=0, keepdims=True)
    dense = dense_counts(
        counts, tile_user, tile_slot, live_tiles, owners * per_owner, user_blocks, item_total
    )
    item_sums, kept, given, user_part = sweep(
        place, dense, item_rows, user_gain, turned_gain, user_level, item_total, columns
    )
    user_parts = lax.all_gather(user_part, "item", axis=0)
    stamped = stamp(user_parts, item_sums)
    item_sums = lax.all_to_all(stamped, "user", 0, 0)
    chip = chip_sums(kept, across(given, "item", 1), in_hbm(stamped))
    own_shapes = slab_shapes(
        place, [chip] + [ahead(chip, "item", count) for count in range(2, columns, 2)], user_gain
    )
    other_shapes = across(own_shapes, "item", 1)
    user_shape_new = jnp.where(
        place[0] % 2 == 0,
        jnp.concatenate([own_shapes, other_shapes], axis=0),
        jnp.concatenate([other_shapes, own_shapes], axis=0),
    )
    user_rate_new = user_level + item_total
    item_shape_new, item_elog = item_update(seat, heads, item_sums, item_gain, item_level, edge, per_owner)
    return (user_shape_new, user_rate_new, item_shape_new, item_elog)


def solution(mesh):
    return jax.shard_map(
        shards,
        mesh=mesh,
        in_specs=(
            P(("user", "item"), None, None),
            P(("user", "item")),
            P(("user", "item")),
            P(("user", "item")),
            P(("user", "item"), None),
            P("user", None),
            P("user", None),
            P(("user", "item"), None),
            P(("user", "item"), None),
        ),
        out_specs=(
            P("user", None),
            P("user", None),
            P(("user", "item"), None),
            P(("user", "item"), None),
        ),
        check_vma=False,
    )
```

```python
import functools

import jax
import jax.numpy as jnp
from jax import lax
from jax.experimental import pallas as pl
from jax.experimental.pallas import tpu as pltpu
from jax.sharding import PartitionSpec as P

user_prior = 0.3
activity_prior = 0.3
activity_scale = 1.0
item_prior = 0.3
popularity_prior = 0.3
popularity_scale = 1.0

VMEM_BYTES = 24 << 20
SWEEP_BYTES = 36 << 20
EXTRA = 16
LANES = 128
IN_VMEM = pl.BlockSpec(memory_space=pltpu.VMEM)
IN_SMEM = pl.BlockSpec(memory_space=pltpu.SMEM)
IN_PLACE = pl.BlockSpec(memory_space=pl.ANY)


def in_hbm(array):
    return pltpu.with_memory_space_constraint(array, pltpu.HBM)


def digamma_rest(x):
    w = x * (x + 3.0)
    steps = (2.0 * x + 3.0) * (2.0 * w + 2.0) / (w * (w + 2.0))
    inverse = 1.0 / (x + 4.0)
    z = inverse * inverse
    series = z * (1.0 / 12.0 - z * (1.0 / 120.0 - z * (1.0 / 252.0 - z * (1.0 / 240.0))))
    return steps + 0.5 * inverse + series


def digamma(x):
    return jnp.log(x + 4.0) - digamma_rest(x)


def gains_of(shape_values, rate_values, prior, strength):
    inverse_rate = 1.0 / rate_values
    gain = (shape_values + 4.0) * jnp.exp(-digamma_rest(shape_values)) * inverse_rate
    mean = shape_values * inverse_rate
    return gain.astype(jnp.bfloat16), strength / (prior + jnp.sum(mean, axis=1, keepdims=True)), mean


def head_kernel(touched_from, shape_from, rate_from, head_ref, touched_ref, shape_ref, rate_ref, arrived):
    per_owner, devices = touched_ref.shape
    rows, factors = shape_ref.shape
    parts = (arrived.shape[0] - 1) // 2
    step = rows // parts

    def fetch(part):
        piece = pl.ds(part * step, step)
        return [
            pltpu.make_async_copy(shape_from.at[piece], shape_ref.at[piece], arrived.at[2 * part]),
            pltpu.make_async_copy(rate_from.at[piece], rate_ref.at[piece], arrived.at[2 * part + 1]),
        ]

    table = pltpu.make_async_copy(touched_from, touched_ref, arrived.at[2 * parts])
    for part in range(parts):
        for copy in fetch(part):
            copy.start()
    table.start()
    total = jnp.zeros((1, factors), jnp.float32)
    for part in range(parts):
        for copy in fetch(part):
            copy.wait()
        piece = pl.ds(part * step, step)
        total += jnp.sum(shape_ref[piece, :] / rate_ref[piece, :], axis=0, keepdims=True)
    table.wait()
    blocks = touched_ref[...].astype(jnp.float32)
    row = jnp.concatenate(
        [blocks[place : place + 1] for place in range(per_owner)]
        + [jnp.zeros((1, LANES - per_owner * devices), jnp.float32), total],
        axis=1,
    )
    head_ref[...] = jnp.broadcast_to(row.reshape(1, 1, LANES + factors), head_ref.shape)


def head_of(touched, item_shape, item_rate):
    rows, factors = item_shape.shape
    devices, per_owner = touched.shape
    head_shape = (devices, 1, LANES + factors)
    return pl.pallas_call(
        head_kernel,
        grid=(1,),
        in_specs=[IN_PLACE, IN_PLACE, IN_PLACE],
        out_specs=pl.BlockSpec(head_shape, lambda r: (0, 0, 0)),
        out_shape=pltpu.HBM(head_shape, jnp.float32),
        scratch_shapes=[
            pltpu.VMEM((per_owner, devices), jnp.int32),
            pltpu.VMEM((rows, factors), jnp.float32),
            pltpu.VMEM((rows, factors), jnp.float32),
            pltpu.SemaphoreType.DMA((9,)),
        ],
        compiler_params=pltpu.CompilerParams(vmem_limit_bytes=VMEM_BYTES),
        cost_estimate=pl.CostEstimate(
            flops=4 * rows * factors, bytes_accessed=8 * rows * factors, transcendentals=rows * factors
        ),
    )(in_hbm(touched.T), in_hbm(item_shape), in_hbm(item_rate))


def item_gain_kernel(strength, shape_ref, rate_ref, gain_ref, level_ref):
    gain_ref[...], level_ref[...], _ = gains_of(
        shape_ref[...], rate_ref[...], popularity_prior / popularity_scale, strength
    )


def item_gains(item_shape, item_rate):
    rows, factors = item_shape.shape
    step = rows // 2
    row_spec = pl.BlockSpec((step, factors), lambda r: (r, 0))
    return pl.pallas_call(
        functools.partial(item_gain_kernel, popularity_prior + factors * item_prior),
        grid=(rows // step,),
        in_specs=[row_spec, row_spec],
        out_specs=[row_spec, pl.BlockSpec((step, 1), lambda r: (r, 0))],
        out_shape=[
            pltpu.HBM((rows, factors), jnp.bfloat16),
            pltpu.HBM((rows, 1), jnp.float32),
        ],
        compiler_params=pltpu.CompilerParams(vmem_limit_bytes=VMEM_BYTES),
        cost_estimate=pl.CostEstimate(
            flops=40 * rows * factors, bytes_accessed=10 * rows * factors, transcendentals=4 * rows * factors
        ),
    )(in_hbm(item_shape), in_hbm(item_rate))


def user_gain_kernel(strength, shape_ref, rate_ref, head_ref, gain_ref, level_ref, turned_ref, column_ref):
    gain, level_ref[...], _ = gains_of(shape_ref[...], rate_ref[...], activity_prior / activity_scale, strength)
    gain_ref[...] = gain
    turned_ref[...] = gain.T

    @pl.when(pl.program_id(0) == 0)
    def _():
        factors = gain.shape[1]
        means = head_ref[:, :, pl.ds(head_ref.shape[2] - factors, factors)]
        column_ref[...] = jnp.sum(means, axis=0).reshape(1, factors)


def user_gains(user_shape, user_rate, heads):
    rows, factors = user_shape.shape
    step = rows // 4
    row_spec = pl.BlockSpec((step, factors), lambda r: (r, 0))
    return pl.pallas_call(
        functools.partial(user_gain_kernel, activity_prior + factors * user_prior),
        grid=(rows // step,),
        in_specs=[row_spec, row_spec, pl.BlockSpec(heads.shape, lambda r: (0, 0, 0))],
        out_specs=[
            row_spec,
            pl.BlockSpec((step, 1), lambda r: (r, 0)),
            pl.BlockSpec((factors, step), lambda r: (0, r)),
            pl.BlockSpec((1, factors), lambda r: (0, 0)),
        ],
        out_shape=[
            pltpu.HBM((rows, factors), jnp.bfloat16),
            pltpu.HBM((rows, 1), jnp.float32),
            pltpu.HBM((factors, rows), jnp.bfloat16),
            pltpu.HBM((1, factors), jnp.float32),
        ],
        compiler_params=pltpu.CompilerParams(vmem_limit_bytes=VMEM_BYTES),
        cost_estimate=pl.CostEstimate(
            flops=40 * rows * factors, bytes_accessed=12 * rows * factors, transcendentals=4 * rows * factors
        ),
    )(in_hbm(user_shape), in_hbm(user_rate), heads)


def block_at(table_ref, device, place, seat):
    return table_ref[device, 0, place * table_ref.shape[0] + seat].astype(jnp.int32)


def pick_kernel(per_owner, seat_ref, head_from, gain_from, picked_out, table_ref, gain_ref, picked_ref, arrived, sent):
    blocks, edge, _ = gain_ref.shape
    devices = table_ref.shape[0]
    fetches = [pltpu.make_async_copy(head_from.at[:, :, pl.ds(0, LANES)], table_ref, arrived.at[blocks])] + [
        pltpu.make_async_copy(gain_from.at[block], gain_ref.at[block], arrived.at[block]) for block in range(blocks)
    ]
    for copy in fetches:
        copy.start()
    for copy in fetches:
        copy.wait()
    per_copy = devices // sent.shape[0]
    copies = []
    for part in range(sent.shape[0]):
        for device in range(part * per_copy, (part + 1) * per_copy):
            for place in range(per_owner):
                block = block_at(table_ref, device, place, seat_ref[0])
                picked_ref[device, pl.ds(place * edge, edge), :] = gain_ref[block]
        piece = pl.ds(part * per_copy, per_copy)
        copies.append(pltpu.make_async_copy(picked_ref.at[piece], picked_out.at[piece], sent.at[part]))
        copies[-1].start()
    for copy in copies:
        copy.wait()


def pick(seat, heads, item_gain, edge, per_owner):
    items, factors = item_gain.shape
    devices = heads.shape[0]
    return pl.pallas_call(
        functools.partial(pick_kernel, per_owner),
        in_specs=[IN_SMEM, IN_PLACE, IN_PLACE],
        out_specs=IN_PLACE,
        scratch_shapes=[
            pltpu.SMEM((devices, 1, LANES), jnp.float32),
            pltpu.VMEM((items // edge, edge, factors), jnp.bfloat16),
            pltpu.VMEM((devices, per_owner * edge, factors), jnp.bfloat16),
            pltpu.SemaphoreType.DMA((items // edge + 1,)),
            pltpu.SemaphoreType.DMA((min(8, devices),)),
        ],
        out_shape=pltpu.HBM((devices, per_owner * edge, factors), jnp.bfloat16),
        compiler_params=pltpu.CompilerParams(vmem_limit_bytes=VMEM_BYTES),
        cost_estimate=pl.CostEstimate(
            flops=0, bytes_accessed=2 * items * factors + 2 * devices * per_owner * edge * factors, transcendentals=0
        ),
    )(seat, heads, in_hbm(item_gain.reshape(items // edge, edge, factors)))


def dense_kernel(user_of, slot_of, live_ref, counts_ref, after_ref, out_ref, dense_ref, held_ref, arrived, sent):
    depth, group = held_ref.shape[:2]
    live = live_ref[0]
    groups = (live + group - 1) // group

    def fetch(index):
        place = lax.rem(index, depth)
        return pltpu.make_async_copy(
            counts_ref.at[pl.ds(index * group, group)], held_ref.at[place], arrived.at[place]
        )

    for index in range(depth):

        @pl.when(index < groups)
        def _():
            fetch(index).start()

    def clear(slot, carry):
        dense_ref[slot] = jnp.zeros(dense_ref.shape[1:], dense_ref.dtype)
        return carry

    lax.fori_loop(0, dense_ref.shape[0], clear, 0)

    def add_group(index, carry):
        fetch(index).wait()
        place = lax.rem(index, depth)
        for offset in range(group):
            tile = index * group + offset

            @pl.when(tile < live)
            def _():
                user, slot = user_of[tile], slot_of[tile]
                dense_ref[slot, user] += held_ref[place, offset].astype(jnp.float32).astype(jnp.bfloat16)

        @pl.when(index + depth < groups)
        def _():
            fetch(index + depth).start()

        return carry

    lax.fori_loop(0, groups, add_group, 0)
    slots = dense_ref.shape[0] // sent.shape[0]
    copies = [
        pltpu.make_async_copy(
            dense_ref.at[pl.ds(part * slots, slots)], out_ref.at[pl.ds(part * slots, slots)], sent.at[part]
        )
        for part in range(sent.shape[0])
    ]
    for copy in copies:
        copy.start()
    for copy in copies:
        copy.wait()


def dense_counts(counts, tile_user, tile_slot, live_tiles, slot_count, user_blocks, after):
    tiles, edge, _ = counts.shape
    group = 8
    depth = min(8, tiles // group)
    return pl.pallas_call(
        dense_kernel,
        in_specs=[IN_SMEM, IN_SMEM, IN_SMEM, IN_PLACE, IN_VMEM],
        out_specs=IN_PLACE,
        scratch_shapes=[
            pltpu.VMEM((slot_count, user_blocks, edge, edge), jnp.bfloat16),
            pltpu.VMEM((depth, group, edge, edge), jnp.int32),
            pltpu.SemaphoreType.DMA((depth,)),
            pltpu.SemaphoreType.DMA((min(16, slot_count),)),
        ],
        out_shape=pltpu.HBM((slot_count, user_blocks, edge, edge), jnp.bfloat16),
        compiler_params=pltpu.CompilerParams(vmem_limit_bytes=VMEM_BYTES),
        cost_estimate=pl.CostEstimate(
            flops=tiles * edge * edge, bytes_accessed=4 * counts.size + 2 * slot_count * user_blocks * edge * edge,
            transcendentals=0,
        ),
    )(tile_user, tile_slot, live_tiles, in_hbm(counts), after)


def split_rows(value, rows):
    high = value.astype(jnp.bfloat16).astype(jnp.float32)
    middle = (value - high).astype(jnp.bfloat16).astype(jnp.float32)
    low = value - high - middle
    row = lax.broadcasted_iota(jnp.int32, (rows, value.shape[1]), 0)
    block = jnp.where(row == 0, high, jnp.where(row == 1, middle, jnp.where(row == 2, low, 0.0)))
    return block.astype(jnp.bfloat16)


def sweep_kernel(
    prior_share, place_ref, dense_from, items_ref, gain_from, turned_from, level_from, total_ref, item_ref, *rest
):
    user_outs, rest = rest[:-12], rest[-12:]
    dense_ref, gain_ref, turned_ref, level_ref, acc_ref, early_ref, late_ref, sums_ref, extra_ref, users_ref = rest[:10]
    arrived, sent = rest[10:]
    owners, touched_rows, factors = items_ref.shape
    slots, user_blocks, edge, _ = dense_ref.shape
    users = user_blocks * edge
    per_owner = slots // owners
    pair = 2
    chunk = users // 2
    last = owners // pair - 1

    def items_of(index):
        return items_ref[pl.ds(index * pair, pair)].reshape(pair * touched_rows, factors)

    def denominators(index):
        items = items_of(index)
        return [
            lax.dot_general(
                gain_ref[pl.ds(first, chunk), :], items, (((1,), (1,)), ((), ())), preferred_element_type=jnp.float32
            )
            for first in range(0, users, chunk)
        ]

    def put_ratios(index, parts, ratio_ref):
        for place, denominator in enumerate(parts):
            blocks = pl.ds(place * (chunk // edge), chunk // edge)
            counted = jnp.concatenate(
                [
                    dense_ref[index * pair * per_owner + slot, blocks].reshape(chunk, edge)
                    for slot in range(pair * per_owner)
                ],
                axis=1,
            ).astype(jnp.float32)
            ratio_ref[pl.ds(place * chunk, chunk), :] = (counted * pl.reciprocal(denominator, approx=True)).astype(
                jnp.bfloat16
            )

    def copy_of(index):
        return pltpu.make_async_copy(
            sums_ref.at[pl.ds(index * pair, pair)],
            item_ref.at[pl.ds(index * pair, pair), pl.ds(0, touched_rows)],
            sent.at[index],
        )

    def add_products(index, ratio_ref):
        items = items_of(index)
        for first in range(0, users, chunk):
            rows = pl.ds(first, chunk)
            acc_ref[rows, :] += jnp.dot(ratio_ref[rows, :], items, preferred_element_type=jnp.float32)
        sums = jnp.dot(turned_ref[...], ratio_ref[...], preferred_element_type=jnp.float32)
        sums_ref[pl.ds(index * pair, pair)] = sums.astype(jnp.bfloat16).T.reshape(pair, touched_rows, factors)
        copy_of(index).start()

    def fetch(index):
        slots_of = pl.ds(index * pair * per_owner, pair * per_owner)
        return pltpu.make_async_copy(dense_from.at[slots_of], dense_ref.at[slots_of], arrived.at[index])

    gain_rows = [pl.ds(first, chunk) for first in range(0, users, chunk)]
    first_copies = [
        pltpu.make_async_copy(gain_from.at[rows], gain_ref.at[rows], arrived.at[last + 1 + place])
        for place, rows in enumerate(gain_rows)
    ]
    later_copies = [
        pltpu.make_async_copy(source, target, arrived.at[last + 3 + place])
        for place, (source, target) in enumerate(((turned_from, turned_ref), (level_from, level_ref)))
    ]
    first_copies[0].start()
    fetch(0).start()
    first_copies[1].start()
    acc_ref[...] = jnp.zeros_like(acc_ref)
    for copy in first_copies:
        copy.wait()
    later_copies[0].start()
    for index in range(1, last + 1):
        fetch(index).start()
    later_copies[1].start()
    fetch(0).wait()
    put_ratios(0, denominators(0), early_ref)
    later_copies[0].wait()

    def turn(step, carry):
        first, second, third = 2 * step, 2 * step + 1, jnp.minimum(2 * step + 2, last)
        fetch(second).wait()

        @pl.when(third > second)
        def _():
            fetch(third).wait()

        late = denominators(second)
        add_products(first, early_ref)
        put_ratios(second, late, late_ref)
        early = denominators(third)
        add_products(second, late_ref)
        put_ratios(third, early, early_ref)
        return carry

    lax.fori_loop(0, (last + 1) // 2, turn, 0)

    own = users // len(user_outs)
    copies = []
    for ahead, user_out in enumerate(user_outs):
        target = (place_ref[0] + ahead) % len(user_outs)
        rows = pl.ds(pl.multiple_of(target * own, own), own)
        users_ref[ahead] = acc_ref[rows, :].astype(jnp.bfloat16)
        copies.append(pltpu.make_async_copy(users_ref.at[ahead], user_out, sent.at[last + 2 + ahead]))
        copies[-1].start()
    later_copies[1].wait()
    part = jnp.zeros((1, factors), jnp.float32)
    for first in range(0, users, own):
        rows = pl.ds(first, own)
        shape_share = prior_share + gain_ref[rows, :].astype(jnp.float32) * acc_ref[rows, :]
        inverse_rate = pl.reciprocal(level_ref[rows, :] + total_ref[...], approx=True)
        part += jnp.sum(shape_share * inverse_rate, axis=0, keepdims=True)
    extra_ref[...] = jnp.broadcast_to(split_rows(part, EXTRA)[None], extra_ref.shape)
    copies.append(
        pltpu.make_async_copy(extra_ref, item_ref.at[:, pl.ds(touched_rows, EXTRA)], sent.at[last + 1])
    )
    copies[-1].start()
    for index in range(last + 1):
        copy_of(index).wait()
    for copy in copies:
        copy.wait()


def sweep(place, dense, items, user_gain, turned_gain, user_level, item_total, parts):
    owners, touched_rows, factors = items.shape
    users = user_gain.shape[0]
    own = users // parts
    pair = 2
    out = pl.pallas_call(
        functools.partial(sweep_kernel, user_prior / parts),
        in_specs=[IN_SMEM, IN_PLACE, IN_VMEM, IN_PLACE, IN_PLACE, IN_PLACE, IN_VMEM],
        out_specs=[IN_PLACE] * (parts + 1),
        scratch_shapes=[
            pltpu.VMEM(dense.shape, jnp.bfloat16),
            pltpu.VMEM((users, factors), jnp.bfloat16),
            pltpu.VMEM((factors, users), jnp.bfloat16),
            pltpu.VMEM((users, 1), jnp.float32),
            pltpu.VMEM((users, factors), jnp.float32),
            pltpu.VMEM((users, pair * touched_rows), jnp.bfloat16),
            pltpu.VMEM((users, pair * touched_rows), jnp.bfloat16),
            pltpu.VMEM((owners, touched_rows, factors), jnp.bfloat16),
            pltpu.VMEM((owners, EXTRA, factors), jnp.bfloat16),
            pltpu.VMEM((parts, own, factors), jnp.bfloat16),
            pltpu.SemaphoreType.DMA((owners // pair + 4,)),
            pltpu.SemaphoreType.DMA((owners // pair + 1 + parts,)),
        ],
        out_shape=[pltpu.HBM((owners, touched_rows + EXTRA, factors), jnp.bfloat16)]
        + [pltpu.HBM((own, factors), jnp.bfloat16)] * parts,
        compiler_params=pltpu.CompilerParams(vmem_limit_bytes=SWEEP_BYTES),
        cost_estimate=pl.CostEstimate(
            flops=6 * owners * touched_rows * users * factors,
            bytes_accessed=2 * dense.size + 4 * items.size + 4 * users * factors,
            transcendentals=owners * touched_rows * users,
        ),
    )(place, in_hbm(dense), items, in_hbm(user_gain), in_hbm(turned_gain), in_hbm(user_level), item_total)
    return out[0], out[1:]


def own_kernel(place_ref, gain_ref, *rest):
    sums_refs, sum_ref = rest[:-1], rest[-1]
    sums = jnp.zeros(sum_ref.shape, jnp.float32)
    for sums_ref in sums_refs:
        sums += sums_ref[...].astype(jnp.float32)
    sum_ref[...] = (gain_ref[...].astype(jnp.float32) * sums).astype(jnp.bfloat16)


def own_users(place, sums, user_gain):
    own, factors = sums[0].shape
    first = lambda step, place_ref: (0, 0)
    return pl.pallas_call(
        own_kernel,
        grid_spec=pltpu.PrefetchScalarGridSpec(
            num_scalar_prefetch=1,
            grid=(1,),
            in_specs=[pl.BlockSpec((own, factors), lambda step, place_ref: (place_ref[0], 0))]
            + [pl.BlockSpec((own, factors), first)] * len(sums),
            out_specs=pl.BlockSpec((own, factors), first),
        ),
        out_shape=pltpu.HBM((own, factors), jnp.bfloat16),
        compiler_params=pltpu.CompilerParams(vmem_limit_bytes=VMEM_BYTES),
        cost_estimate=pl.CostEstimate(
            flops=2 * len(sums) * own * factors, bytes_accessed=2 * len(sums) * own * factors, transcendentals=0
        ),
    )(place, in_hbm(user_gain), *sums)


def fold_kernel(sums_ref, shape_after_ref, rate_after_ref, part_ref):
    extra = sums_ref[0].astype(jnp.float32)
    for sender in range(1, sums_ref.shape[0]):
        extra += sums_ref[sender].astype(jnp.float32)
    part_ref[...] = jnp.broadcast_to(jnp.sum(extra, axis=0).reshape(1, 1, -1), part_ref.shape)


def fold(sums, copies, *after):
    senders, extended, factors = sums.shape
    return pl.pallas_call(
        fold_kernel,
        grid=(1,),
        in_specs=[pl.BlockSpec((senders, EXTRA, factors), lambda step: (0, extended // EXTRA - 1, 0)), IN_PLACE, IN_PLACE],
        out_specs=pl.BlockSpec((copies, 1, factors), lambda step: (0, 0, 0)),
        out_shape=pltpu.HBM((copies, 1, factors), jnp.float32),
        compiler_params=pltpu.CompilerParams(vmem_limit_bytes=VMEM_BYTES),
        cost_estimate=pl.CostEstimate(flops=0, bytes_accessed=2 * senders * EXTRA * factors, transcendentals=0),
    )(sums, *(in_hbm(array) for array in after))


def shape_kernel(
    per_owner, seat_ref, head_from, sums_ref, gain_from, shape_out, digamma_ref, table_ref, acc_ref, gain_ref, shape_ref,
    arrived, sent,
):
    blocks, edge, _ = acc_ref.shape
    table = pltpu.make_async_copy(head_from.at[:, :, pl.ds(0, LANES)], table_ref, arrived.at[0])
    gains = pltpu.make_async_copy(gain_from, gain_ref, arrived.at[1])
    table.start()
    gains.start()
    acc_ref[...] = jnp.zeros_like(acc_ref)
    table.wait()
    for sender in range(sums_ref.shape[0]):
        for place in range(per_owner):
            block = block_at(table_ref, sender, place, seat_ref[0])
            acc_ref[block] += sums_ref[sender, pl.ds(place * edge, edge), :].astype(jnp.float32)
    gains.wait()
    copies = []
    for block in range(blocks):
        rows = pl.ds(block * edge, edge)
        shape_new = item_prior + gain_ref[rows, :].astype(jnp.float32) * acc_ref[block]
        shape_ref[rows, :] = shape_new
        copies.append(pltpu.make_async_copy(shape_ref.at[rows], shape_out.at[rows], sent.at[block]))
        copies[-1].start()
        digamma_ref[rows, :] = digamma(shape_new)
    for copy in copies:
        copy.wait()


def item_shapes(seat, heads, sums, item_gain, edge, per_owner):
    items, factors = item_gain.shape
    return pl.pallas_call(
        functools.partial(shape_kernel, per_owner),
        in_specs=[IN_SMEM, IN_PLACE, IN_VMEM, IN_PLACE],
        out_specs=[IN_PLACE, IN_VMEM],
        scratch_shapes=[
            pltpu.SMEM((heads.shape[0], 1, LANES), jnp.float32),
            pltpu.VMEM((items // edge, edge, factors), jnp.float32),
            pltpu.VMEM((items, factors), jnp.bfloat16),
            pltpu.VMEM((items, factors), jnp.float32),
            pltpu.SemaphoreType.DMA((2,)),
            pltpu.SemaphoreType.DMA((items // edge,)),
        ],
        out_shape=[pltpu.HBM((items, factors), jnp.float32), jax.ShapeDtypeStruct((items, factors), jnp.float32)],
        compiler_params=pltpu.CompilerParams(vmem_limit_bytes=VMEM_BYTES),
        cost_estimate=pl.CostEstimate(
            flops=40 * items * factors, bytes_accessed=2 * sums.size + 10 * items * factors,
            transcendentals=3 * items * factors,
        ),
    )(seat, heads, sums, in_hbm(item_gain))


def elog_kernel(digamma_ref, level_ref, parts_ref, elog_out, elog_ref, sent):
    user_total = jnp.sum(parts_ref[...], axis=0)
    step = elog_ref.shape[0] // sent.shape[0]
    copies = []
    for piece in range(sent.shape[0]):
        rows = pl.ds(piece * step, step)
        elog_ref[rows, :] = digamma_ref[rows, :] - jnp.log(level_ref[rows, :] + user_total)
        copies.append(pltpu.make_async_copy(elog_ref.at[rows], elog_out.at[rows], sent.at[piece]))
        copies[-1].start()
    for copy in copies:
        copy.wait()


def item_elogs(digammas, item_level, user_parts):
    items, factors = digammas.shape
    return pl.pallas_call(
        elog_kernel,
        in_specs=[IN_VMEM, IN_VMEM, IN_VMEM],
        out_specs=IN_PLACE,
        scratch_shapes=[pltpu.VMEM((items, factors), jnp.float32), pltpu.SemaphoreType.DMA((4,))],
        out_shape=pltpu.HBM((items, factors), jnp.float32),
        compiler_params=pltpu.CompilerParams(vmem_limit_bytes=VMEM_BYTES),
        cost_estimate=pl.CostEstimate(
            flops=2 * items * factors, bytes_accessed=8 * items * factors, transcendentals=items * factors
        ),
    )(digammas, item_level, user_parts)


def shards(
    counts, tile_user, tile_slot, live_tiles, touched, user_shape, user_rate, item_shape, item_rate
):
    edge = counts.shape[1]
    users, factors = user_shape.shape
    user_blocks = users // edge
    owners, per_owner = touched.shape
    columns = lax.axis_size("item")
    place = lax.axis_index("item").astype(jnp.int32).reshape(1)
    seat = lax.axis_index("user").astype(jnp.int32).reshape(1)
    heads = lax.all_to_all(head_of(touched, item_shape, item_rate), "user", 0, 0)
    item_gain, item_level = item_gains(item_shape, item_rate)
    item_rows = lax.all_to_all(pick(seat, heads, item_gain, edge, per_owner), "user", 0, 0)
    user_gain, user_level, turned_gain, column_total = user_gains(user_shape, user_rate, heads)
    item_total = jnp.sum(lax.all_gather(column_total, "item", axis=0, tiled=True), axis=0, keepdims=True)
    dense = dense_counts(
        counts, tile_user, tile_slot, live_tiles, owners * per_owner, user_blocks, item_total
    )
    item_sums, user_sums = sweep(
        place, dense, item_rows, user_gain, turned_gain, user_level, item_total, columns
    )
    item_sums = lax.all_to_all(item_sums, "user", 0, 0)
    user_sums = [user_sums[0]] + [
        lax.ppermute(user_sums[k], "item", [(j, (j + k) % columns) for j in range(columns)])
        for k in range(1, columns)
    ]
    user_sum = lax.all_gather(own_users(place, user_sums, user_gain), "item", axis=0, tiled=True)
    user_shape_new = user_prior + user_sum.astype(jnp.float32)
    user_rate_new = user_level + item_total
    user_parts = lax.all_to_all(fold(item_sums, columns, user_shape_new, user_rate_new), "item", 0, 0)
    item_shape_new, digammas = item_shapes(seat, heads, item_sums, item_gain, edge, per_owner)
    item_elog = item_elogs(digammas, item_level, user_parts)
    return (user_shape_new, user_rate_new, item_shape_new, item_elog)


def solution(mesh):
    return jax.shard_map(
        shards,
        mesh=mesh,
        in_specs=(
            P(("user", "item"), None, None),
            P(("user", "item")),
            P(("user", "item")),
            P(("user", "item")),
            P(("user", "item"), None),
            P("user", None),
            P("user", None),
            P(("user", "item"), None),
            P(("user", "item"), None),
        ),
        out_specs=(
            P("user", None),
            P("user", None),
            P(("user", "item"), None),
            P(("user", "item"), None),
        ),
        check_vma=False,
    )
```
